256 devices in a mesh: dp: 32 (over y, x, core), tensor: 8 (over z).
Axes of the slice: x: 4, y: 4, z: 8, core: 2. Of those that a mesh axis runs over, the one named last changes fastest.
Arguments:
- qkv: bfloat16 [4, 2560, 3, 4096], P(None, 'dp', None, 'tensor'), may hold values from -6 to 6
- fir_buffer: bfloat16 [2560, 3, 2, 4096], P('dp', None, None, 'tensor'), may hold values from -6 to 6
- fir_taps: float32 [3, 3, 4096], P(None, None, 'tensor'), may hold values from -3 to 3
- modal_state: float32 [2560, 16, 4096], P('dp', None, 'tensor'), may hold values from -6 to 6
- poles: float32 [16, 4096], P(None, 'tensor'), may hold values from 0.5 to 0.999
- residues: float32 [16, 4096], P(None, 'tensor'), may hold values from -1.5 to 1.5
- skip: float32 [4096], P('tensor'), may hold values from -3 to 3
- out_weight: bfloat16 [4096, 4096], P('tensor')
- norm_gain: float32 [4096], P('tensor'), may hold values from 0.25 to 1.75
- finished: int32 [3, 2560], P(None, 'dp'), may hold values 0 or 1
- dest_group: int32 [3, 2560], P(None, 'dp'), may hold values from 0 to 31, as said below
Outputs:
- mixed: bfloat16 [4, 2560, 4096], P(None, 'dp', 'tensor')
- final_state: float32 [2560, 16, 4096], P('dp', None, 'tensor')
- final_lagged: bfloat16 [2560, 3, 2, 4096], P('dp', None, None, 'tensor')
The draws below stay inside these ranges and needn't reach their ends.
Inputs may be any that keep to these rules, and one draw needn't show every extreme that they name: `dest_group`: for each migration, the slots s < 64 of every group form bands of 2 slots; all rows of band b of group g go to group (g + k_b) mod 32, where k_b is the same for every group and takes each value of 0 to 31 for exactly one band. Rows in later slots stay. So each group sends exactly 2 rows to every group and the moves are a permutation of the rows.
All inputs are finite; a program needn't handle non-finite values. No bound on the sum of `finished` on one device may be relied on, other than what follows from the above.
Results may differ from the reference program's by a relative error of at most 0.0048.
Values may be sent and summed in bfloat16 or wider, within the bound.
No kernel may reach another device: no remote copies, remote signals or barrier semaphores. Data moves between devices by JAX's collectives and lax.ppermute only.
A program may use at most 64 MiB of HBM per device.

```python
import math
import jax
import jax.numpy as jnp
from jax import lax

C = 4096
DOUT = 4096
ORDER = 16
TAPS = 3
STEPS = 4
CAP = 2
ROWS_DEV = 80
MIGS = 3
ROWS = 2560


def draw_out_weight(key, part):
    key = jax.random.fold_in(key, 11)
    columns = jnp.arange(DOUT, dtype=jnp.float32) / DOUT
    col_scale = jnp.exp(columns * math.log(10.0)) * (0.25 / math.sqrt(C))
    noise = jax.random.normal(key, (C, DOUT), jnp.float32)
    return (noise * col_scale[None, :]).astype(jnp.bfloat16)


def draw_dest_group(key, part):
    key = jax.random.fold_in(key, 7)
    groups = ROWS // ROWS_DEV
    row_index = jnp.arange(ROWS, dtype=jnp.int32)
    home_group = row_index // ROWS_DEV
    slot_index = row_index % ROWS_DEV
    band_index = jnp.minimum(slot_index // CAP, groups - 1)
    moving = slot_index < groups * CAP
    plans = []
    for turn_index in range(MIGS):
        shifts = jax.random.permutation(jax.random.fold_in(key, turn_index), groups).astype(jnp.int32)
        plans.append(jnp.where(moving, (home_group + shifts[band_index]) % groups, home_group))
    return jnp.stack(plans).astype(jnp.int32)


def touch_ends(result, stream_key, smallest, high):
    longest = result.shape.index(max(result.shape))
    spots = []
    for shift in (0, 1):
        where = [jax.random.randint(jax.random.fold_in(stream_key, axis), (), 0, length) for axis, length in enumerate(result.shape)]
        where[longest] = (where[longest] + shift) % result.shape[longest]
        spots.append(tuple(where))
    return result.at[spots[0]].set(smallest).at[spots[1]].set(high)


def level_of(own_key, extent, shards, low, largest):
    loudness = 1.0
    for axis_at, shards_of in shards:
        steps = jax.random.uniform(jax.random.fold_in(jax.random.fold_in(own_key, 6), axis_at), (shards_of,), jnp.float32, low / len(shards), largest / len(shards))
        loudness = loudness * jnp.repeat(jnp.exp(steps), extent[axis_at] // shards_of).reshape((-1,) + (1,) * (len(extent) - 1 - axis_at))
    return loudness


def gaussian(stream_key, shape, spread, reach, pieces=(), kind=jnp.bfloat16):
    values = jax.random.normal(stream_key, shape, jnp.float32) * spread
    if len(pieces) > 0:
        values = level_of(stream_key, shape, pieces, -0.22, 0.18) * values
    return jnp.clip(values, min=-reach, max=reach).astype(kind)


def setup_inputs(seed: int = 0) -> dict:
    arg_keys = jax.random.split(jax.random.key(seed), 12)
    qkv = gaussian(arg_keys[0], (STEPS, ROWS, 3, C), 1.0, 6.0, ((1, 32), (3, 8)))
    fir_buffer = gaussian(arg_keys[1], (ROWS, 3, 2, C), 1.0, 6.0, ((0, 32), (3, 8)))
    fir_taps = gaussian(arg_keys[2], (3, TAPS, C), 0.6, 3.0, ((2, 8),), jnp.float32)
    modal_state = gaussian(arg_keys[3], (ROWS, ORDER, C), 1.0, 6.0, ((0, 32), (2, 8)), jnp.float32)
    poles = jnp.clip(0.5 + 0.499 * jax.random.uniform(arg_keys[4], (ORDER, C), jnp.float32) ** level_of(arg_keys[4], (ORDER, C), ((1, 8),), -0.2, 0.2), 0.5, 0.999)
    residues = gaussian(arg_keys[5], (ORDER, C), 0.25, 1.5, ((1, 8),), jnp.float32)
    skip = gaussian(arg_keys[6], (C,), 0.5, 3.0, ((0, 8),), jnp.float32)
    out_weight = draw_out_weight(jax.random.fold_in(arg_keys[11], 71), 0)
    norm_gain = jnp.clip(1.0 + 0.15 * jax.random.normal(arg_keys[8], (DOUT,), jnp.float32), 0.25, 1.75)
    finished = touch_ends((jax.random.randint(arg_keys[9], (MIGS, ROWS), 0, 4) < 1).astype(jnp.int32), jax.random.fold_in(arg_keys[9], 1), 0, 1)
    dest_group = draw_dest_group(jax.random.fold_in(arg_keys[11], 71), 0)
    return dict(qkv=qkv, fir_buffer=fir_buffer, fir_taps=fir_taps, modal_state=modal_state, poles=poles, residues=residues, skip=skip, out_weight=out_weight, norm_gain=norm_gain, finished=finished, dest_group=dest_group)


def reference(qkv, fir_buffer, fir_taps, modal_state, poles, residues, skip, out_weight, norm_gain, finished, dest_group):
    state_now = modal_state
    lagged = fir_buffer
    slot_index = jnp.arange(ROWS, dtype=jnp.int32) % ROWS_DEV
    results = []
    for turn_index in range(STEPS):
        incoming = qkv[turn_index]
        filtered = fir_taps[None, :, 0, :] * incoming.astype(jnp.float32)
        filtered = filtered + fir_taps[None, :, 1, :] * lagged[:, :, 0, :].astype(jnp.float32)
        filtered = filtered + fir_taps[None, :, 2, :] * lagged[:, :, 1, :].astype(jnp.float32)
        lagged = jnp.stack([incoming, lagged[:, :, 0, :]], axis=2)
        product = filtered[:, 1] * filtered[:, 2]
        state_now = poles[None] * state_now + product[:, None, :]
        modal_out = lax.optimization_barrier(jnp.sum(residues[None] * state_now, axis=1)) + skip[None] * product
        gated_out = (filtered[:, 0] * modal_out).astype(jnp.bfloat16)
        projected = jnp.dot(gated_out, out_weight, preferred_element_type=jnp.float32)
        norm_scale = lax.rsqrt(lax.optimization_barrier(jnp.mean(projected * projected, axis=1, keepdims=True)) + 1e-05)
        results.append((projected * norm_scale * norm_gain[None]).astype(jnp.bfloat16))
        if turn_index < STEPS - 1:
            alive = (1 - finished[turn_index]).astype(jnp.float32)
            target = (dest_group[turn_index] * ROWS_DEV + slot_index).astype(jnp.int32)
            state_now = jnp.zeros_like(state_now).at[target].set(state_now * alive[:, None, None])
            lagged = jnp.zeros_like(lagged).at[target].set(lagged * alive.astype(jnp.bfloat16)[:, None, None, None])
    return (jnp.stack(results), state_now, lagged)
```

```python
import jax
import jax.numpy as jnp
from jax import lax
from jax.experimental import pallas as pl
from jax.experimental.pallas import tpu as pltpu
from jax.sharding import PartitionSpec as P

CAP = 2
MODES = 16
KINDS = 16
F32, BF16 = jnp.float32, jnp.bfloat16


def dot(a, b):
    return jnp.dot(a, b, preferred_element_type=F32)


def wide(x, width):
    return jnp.concatenate([x] * (width // x.shape[-1]), axis=-1)


def home_kernel(qkv, fir, taps, state, poles, residues, skip, alive, packed, gated, stay_state, y_rows):
    block = pl.program_id(0)
    rows, width = 16, qkv.shape[-1]
    alive0 = wide(alive[0], width)
    q0 = [qkv[0, j].astype(F32) for j in range(3)]
    l0 = [fir[j, 0].astype(F32) for j in range(3)]
    f = [
        taps[j, 0:1] * q0[j] + taps[j, 1:2] * l0[j] + taps[j, 2:3] * fir[j, 1].astype(F32)
        for j in range(3)
    ]
    product = f[1] * f[2]
    modes = []
    for r in range(rows):
        s = poles[...] * state[r] + product[r : r + 1]
        y_rows[r : r + 1] = jnp.sum(residues[...] * s, axis=0, keepdims=True)
        modes.append(s * alive0[r : r + 1])
    gated[pl.ds(block * rows, rows)] = (f[0] * (y_rows[...] + skip[...] * product)).astype(BF16)

    @pl.when(block < 4)
    def _():
        for pair in range(rows // 2):
            both = jnp.concatenate([modes[2 * pair], modes[2 * pair + 1]], axis=0)
            packed[pair, 0 : 2 * MODES] = both.astype(BF16)
        sent = [(x * alive0).astype(BF16) for x in q0 + l0]
        sent += [qkv[t, j] for t in range(1, 4) for j in range(3)]
        ends = wide(alive[1], width // 2), wide(alive[2], width // 2)
        sent.append(jnp.concatenate(ends, axis=-1).astype(BF16))
        stacked = jnp.concatenate(sent, axis=0)
        n = KINDS * rows
        r = lax.broadcasted_iota(jnp.int32, (n, n), 0)
        c = lax.broadcasted_iota(jnp.int32, (n, n), 1)
        source = ((r >> 1) & 15) * rows + (r >> 5) * 2 + (r & 1)
        order = jnp.where(c == source, 1.0, 0.0).astype(BF16)
        moved = dot(order, stacked).reshape(rows // 2, 2 * KINDS, width)
        packed[:, 2 * MODES :] = moved.astype(BF16)

    @pl.when(block == 4)
    def _():
        for r in range(rows):
            stay_state[r] = modes[r]
        lag0, lag1 = [x * alive0 for x in q0], [x * alive0 for x in l0]
        for t in range(1, 4):
            q = [qkv[t, j].astype(F32) for j in range(3)]
            g = [
                taps[j, 0:1] * q[j] + taps[j, 1:2] * lag0[j] + taps[j, 2:3] * lag1[j]
                for j in range(3)
            ]
            prod = g[1] * g[2]
            live = wide(alive[t], width) if t < 3 else None
            for r in range(rows):
                s = poles[...] * stay_state[r] + prod[r : r + 1]
                y_rows[r : r + 1] = jnp.sum(residues[...] * s, axis=0, keepdims=True)
                stay_state[r] = s * live[r : r + 1] if t < 3 else s
            gated[64 + t * rows : 80 + t * rows] = (
                g[0] * (y_rows[...] + skip[...] * prod)
            ).astype(BF16)
            if t < 3:
                lag0, lag1 = [x * live for x in q], [x * live for x in lag0]


def band_kernel(
    turns, got, taps, poles, residues, skip, sent, gated, lags, inputs, live, heads, products, y_rows
):
    groups, _, width = got.shape
    rows = 2 * groups
    kinds = got[:, 2 * MODES :].reshape(groups * 2 * KINDS, width)

    def taken(first, count, turn):
        shape = (count * rows, groups * 2 * KINDS)
        r = lax.broadcasted_iota(jnp.int32, shape, 0)
        c = lax.broadcasted_iota(jnp.int32, shape, 1)
        group = (((r & (rows - 1)) >> 1) + turn) & (groups - 1)
        source = group * (2 * KINDS) + (first + r // rows) * 2 + (r & 1)
        order = jnp.where(c == source, 1.0, 0.0).astype(BF16)
        return dot(order, kinds).reshape(count, rows, width)

    lags[...] = taken(0, 6, 0)
    for t in range(3):
        inputs[t] = taken(6 + 3 * t, 3, turns[t])
    half = width // 2
    live[0] = wide(taken(15, 1, turns[0])[0, :, :half], width)
    live[1] = wide(taken(15, 1, turns[1])[0, :, half:], width)

    @pl.loop(0, rows // 8)
    def _(i):
        at = pl.ds(pl.multiple_of(i * 8, 8), 8)
        lag0 = [lags[j, at] for j in range(3)]
        lag1 = [lags[3 + j, at] for j in range(3)]
        for t in range(3):
            q = [inputs[t, j, at] for j in range(3)]
            f = [
                taps[j, 0:1] * q[j] + taps[j, 1:2] * lag0[j] + taps[j, 2:3] * lag1[j]
                for j in range(3)
            ]
            heads[t, at] = f[0]
            products[t, at] = f[1] * f[2]
            if t < 2:
                on = live[t, at]
                lag0, lag1 = [x * on for x in q], [x * on for x in lag0]
                if t == 1:
                    for j in range(3):
                        lags[j, at] = lag0[j]

    shape = (groups * 16, 3 * rows)
    r = lax.broadcasted_iota(jnp.int32, shape, 0)
    c = lax.broadcasted_iota(jnp.int32, shape, 1)
    group = ((r >> 4) - turns[2] + groups) & (groups - 1)
    source = ((r & 15) >> 1) * rows + group * 2 + (r & 1)
    order = jnp.where((c == source) & ((r & 15) < 6), 1.0, 0.0).astype(BF16)
    last = lags[0:3].reshape(3 * rows, width).astype(BF16)
    sent[:, 2 * MODES :] = dot(order, last).reshape(groups, 16, width).astype(BF16)

    @pl.loop(0, groups)
    def _(g):
        final = []
        for side in range(2):
            row = pl.ds(g * 2 + side, 1)
            s = got[g, side * MODES : (side + 1) * MODES].astype(F32)
            for t in range(3):
                product = products[t, row]
                s = poles[...] * s + product
                y = jnp.sum(residues[...] * s, axis=0, keepdims=True)
                there = ((g + turns[t]) & (groups - 1)) * 2 + side
                y_rows[t, pl.ds(there, 1)] = heads[t, row] * (y + skip[...] * product)
                if t < 2:
                    s = s * live[t, row]
            final.append(s)
        end = (g + turns[2]) & (groups - 1)
        sent[end, 0 : 2 * MODES] = jnp.concatenate(final, axis=0).astype(BF16)

    gated[...] = y_rows[...].astype(BF16)


def whole(shape):
    return pl.BlockSpec(shape, lambda *_: (0,) * len(shape))


def ring_sums(part, own_cols):
    n = lax.axis_size("tensor")
    me = lax.axis_index("tensor")

    def piece(away):
        return lax.dynamic_slice_in_dim(part, ((me + away) % n) * own_cols, own_cols, 1)

    right = left = None
    for away in range(n // 2, 0, -1):
        held = [right, left]
        for side, step in enumerate((1, -1)):
            if step == -1 and away > (n - 1) // 2:
                continue
            mine = piece(step * away)
            held[side] = (mine if held[side] is None else mine + held[side].astype(F32)).astype(BF16)
        held = [
            x if x is None else lax.ppermute(x, "tensor", [(i, (i + step) % n) for i in range(n)])
            for x, step in zip(held, (1, -1))
        ]
        right, left = lax.optimization_barrier(tuple(held))
    total = piece(0) + right.astype(F32)
    return total if left is None else total + left.astype(F32)


def normed(part, gain):
    n = lax.axis_size("tensor")
    own = ring_sums(part, gain.shape[0])
    mine = jnp.sum(own * own, axis=1)
    squares = mine
    for away in range(1, n):
        squares = squares + lax.ppermute(mine, "tensor", [(i, (i + away) % n) for i in range(n)])
    scale = lax.rsqrt(squares / (n * gain.shape[0]) + 1e-05)
    return (own * scale[:, None] * gain[None]).astype(BF16)


def per_device(
    qkv,
    fir_buffer,
    fir_taps,
    modal_state,
    poles,
    residues,
    skip,
    out_weight,
    norm_gain,
    finished,
    dest_group,
):
    groups = lax.axis_size("dp")
    own_group = lax.axis_index("dp")
    slots, width = modal_state.shape[0], modal_state.shape[2]
    moving = groups * CAP
    qkv_kinds = jnp.transpose(qkv, (0, 2, 1, 3))
    fir_kinds = jnp.transpose(fir_buffer, (1, 2, 0, 3))
    alive = jnp.broadcast_to((1 - finished).astype(F32)[:, :, None], (3, slots, 128))
    skip_row = skip[None]
    shifts = lax.dynamic_slice_in_dim(dest_group, own_group * CAP, 1, 1)[:, 0] - own_group + groups
    turns = jnp.cumsum(shifts).astype(jnp.int32) % groups

    params = pltpu.CompilerParams(vmem_limit_bytes=32 * 1024 * 1024)
    packed, gated_home, stay_state = pl.pallas_call(
        home_kernel,
        grid=(slots // 16,),
        in_specs=[
            pl.BlockSpec((4, 3, 16, width), lambda i: (0, 0, i, 0)),
            pl.BlockSpec((3, 2, 16, width), lambda i: (0, 0, i, 0)),
            whole((3, 3, width)),
            pl.BlockSpec((16, MODES, width), lambda i: (i, 0, 0)),
            whole((MODES, width)),
            whole((MODES, width)),
            whole((1, width)),
            pl.BlockSpec((3, 16, 128), lambda i: (0, i, 0)),
        ],
        out_specs=[
            pl.BlockSpec((8, 2 * MODES + 2 * KINDS, width), lambda i: (jnp.minimum(i, 3), 0, 0)),
            whole((slots + 48, width)),
            whole((16, MODES, width)),
        ],
        out_shape=[
            jax.ShapeDtypeStruct((groups, 2 * MODES + 2 * KINDS, width), BF16),
            jax.ShapeDtypeStruct((slots + 48, width), BF16),
            jax.ShapeDtypeStruct((16, MODES, width), F32),
        ],
        scratch_shapes=[pltpu.VMEM((16, width), F32)],
        compiler_params=params,
        name="home_rows",
    )(qkv_kinds, fir_kinds, fir_taps, modal_state, poles, residues, skip_row, alive)

    got = lax.all_to_all(packed, "dp", split_axis=0, concat_axis=0, tiled=True)
    mixed_home = normed(dot(gated_home, out_weight), norm_gain)
    got, mixed_home = lax.optimization_barrier((got, mixed_home))

    sent, gated_band = pl.pallas_call(
        band_kernel,
        in_specs=[pl.BlockSpec(memory_space=pltpu.SMEM)]
        + [pl.BlockSpec(memory_space=pltpu.VMEM)] * 5,
        out_specs=[pl.BlockSpec(memory_space=pltpu.VMEM)] * 2,
        out_shape=[
            jax.ShapeDtypeStruct((groups, 2 * MODES + 16, width), BF16),
            jax.ShapeDtypeStruct((3, moving, width), BF16),
        ],
        scratch_shapes=[
            pltpu.VMEM((6, moving, width), F32),
            pltpu.VMEM((3, 3, moving, width), F32),
            pltpu.VMEM((2, moving, width), F32),
            pltpu.VMEM((3, moving, width), F32),
            pltpu.VMEM((3, moving, width), F32),
            pltpu.VMEM((3, moving, width), F32),
        ],
        compiler_params=params,
        name="band_rows",
    )(turns, got, fir_taps, poles, residues, skip_row)

    back = lax.all_to_all(sent, "dp", split_axis=0, concat_axis=0, tiled=True)
    mixed_band = normed(dot(gated_band.reshape(3 * moving, width), out_weight), norm_gain)
    own_cols = norm_gain.shape[0]
    back, mixed_band = lax.optimization_barrier((back, mixed_band))
    mixed_band = jnp.transpose(mixed_band.reshape(3, groups, CAP, own_cols), (1, 0, 2, 3))
    mixed_back = lax.all_to_all(mixed_band, "dp", split_axis=0, concat_axis=0, tiled=True)
    mixed_later = jnp.transpose(mixed_back, (1, 0, 2, 3)).reshape(3, moving, own_cols)
    mixed_stay = mixed_home[slots:].reshape(3, 16, own_cols)
    mixed = jnp.concatenate(
        [mixed_home[None, :slots], jnp.concatenate([mixed_later, mixed_stay], axis=1)], axis=0
    )

    moved_state = back[:, : 2 * MODES].reshape(moving, MODES, width).astype(F32)
    final_state = jnp.concatenate([moved_state, stay_state], axis=0)
    moved_lag = back[:, 2 * MODES : 2 * MODES + 6].reshape(groups, 3, CAP, width)
    moved_lag = jnp.transpose(moved_lag, (0, 2, 1, 3)).reshape(moving, 3, width)
    stay_alive = (1 - finished[2, moving:]).astype(BF16)[:, None, None]
    last_lag = jnp.concatenate([moved_lag, qkv[2, moving:] * stay_alive], axis=0)
    final_lagged = jnp.stack([qkv[3], last_lag], axis=2)
    return (mixed, final_state, final_lagged)


def solution(mesh):
    return jax.shard_map(
        per_device,
        mesh=mesh,
        in_specs=(
            P(None, "dp", None, "tensor"),
            P("dp", None, None, "tensor"),
            P(None, None, "tensor"),
            P("dp", None, "tensor"),
            P(None, "tensor"),
            P(None, "tensor"),
            P("tensor"),
            P("tensor", None),
            P("tensor"),
            P(None, "dp"),
            P(None, "dp"),
        ),
        out_specs=(P(None, "dp", "tensor"), P("dp", None, "tensor"), P("dp", None, None, "tensor")),
        check_vma=False,
    )
```

```python
import jax
import jax.numpy as jnp
from jax import lax
from jax.experimental import pallas as pl
from jax.experimental.pallas import tpu as pltpu
from jax.sharding import PartitionSpec as P

CAP = 2
MODES = 16
KINDS = 16
F32, BF16 = jnp.float32, jnp.bfloat16


def dot(a, b):
    return jnp.dot(a, b, preferred_element_type=F32)


def wide(x, width):
    return jnp.concatenate([x] * (width // x.shape[-1]), axis=-1)


def home_kernel(qkv, fir, taps, state, poles, residues, skip, finished, packed, gated, stay_state, y_rows):
    block = pl.program_id(0)
    rows, width = 16, qkv.shape[-1]
    at = lax.broadcasted_iota(jnp.int32, (rows, finished.shape[1]), 0) + block * rows
    own = at == lax.broadcasted_iota(jnp.int32, at.shape, 1)
    alive = [
        jnp.broadcast_to(
            1.0 - jnp.sum(jnp.where(own, finished[t : t + 1].astype(F32), 0.0), axis=1, keepdims=True),
            (rows, width),
        )
        for t in range(3)
    ]
    alive0 = alive[0]
    q0 = [qkv[0, j].astype(F32) for j in range(3)]
    l0 = [fir[j, 0].astype(F32) for j in range(3)]
    f = [
        taps[j, 0:1] * q0[j] + taps[j, 1:2] * l0[j] + taps[j, 2:3] * fir[j, 1].astype(F32)
        for j in range(3)
    ]
    product = f[1] * f[2]
    modes = []
    for r in range(rows):
        s = poles[...] * state[r] + product[r : r + 1]
        y_rows[r : r + 1] = jnp.sum(residues[...] * s, axis=0, keepdims=True)
        modes.append(s * alive0[r : r + 1])
    gated[pl.ds(block * rows, rows)] = (f[0] * (y_rows[...] + skip[...] * product)).astype(BF16)

    @pl.when(block < 4)
    def _():
        for pair in range(rows // 2):
            both = jnp.concatenate([modes[2 * pair], modes[2 * pair + 1]], axis=0)
            packed[pair, 0 : 2 * MODES] = both.astype(BF16)
        sent = [(x * alive0).astype(BF16) for x in q0 + l0]
        sent += [qkv[t, j] for t in range(1, 4) for j in range(3)]
        half = width // 2
        sent.append(jnp.concatenate([alive[1][:, :half], alive[2][:, :half]], axis=-1).astype(BF16))
        stacked = jnp.concatenate(sent, axis=0)
        n = KINDS * rows
        r = lax.broadcasted_iota(jnp.int32, (n, n), 0)
        c = lax.broadcasted_iota(jnp.int32, (n, n), 1)
        source = ((r >> 1) & 15) * rows + (r >> 5) * 2 + (r & 1)
        order = jnp.where(c == source, 1.0, 0.0).astype(BF16)
        moved = dot(order, stacked).reshape(rows // 2, 2 * KINDS, width)
        packed[:, 2 * MODES :] = moved.astype(BF16)

    @pl.when(block == 4)
    def _():
        for r in range(rows):
            stay_state[r] = modes[r]
        lag0, lag1 = [x * alive0 for x in q0], [x * alive0 for x in l0]
        for t in range(1, 4):
            q = [qkv[t, j].astype(F32) for j in range(3)]
            g = [
                taps[j, 0:1] * q[j] + taps[j, 1:2] * lag0[j] + taps[j, 2:3] * lag1[j]
                for j in range(3)
            ]
            prod = g[1] * g[2]
            live = alive[t] if t < 3 else None
            for r in range(rows):
                s = poles[...] * stay_state[r] + prod[r : r + 1]
                y_rows[r : r + 1] = jnp.sum(residues[...] * s, axis=0, keepdims=True)
                stay_state[r] = s * live[r : r + 1] if t < 3 else s
            gated[64 + t * rows : 80 + t * rows] = (
                g[0] * (y_rows[...] + skip[...] * prod)
            ).astype(BF16)
            if t < 3:
                lag0, lag1 = [x * live for x in q], [x * live for x in lag0]


def band_kernel(
    turns, got, taps, poles, residues, skip, sent, gated, lags, inputs, live, heads, products, y_rows
):
    groups, _, width = got.shape
    rows = 2 * groups
    kinds = got[:, 2 * MODES :].reshape(groups * 2 * KINDS, width)

    def taken(first, count, turn):
        shape = (count * rows, groups * 2 * KINDS)
        r = lax.broadcasted_iota(jnp.int32, shape, 0)
        c = lax.broadcasted_iota(jnp.int32, shape, 1)
        group = (((r & (rows - 1)) >> 1) + turn) & (groups - 1)
        source = group * (2 * KINDS) + (first + r // rows) * 2 + (r & 1)
        order = jnp.where(c == source, 1.0, 0.0).astype(BF16)
        return dot(order, kinds).reshape(count, rows, width)

    lags[...] = taken(0, 6, 0)
    for t in range(3):
        inputs[t] = taken(6 + 3 * t, 3, turns[t])
    half = width // 2
    live[0] = wide(taken(15, 1, turns[0])[0, :, :half], width)
    live[1] = wide(taken(15, 1, turns[1])[0, :, half:], width)

    @pl.loop(0, rows // 8)
    def _(i):
        at = pl.ds(pl.multiple_of(i * 8, 8), 8)
        lag0 = [lags[j, at] for j in range(3)]
        lag1 = [lags[3 + j, at] for j in range(3)]
        for t in range(3):
            q = [inputs[t, j, at] for j in range(3)]
            f = [
                taps[j, 0:1] * q[j] + taps[j, 1:2] * lag0[j] + taps[j, 2:3] * lag1[j]
                for j in range(3)
            ]
            heads[t, at] = f[0]
            products[t, at] = f[1] * f[2]
            if t < 2:
                on = live[t, at]
                lag0, lag1 = [x * on for x in q], [x * on for x in lag0]
                if t == 1:
                    for j in range(3):
                        lags[j, at] = lag0[j]

    shape = (groups * 16, 3 * rows)
    r = lax.broadcasted_iota(jnp.int32, shape, 0)
    c = lax.broadcasted_iota(jnp.int32, shape, 1)
    group = ((r >> 4) - turns[2] + groups) & (groups - 1)
    source = ((r & 15) >> 1) * rows + group * 2 + (r & 1)
    order = jnp.where((c == source) & ((r & 15) < 6), 1.0, 0.0).astype(BF16)
    last = lags[0:3].reshape(3 * rows, width).astype(BF16)
    sent[:, 2 * MODES :] = dot(order, last).reshape(groups, 16, width).astype(BF16)

    @pl.loop(0, groups)
    def _(g):
        final = []
        for side in range(2):
            row = pl.ds(g * 2 + side, 1)
            s = got[g, side * MODES : (side + 1) * MODES].astype(F32)
            for t in range(3):
                product = products[t, row]
                s = poles[...] * s + product
                y = jnp.sum(residues[...] * s, axis=0, keepdims=True)
                there = ((g + turns[t]) & (groups - 1)) * 2 + side
                y_rows[t, pl.ds(there, 1)] = heads[t, row] * (y + skip[...] * product)
                if t < 2:
                    s = s * live[t, row]
            final.append(s)
        end = (g + turns[2]) & (groups - 1)
        sent[end, 0 : 2 * MODES] = jnp.concatenate(final, axis=0).astype(BF16)

    gated[...] = y_rows[...].astype(BF16)


def whole(shape):
    return pl.BlockSpec(shape, lambda *_: (0,) * len(shape))


def swap(blocks):
    return lax.all_to_all(blocks, "dp", split_axis=0, concat_axis=0, tiled=True)


def ring_sums(gated, weight, block=None):
    n = lax.axis_size("tensor")
    me = lax.axis_index("tensor")
    own_cols = weight.shape[1] // n
    half = gated.shape[0] // 2

    def piece(away, rows):
        return dot(rows, lax.dynamic_slice_in_dim(weight, ((me + away) % n) * own_cols, own_cols, 1))

    def pass_on(right, left):
        right = lax.ppermute(right, "tensor", [(i, (i + 1) % n) for i in range(n)])
        left = lax.ppermute(left, "tensor", [(i, (i - 1) % n) for i in range(n)])
        return right, left

    far = piece(n // 2, gated).astype(BF16)
    right, left = pass_on(far[:half], far[half:])
    ahead, behind = piece(n // 2 - 1, gated), piece(1 - n // 2, gated)
    for away in range(n // 2 - 1, 0, -1):
        right, left, gated, block = lax.optimization_barrier((right, left, gated, block))
        if right.shape[0] == half:
            if block is not None:
                block = swap(block)
            ahead = jnp.concatenate([ahead[:half] + right.astype(F32), ahead[half:]], axis=0)
            behind = jnp.concatenate([behind[:half], behind[half:] + left.astype(F32)], axis=0)
            swapped, block = block, None
        else:
            ahead, behind = ahead + right.astype(F32), behind + left.astype(F32)
        right, left = pass_on(ahead.astype(BF16), behind.astype(BF16))
        ahead = lax.optimization_barrier(piece(away - 1, gated))
        behind = lax.optimization_barrier(piece(1 - away, gated)) if away > 1 else None
    total = ahead + right.astype(F32) + left.astype(F32)
    return total if swapped is None else lax.optimization_barrier((total, swapped))


def row_scales(own):
    n = lax.axis_size("tensor")
    squares = jnp.concatenate([jnp.sum(x * x, axis=1) for x in own])
    away = 1
    while away < n:
        pairs = [(i, (i + away) % n) for i in range(n)]
        squares = squares + lax.ppermute(squares, "tensor", pairs)
        away *= 2
    return lax.rsqrt(squares / (n * own[0].shape[1]) + 1e-05)[:, None]


def per_device(
    qkv,
    fir_buffer,
    fir_taps,
    modal_state,
    poles,
    residues,
    skip,
    out_weight,
    norm_gain,
    finished,
    dest_group,
):
    groups = lax.axis_size("dp")
    own_group = lax.axis_index("dp")
    slots, width = modal_state.shape[0], modal_state.shape[2]
    moving = groups * CAP
    qkv_kinds = jnp.transpose(qkv, (0, 2, 1, 3))
    fir_kinds = jnp.transpose(fir_buffer, (1, 2, 0, 3))
    skip_row = skip[None]
    shifts = lax.dynamic_slice_in_dim(dest_group, own_group * CAP, 1, 1)[:, 0] - own_group + groups
    turns = jnp.cumsum(shifts).astype(jnp.int32) % groups

    packed, gated_home, stay_state = pl.pallas_call(
        home_kernel,
        grid=(slots // 16,),
        in_specs=[
            pl.BlockSpec((4, 3, 16, width), lambda i: (0, 0, i, 0)),
            pl.BlockSpec((3, 2, 16, width), lambda i: (0, 0, i, 0)),
            whole((3, 3, width)),
            pl.BlockSpec((16, MODES, width), lambda i: (i, 0, 0)),
            whole((MODES, width)),
            whole((MODES, width)),
            whole((1, width)),
            whole((3, slots)),
        ],
        out_specs=[
            pl.BlockSpec((8, 2 * MODES + 2 * KINDS, width), lambda i: (jnp.minimum(i, 3), 0, 0)),
            whole((slots + 48, width)),
            whole((16, MODES, width)),
        ],
        out_shape=[
            jax.ShapeDtypeStruct((groups, 2 * MODES + 2 * KINDS, width), BF16),
            jax.ShapeDtypeStruct((slots + 48, width), BF16),
            jax.ShapeDtypeStruct((16, MODES, width), F32),
        ],
        scratch_shapes=[pltpu.VMEM((16, width), F32)],
        compiler_params=pltpu.CompilerParams(vmem_limit_bytes=56 * 1024 * 1024),
        name="home_rows",
    )(qkv_kinds, fir_kinds, fir_taps, modal_state, poles, residues, skip_row, finished)

    got = swap(packed)
    own_home = ring_sums(gated_home, out_weight)
    got, own_home = lax.optimization_barrier((got, own_home))

    sent, gated_band = pl.pallas_call(
        band_kernel,
        in_specs=[pl.BlockSpec(memory_space=pltpu.SMEM)]
        + [pl.BlockSpec(memory_space=pltpu.VMEM)] * 5,
        out_specs=[pl.BlockSpec(memory_space=pltpu.VMEM)] * 2,
        out_shape=[
            jax.ShapeDtypeStruct((groups, 2 * MODES + 16, width), BF16),
            jax.ShapeDtypeStruct((3, moving, width), BF16),
        ],
        scratch_shapes=[
            pltpu.VMEM((6, moving, width), F32),
            pltpu.VMEM((3, 3, moving, width), F32),
            pltpu.VMEM((2, moving, width), F32),
            pltpu.VMEM((3, moving, width), F32),
            pltpu.VMEM((3, moving, width), F32),
            pltpu.VMEM((3, moving, width), F32),
        ],
        compiler_params=pltpu.CompilerParams(vmem_limit_bytes=32 * 1024 * 1024),
        name="band_rows",
    )(turns, got, fir_taps, poles, residues, skip_row)

    own_band, back = ring_sums(gated_band.reshape(3 * moving, width), out_weight, sent)
    scales = row_scales([own_band, own_home])
    mixed_band = (own_band * scales[: 3 * moving] * norm_gain[None]).astype(BF16)
    own_cols = norm_gain.shape[0]
    mixed_band = jnp.transpose(mixed_band.reshape(3, groups, CAP, own_cols), (1, 0, 2, 3))
    mixed_back = swap(mixed_band)
    mixed_later = jnp.transpose(mixed_back, (1, 0, 2, 3)).reshape(3, moving, own_cols)
    mixed_home = (own_home * scales[3 * moving :] * norm_gain[None]).astype(BF16)
    mixed_stay = mixed_home[slots:].reshape(3, 16, own_cols)
    mixed = jnp.concatenate(
        [mixed_home[None, :slots], jnp.concatenate([mixed_later, mixed_stay], axis=1)], axis=0
    )

    moved_state = back[:, : 2 * MODES].reshape(moving, MODES, width).astype(F32)
    final_state = jnp.concatenate([moved_state, stay_state], axis=0)
    moved_lag = back[:, 2 * MODES : 2 * MODES + 6].reshape(groups, 3, CAP, width)
    moved_lag = jnp.transpose(moved_lag, (0, 2, 1, 3)).reshape(moving, 3, width)
    stay_alive = (1 - finished[2, moving:]).astype(BF16)[:, None, None]
    last_lag = jnp.concatenate([moved_lag, qkv[2, moving:] * stay_alive], axis=0)
    final_lagged = jnp.stack([qkv[3], last_lag], axis=2)
    return (mixed, final_state, final_lagged)


def solution(mesh):
    return jax.shard_map(
        per_device,
        mesh=mesh,
        in_specs=(
            P(None, "dp", None, "tensor"),
            P("dp", None, None, "tensor"),
            P(None, None, "tensor"),
            P("dp", None, "tensor"),
            P(None, "tensor"),
            P(None, "tensor"),
            P("tensor"),
            P("tensor", None),
            P("tensor"),
            P(None, "dp"),
            P(None, "dp"),
        ),
        out_specs=(P(None, "dp", "tensor"), P("dp", None, "tensor"), P("dp", None, None, "tensor")),
        check_vma=False,
    )
```

```python
import jax
import jax.numpy as jnp
from jax import lax
from jax.experimental import pallas as pl
from jax.experimental.pallas import tpu as pltpu
from jax.sharding import PartitionSpec as P

CAP = 2
MODES = 16
KINDS = 16
F32, BF16 = jnp.float32, jnp.bfloat16


def dot(a, b):
    return jnp.dot(a, b, preferred_element_type=F32)


def wide(x, width):
    return jnp.concatenate([x] * (width // x.shape[-1]), axis=-1)


def home_kernel(qkv, fir, taps, state, poles, residues, skip, finished, packed, gated, stay_state, y_rows):
    block = pl.program_id(0)
    rows, width = 16, qkv.shape[-1]
    at = lax.broadcasted_iota(jnp.int32, (rows, finished.shape[1]), 0) + block * rows
    own = at == lax.broadcasted_iota(jnp.int32, at.shape, 1)
    alive = [
        jnp.broadcast_to(
            1.0 - jnp.sum(jnp.where(own, finished[t : t + 1].astype(F32), 0.0), axis=1, keepdims=True),
            (rows, width),
        )
        for t in range(3)
    ]
    alive0 = alive[0]
    q0 = [qkv[0, j].astype(F32) for j in range(3)]
    l0 = [fir[:, j].astype(F32)[:, 0] for j in range(3)]
    l1 = [fir[:, j].astype(F32)[:, 1] for j in range(3)]
    f = [
        taps[j, 0:1] * q0[j] + taps[j, 1:2] * l0[j] + taps[j, 2:3] * l1[j]
        for j in range(3)
    ]
    product = f[1] * f[2]
    modes = []
    for r in range(rows):
        s = poles[...] * state[r] + product[r : r + 1]
        y_rows[r : r + 1] = jnp.sum(residues[...] * s, axis=0, keepdims=True)
        modes.append(s * alive0[r : r + 1])
    gated[pl.ds(block * rows, rows)] = (f[0] * (y_rows[...] + skip[...] * product)).astype(BF16)

    @pl.when(block < 4)
    def _():
        for pair in range(rows // 2):
            both = jnp.concatenate([modes[2 * pair], modes[2 * pair + 1]], axis=0)
            packed[pair, 0 : 2 * MODES] = both.astype(BF16)
        sent = [(x * alive0).astype(BF16) for x in q0 + l0]
        sent += [qkv[t, j] for t in range(1, 4) for j in range(3)]
        half = width // 2
        sent.append(jnp.concatenate([alive[1][:, :half], alive[2][:, :half]], axis=-1).astype(BF16))
        stacked = jnp.concatenate(sent, axis=0)
        n = KINDS * rows
        r = lax.broadcasted_iota(jnp.int32, (n, n), 0)
        c = lax.broadcasted_iota(jnp.int32, (n, n), 1)
        source = ((r >> 1) & 15) * rows + (r >> 5) * 2 + (r & 1)
        order = jnp.where(c == source, 1.0, 0.0).astype(BF16)
        moved = dot(order, stacked).reshape(rows // 2, 2 * KINDS, width)
        packed[:, 2 * MODES :] = moved.astype(BF16)

    @pl.when(block == 4)
    def _():
        for r in range(rows):
            stay_state[r] = modes[r]
        lag0, lag1 = [x * alive0 for x in q0], [x * alive0 for x in l0]
        for t in range(1, 4):
            q = [qkv[t, j].astype(F32) for j in range(3)]
            g = [
                taps[j, 0:1] * q[j] + taps[j, 1:2] * lag0[j] + taps[j, 2:3] * lag1[j]
                for j in range(3)
            ]
            prod = g[1] * g[2]
            live = alive[t] if t < 3 else None
            for r in range(rows):
                s = poles[...] * stay_state[r] + prod[r : r + 1]
                y_rows[r : r + 1] = jnp.sum(residues[...] * s, axis=0, keepdims=True)
                stay_state[r] = s * live[r : r + 1] if t < 3 else s
            gated[64 + t * rows : 80 + t * rows] = (
                g[0] * (y_rows[...] + skip[...] * prod)
            ).astype(BF16)
            if t < 3:
                lag0, lag1 = [x * live for x in q], [x * live for x in lag0]


def band_kernel(
    turns, place, got_hbm, weight_hbm, taps, poles, residues, skip, sent_hbm, far_hbm, part_hbm, *scratch
):
    lags, inputs, live, heads, products, y_rows, got, weight, sent, far, part, sems = scratch
    groups, _, width = got.shape
    rows = 2 * groups
    halves = [pl.ds(2 * MODES, 2 * KINDS), pl.ds(0, 2 * MODES)]
    fetches = [
        pltpu.make_async_copy(got_hbm.at[:, at], got.at[:, at], sems.at[i])
        for i, at in enumerate(halves)
    ] + [pltpu.make_async_copy(weight_hbm, weight, sems.at[2])]
    for fetch in fetches:
        fetch.start()
    fetches[0].wait()
    kinds = got[:, 2 * MODES :].reshape(groups * 2 * KINDS, width)

    def taken(first, count, turn):
        shape = (count * rows, groups * 2 * KINDS)
        r = lax.broadcasted_iota(jnp.int32, shape, 0)
        c = lax.broadcasted_iota(jnp.int32, shape, 1)
        group = (((r & (rows - 1)) >> 1) + turn) & (groups - 1)
        source = group * (2 * KINDS) + (first + r // rows) * 2 + (r & 1)
        order = jnp.where(c == source, 1.0, 0.0).astype(BF16)
        return dot(order, kinds).reshape(count, rows, width)

    lags[...] = taken(0, 6, 0)
    for t in range(3):
        inputs[t] = taken(6 + 3 * t, 3, turns[t])
    half = width // 2
    live[0] = wide(taken(15, 1, turns[0])[0, :, :half], width)
    live[1] = wide(taken(15, 1, turns[1])[0, :, half:], width)

    @pl.loop(0, rows // 8)
    def _(i):
        at = pl.ds(pl.multiple_of(i * 8, 8), 8)
        lag0 = [lags[j, at] for j in range(3)]
        lag1 = [lags[3 + j, at] for j in range(3)]
        for t in range(3):
            q = [inputs[t, j, at] for j in range(3)]
            f = [
                taps[j, 0:1] * q[j] + taps[j, 1:2] * lag0[j] + taps[j, 2:3] * lag1[j]
                for j in range(3)
            ]
            heads[t, at] = f[0]
            products[t, at] = f[1] * f[2]
            if t < 2:
                on = live[t, at]
                lag0, lag1 = [x * on for x in q], [x * on for x in lag0]
                if t == 1:
                    for j in range(3):
                        lags[j, at] = lag0[j]

    shape = (groups * 16, 3 * rows)
    r = lax.broadcasted_iota(jnp.int32, shape, 0)
    c = lax.broadcasted_iota(jnp.int32, shape, 1)
    group = ((r >> 4) - turns[2] + groups) & (groups - 1)
    source = ((r & 15) >> 1) * rows + group * 2 + (r & 1)
    order = jnp.where((c == source) & ((r & 15) < 6), 1.0, 0.0).astype(BF16)
    last = lags[0:3].reshape(3 * rows, width).astype(BF16)
    sent[:, 2 * MODES :] = dot(order, last).reshape(groups, 16, width).astype(BF16)

    fetches[1].wait()

    @pl.loop(0, groups)
    def _(g):
        final = []
        for side in range(2):
            row = pl.ds(g * 2 + side, 1)
            s = got[g, side * MODES : (side + 1) * MODES].astype(F32)
            for t in range(3):
                product = products[t, row]
                s = poles[...] * s + product
                y = jnp.sum(residues[...] * s, axis=0, keepdims=True)
                there = ((g + turns[t]) & (groups - 1)) * 2 + side
                y_rows[t, pl.ds(there, 1)] = heads[t, row] * (y + skip[...] * product)
                if t < 2:
                    s = s * live[t, row]
            final.append(s)
        end = (g + turns[2]) & (groups - 1)
        sent[end, 0 : 2 * MODES] = jnp.concatenate(final, axis=0).astype(BF16)

    stores = [pltpu.make_async_copy(sent, sent_hbm, sems.at[3])]
    stores[0].start()
    fetches[2].wait()

    gated = y_rows[...].reshape(3 * rows, width).astype(BF16)
    n, _, own_cols = part.shape
    for i in range(n):
        away = (i + n // 2) % n
        start = pl.multiple_of(((place[0] + away) % n) * own_cols, own_cols)
        made = dot(gated, weight[:, pl.ds(start, own_cols)])
        if away == n // 2:
            far[...] = made.astype(BF16)
            store = pltpu.make_async_copy(far, far_hbm, sems.at[4])
        else:
            part[away] = made
            store = pltpu.make_async_copy(part.at[away], part_hbm.at[away], sems.at[5 + away])
        store.start()
        stores.append(store)
    for store in stores:
        store.wait()


def whole(shape):
    return pl.BlockSpec(shape, lambda *_: (0,) * len(shape))


def swap(blocks):
    return lax.all_to_all(blocks, "dp", split_axis=0, concat_axis=0, tiled=True)


def ring_sums(far, part, block):
    n = part.shape[0]
    half = far.shape[0] // 2

    def pass_on(right, left):
        right = lax.ppermute(right, "tensor", [(i, (i + 1) % n) for i in range(n)])
        left = lax.ppermute(left, "tensor", [(i, (i - 1) % n) for i in range(n)])
        return right, left

    right, left = pass_on(far[:half], far[half:])
    right, left = lax.optimization_barrier((right, left))
    for away in range(n // 2 - 1, 0, -1):
        ahead, behind = part[away], part[n - away]
        if right.shape[0] == half:
            ahead = ahead.at[:half].add(right.astype(F32)).astype(BF16)
            behind = behind.at[half:].add(left.astype(F32)).astype(BF16)
            ahead, behind, block = lax.optimization_barrier((ahead, behind, block))
            right, left = pass_on(ahead, behind)
            block = swap(block)
        else:
            ahead, behind = ahead + right.astype(F32), behind + left.astype(F32)
            right, left = pass_on(ahead.astype(BF16), behind.astype(BF16))
        right, left = lax.optimization_barrier((right, left))
    return lax.optimization_barrier((part[0] + right.astype(F32) + left.astype(F32), block))


def row_scales(own):
    n = lax.axis_size("tensor")
    squares = lax.psum(jnp.concatenate([jnp.sum(x * x, axis=1) for x in own]), "tensor")
    return lax.rsqrt(squares / (n * own[0].shape[1]) + 1e-05)[:, None]


def per_device(
    qkv,
    fir_buffer,
    fir_taps,
    modal_state,
    poles,
    residues,
    skip,
    out_weight,
    norm_gain,
    finished,
    dest_group,
):
    groups = lax.axis_size("dp")
    own_group = lax.axis_index("dp")
    slots, width = modal_state.shape[0], modal_state.shape[2]
    moving = groups * CAP
    qkv_kinds = jnp.transpose(qkv, (0, 2, 1, 3))
    skip_row = skip[None]
    shifts = lax.dynamic_slice_in_dim(dest_group, own_group * CAP, 1, 1)[:, 0] - own_group + groups
    turns = jnp.cumsum(shifts).astype(jnp.int32) % groups

    packed, gated_home, stay_state = pl.pallas_call(
        home_kernel,
        grid=(slots // 16,),
        in_specs=[
            pl.BlockSpec((4, 3, 16, width), lambda i: (0, 0, i, 0)),
            pl.BlockSpec((16, 3, 2, width), lambda i: (i, 0, 0, 0)),
            whole((3, 3, width)),
            pl.BlockSpec((16, MODES, width), lambda i: (i, 0, 0)),
            whole((MODES, width)),
            whole((MODES, width)),
            whole((1, width)),
            whole((3, slots)),
        ],
        out_specs=[
            pl.BlockSpec((8, 2 * MODES + 2 * KINDS, width), lambda i: (jnp.minimum(i, 3), 0, 0)),
            whole((slots + 48, width)),
            whole((16, MODES, width)),
        ],
        out_shape=[
            jax.ShapeDtypeStruct((groups, 2 * MODES + 2 * KINDS, width), BF16),
            jax.ShapeDtypeStruct((slots + 48, width), BF16),
            jax.ShapeDtypeStruct((16, MODES, width), F32),
        ],
        scratch_shapes=[pltpu.VMEM((16, width), F32)],
        compiler_params=pltpu.CompilerParams(vmem_limit_bytes=56 * 1024 * 1024),
        name="home_rows",
    )(qkv_kinds, fir_buffer, fir_taps, modal_state, poles, residues, skip_row, finished)

    got = swap(packed)
    own_home = lax.psum_scatter(
        dot(gated_home, out_weight), "tensor", scatter_dimension=1, tiled=True
    )

    n, own_cols = lax.axis_size("tensor"), norm_gain.shape[0]
    place = lax.axis_index("tensor").astype(jnp.int32)[None]
    sent, far, part = pl.pallas_call(
        band_kernel,
        in_specs=[pl.BlockSpec(memory_space=pltpu.SMEM)] * 2
        + [pl.BlockSpec(memory_space=pl.ANY)] * 2
        + [pl.BlockSpec(memory_space=pltpu.VMEM)] * 4,
        out_specs=[pl.BlockSpec(memory_space=pl.ANY)] * 3,
        out_shape=[
            jax.ShapeDtypeStruct((groups, 2 * MODES + 16, width), BF16),
            jax.ShapeDtypeStruct((3 * moving, own_cols), BF16),
            jax.ShapeDtypeStruct((n, 3 * moving, own_cols), F32),
        ],
        scratch_shapes=[
            pltpu.VMEM((6, moving, width), F32),
            pltpu.VMEM((3, 3, moving, width), F32),
            pltpu.VMEM((2, moving, width), F32),
            pltpu.VMEM((3, moving, width), F32),
            pltpu.VMEM((3, moving, width), F32),
            pltpu.VMEM((3, moving, width), F32),
            pltpu.VMEM(got.shape, BF16),
            pltpu.VMEM(out_weight.shape, BF16),
            pltpu.VMEM((groups, 2 * MODES + 16, width), BF16),
            pltpu.VMEM((3 * moving, own_cols), BF16),
            pltpu.VMEM((n, 3 * moving, own_cols), F32),
            pltpu.SemaphoreType.DMA((5 + n,)),
        ],
        compiler_params=pltpu.CompilerParams(vmem_limit_bytes=40 * 1024 * 1024),
        name="band_rows",
    )(turns, place, got, out_weight, fir_taps, poles, residues, skip_row)

    own_band, back = ring_sums(far, part, sent)
    scales = row_scales([own_band, own_home])
    mixed_band = (own_band * scales[: 3 * moving] * norm_gain[None]).astype(BF16)
    back, mixed_band = lax.optimization_barrier((back, mixed_band))
    mixed_band = jnp.transpose(mixed_band.reshape(3, groups, CAP, own_cols), (1, 0, 2, 3))
    mixed_back = swap(mixed_band)
    mixed_later = jnp.transpose(mixed_back, (1, 0, 2, 3)).reshape(3, moving, own_cols)
    mixed_home = (own_home * scales[3 * moving :] * norm_gain[None]).astype(BF16)
    mixed_stay = mixed_home[slots:].reshape(3, 16, own_cols)
    mixed = jnp.concatenate(
        [mixed_home[None, :slots], jnp.concatenate([mixed_later, mixed_stay], axis=1)], axis=0
    )

    moved_state = back[:, : 2 * MODES].reshape(moving, MODES, width).astype(F32)
    final_state = jnp.concatenate([moved_state, stay_state], axis=0)
    moved_lag = back[:, 2 * MODES : 2 * MODES + 6].reshape(groups, 3, CAP, width)
    moved_lag = jnp.transpose(moved_lag, (0, 2, 1, 3)).reshape(moving, 3, width)
    stay_alive = (1 - finished[2, moving:]).astype(BF16)[:, None, None]
    last_lag = jnp.concatenate([moved_lag, qkv[2, moving:] * stay_alive], axis=0)
    final_lagged = jnp.stack([qkv[3], last_lag], axis=2)
    return (mixed, final_state, final_lagged)


def solution(mesh):
    return jax.shard_map(
        per_device,
        mesh=mesh,
        in_specs=(
            P(None, "dp", None, "tensor"),
            P("dp", None, None, "tensor"),
            P(None, None, "tensor"),
            P("dp", None, "tensor"),
            P(None, "tensor"),
            P(None, "tensor"),
            P("tensor"),
            P("tensor", None),
            P("tensor"),
            P(None, "dp"),
            P(None, "dp"),
        ),
        out_specs=(P(None, "dp", "tensor"), P("dp", None, "tensor"), P("dp", None, None, "tensor")),
        check_vma=False,
    )
```

```python
import jax
import jax.numpy as jnp
from jax import lax
from jax.experimental import pallas as pl
from jax.experimental.pallas import tpu as pltpu
from jax.sharding import PartitionSpec as P

CAP = 2
MODES = 16
KINDS = 16
F32, BF16 = jnp.float32, jnp.bfloat16


def dot(a, b):
    return jnp.dot(a, b, preferred_element_type=F32)


def wide(x, width):
    return jnp.concatenate([x] * (width // x.shape[-1]), axis=-1)


def home_kernel(qkv, fir, taps, state, poles, residues, skip, finished, packed, gated, stay_state, y_rows):
    block = pl.program_id(0)
    rows, width = 16, qkv.shape[-1]
    at = lax.broadcasted_iota(jnp.int32, (rows, finished.shape[1]), 0) + block * rows
    own = at == lax.broadcasted_iota(jnp.int32, at.shape, 1)
    alive = [
        jnp.broadcast_to(
            1.0 - jnp.sum(jnp.where(own, finished[t : t + 1].astype(F32), 0.0), axis=1, keepdims=True),
            (rows, width),
        )
        for t in range(3)
    ]
    alive0 = alive[0]
    q0 = [qkv[0, j].astype(F32) for j in range(3)]
    l0 = [fir[:, j].astype(F32)[:, 0] for j in range(3)]
    l1 = [fir[:, j].astype(F32)[:, 1] for j in range(3)]
    f = [
        taps[j, 0:1] * q0[j] + taps[j, 1:2] * l0[j] + taps[j, 2:3] * l1[j]
        for j in range(3)
    ]
    product = f[1] * f[2]
    modes = []
    for r in range(rows):
        s = poles[...] * state[r] + product[r : r + 1]
        y_rows[r : r + 1] = jnp.sum(residues[...] * s, axis=0, keepdims=True)
        modes.append(s * alive0[r : r + 1])
    gated[pl.ds(block * rows, rows)] = (f[0] * (y_rows[...] + skip[...] * product)).astype(BF16)

    @pl.when(block < 4)
    def _():
        for pair in range(rows // 2):
            both = jnp.concatenate([modes[2 * pair], modes[2 * pair + 1]], axis=0)
            packed[pair, 0 : 2 * MODES] = both.astype(BF16)
        sent = [(x * alive0).astype(BF16) for x in q0 + l0]
        sent += [qkv[t, j] for t in range(1, 4) for j in range(3)]
        half = width // 2
        sent.append(jnp.concatenate([alive[1][:, :half], alive[2][:, :half]], axis=-1).astype(BF16))
        stacked = jnp.concatenate(sent, axis=0)
        n = KINDS * rows
        r = lax.broadcasted_iota(jnp.int32, (n, n), 0)
        c = lax.broadcasted_iota(jnp.int32, (n, n), 1)
        source = ((r >> 1) & 15) * rows + (r >> 5) * 2 + (r & 1)
        order = jnp.where(c == source, 1.0, 0.0).astype(BF16)
        moved = dot(order, stacked).reshape(rows // 2, 2 * KINDS, width)
        packed[:, 2 * MODES :] = moved.astype(BF16)

    @pl.when(block == 4)
    def _():
        for r in range(rows):
            stay_state[r] = modes[r]
        lag0, lag1 = [x * alive0 for x in q0], [x * alive0 for x in l0]
        for t in range(1, 4):
            q = [qkv[t, j].astype(F32) for j in range(3)]
            g = [
                taps[j, 0:1] * q[j] + taps[j, 1:2] * lag0[j] + taps[j, 2:3] * lag1[j]
                for j in range(3)
            ]
            prod = g[1] * g[2]
            live = alive[t] if t < 3 else None
            for r in range(rows):
                s = poles[...] * stay_state[r] + prod[r : r + 1]
                y_rows[r : r + 1] = jnp.sum(residues[...] * s, axis=0, keepdims=True)
                stay_state[r] = s * live[r : r + 1] if t < 3 else s
            gated[64 + t * rows : 80 + t * rows] = (
                g[0] * (y_rows[...] + skip[...] * prod)
            ).astype(BF16)
            if t < 3:
                lag0, lag1 = [x * live for x in q], [x * live for x in lag0]


def band_kernel(
    turns, got_hbm, taps, poles, residues, skip, far_weight, sent, gated, far, *scratch
):
    lags, inputs, live, heads, products, y_rows, got, sems = scratch
    groups, _, width = got.shape
    rows = 2 * groups
    halves = [pl.ds(2 * MODES, 2 * KINDS), pl.ds(0, 2 * MODES)]
    fetches = [
        pltpu.make_async_copy(got_hbm.at[:, at], got.at[:, at], sems.at[i])
        for i, at in enumerate(halves)
    ]
    for fetch in fetches:
        fetch.start()
    fetches[0].wait()
    kinds = got[:, 2 * MODES :].reshape(groups * 2 * KINDS, width)

    def taken(first, count, turn):
        shape = (count * rows, groups * 2 * KINDS)
        r = lax.broadcasted_iota(jnp.int32, shape, 0)
        c = lax.broadcasted_iota(jnp.int32, shape, 1)
        group = (((r & (rows - 1)) >> 1) + turn) & (groups - 1)
        source = group * (2 * KINDS) + (first + r // rows) * 2 + (r & 1)
        order = jnp.where(c == source, 1.0, 0.0).astype(BF16)
        return dot(order, kinds).reshape(count, rows, width)

    lags[...] = taken(0, 6, 0)
    for t in range(3):
        inputs[t] = taken(6 + 3 * t, 3, turns[t])
    half = width // 2
    live[0] = wide(taken(15, 1, turns[0])[0, :, :half], width)
    live[1] = wide(taken(15, 1, turns[1])[0, :, half:], width)

    @pl.loop(0, rows // 8)
    def _(i):
        at = pl.ds(pl.multiple_of(i * 8, 8), 8)
        lag0 = [lags[j, at] for j in range(3)]
        lag1 = [lags[3 + j, at] for j in range(3)]
        for t in range(3):
            q = [inputs[t, j, at] for j in range(3)]
            f = [
                taps[j, 0:1] * q[j] + taps[j, 1:2] * lag0[j] + taps[j, 2:3] * lag1[j]
                for j in range(3)
            ]
            heads[t, at] = f[0]
            products[t, at] = f[1] * f[2]
            if t < 2:
                on = live[t, at]
                lag0, lag1 = [x * on for x in q], [x * on for x in lag0]
                if t == 1:
                    for j in range(3):
                        lags[j, at] = lag0[j]

    shape = (groups * 16, 3 * rows)
    r = lax.broadcasted_iota(jnp.int32, shape, 0)
    c = lax.broadcasted_iota(jnp.int32, shape, 1)
    group = ((r >> 4) - turns[2] + groups) & (groups - 1)
    source = ((r & 15) >> 1) * rows + group * 2 + (r & 1)
    order = jnp.where((c == source) & ((r & 15) < 6), 1.0, 0.0).astype(BF16)
    last = lags[0:3].reshape(3 * rows, width).astype(BF16)
    sent[:, 2 * MODES :] = dot(order, last).reshape(groups, 16, width).astype(BF16)

    fetches[1].wait()

    @pl.loop(0, groups)
    def _(g):
        final = []
        for side in range(2):
            row = pl.ds(g * 2 + side, 1)
            s = got[g, side * MODES : (side + 1) * MODES].astype(F32)
            for t in range(3):
                product = products[t, row]
                s = poles[...] * s + product
                y = jnp.sum(residues[...] * s, axis=0, keepdims=True)
                there = ((g + turns[t]) & (groups - 1)) * 2 + side
                y_rows[t, pl.ds(there, 1)] = heads[t, row] * (y + skip[...] * product)
                if t < 2:
                    s = s * live[t, row]
            final.append(s)
        end = (g + turns[2]) & (groups - 1)
        sent[end, 0 : 2 * MODES] = jnp.concatenate(final, axis=0).astype(BF16)

    gated[...] = y_rows[...].reshape(3 * rows, width).astype(BF16)
    far[...] = dot(gated[...], far_weight[...]).astype(BF16)


def products_kernel(place, gated, weight, part):
    part[0] = dot(gated[...], weight[...])


def products(place, gated, weight, n):
    rows, width = gated.shape
    own_cols = weight.shape[1] // n

    def away(i):
        return (n // 2 + 1 + i) % n

    return pl.pallas_call(
        products_kernel,
        grid_spec=pltpu.PrefetchScalarGridSpec(
            num_scalar_prefetch=1,
            grid=(n - 1,),
            in_specs=[
                whole((rows, width)),
                pl.BlockSpec((width, own_cols), lambda i, place: (0, (place[0] + away(i)) % n)),
            ],
            out_specs=pl.BlockSpec((1, rows, own_cols), lambda i, place: (away(i), 0, 0)),
        ),
        out_shape=jax.ShapeDtypeStruct((n, rows, own_cols), F32),
        cost_estimate=pl.CostEstimate(
            flops=16 * rows * width * weight.shape[1], bytes_accessed=2 * weight.size, transcendentals=0
        ),
        compiler_params=pltpu.CompilerParams(vmem_limit_bytes=56 * 1024 * 1024),
        name="ring_products",
    )(place, gated, weight)


def finish_kernel(back, qkv, stay_state, finished, state, lagged):
    block = pl.program_id(0)
    rows, width = 16, qkv.shape[-1]

    def put(j, last):
        both = [qkv[1, j].astype(F32)[:, None], last[:, None]]
        lagged[:, j] = jnp.concatenate(both, axis=1).astype(BF16)

    @pl.when(block < 4)
    def _():
        n = back.shape[0]
        for b in range(n):
            for side in range(2):
                state[2 * b + side] = back[b, side * MODES : (side + 1) * MODES].astype(F32)
        shape = (3 * rows, n * 16)
        r = lax.broadcasted_iota(jnp.int32, shape, 0)
        c = lax.broadcasted_iota(jnp.int32, shape, 1)
        source = ((r & 15) >> 1) * 16 + (r >> 4) * 2 + (r & 1)
        order = jnp.where(c == source, 1.0, 0.0).astype(BF16)
        last = dot(order, back[:, 2 * MODES :].reshape(n * 16, width))
        for j in range(3):
            put(j, last[j * rows : (j + 1) * rows])

    @pl.when(block == 4)
    def _():
        state[...] = stay_state[...]
        at = lax.broadcasted_iota(jnp.int32, (rows, finished.shape[1]), 0) + block * rows
        own = at == lax.broadcasted_iota(jnp.int32, at.shape, 1)
        ended = jnp.where(own, finished[2:3].astype(F32), 0.0)
        alive = 1.0 - jnp.sum(ended, axis=1, keepdims=True)
        for j in range(3):
            put(j, qkv[0, j].astype(F32) * alive)


def whole(shape):
    return pl.BlockSpec(shape, lambda *_: (0,) * len(shape))


def swap(blocks):
    return lax.all_to_all(blocks, "dp", split_axis=0, concat_axis=0, tiled=True)


def ring_sums(far, part, block=None):
    n = part.shape[0]
    half = far.shape[0] // 2

    def pass_on(right, left):
        right = lax.ppermute(right, "tensor", [(i, (i + 1) % n) for i in range(n)])
        left = lax.ppermute(left, "tensor", [(i, (i - 1) % n) for i in range(n)])
        return lax.optimization_barrier((right, left))

    right, left = pass_on(far[:half], far[half:])
    if block is not None:
        part, block = lax.optimization_barrier((part, block))
        block = swap(block)
    for away in range(n // 2 - 1, 0, -1):
        ahead, behind = part[away], part[n - away]
        if right.shape[0] == half:
            ahead = ahead.at[:half].add(right.astype(F32))
            behind = behind.at[half:].add(left.astype(F32))
        else:
            ahead, behind = ahead + right.astype(F32), behind + left.astype(F32)
        right, left = pass_on(ahead.astype(BF16), behind.astype(BF16))
    total = part[0] + right.astype(F32) + left.astype(F32)
    return total if block is None else lax.optimization_barrier((total, block))


def row_scales(own):
    n = lax.axis_size("tensor")
    squares = lax.psum(jnp.concatenate([jnp.sum(x * x, axis=1) for x in own]), "tensor")
    return lax.rsqrt(squares / (n * own[0].shape[1]) + 1e-05)[:, None]


def per_device(
    qkv,
    fir_buffer,
    fir_taps,
    modal_state,
    poles,
    residues,
    skip,
    out_weight,
    norm_gain,
    finished,
    dest_group,
):
    groups = lax.axis_size("dp")
    own_group = lax.axis_index("dp")
    slots, width = modal_state.shape[0], modal_state.shape[2]
    moving = groups * CAP
    qkv_kinds = jnp.transpose(qkv, (0, 2, 1, 3))
    skip_row = skip[None]
    shifts = lax.dynamic_slice_in_dim(dest_group, own_group * CAP, 1, 1)[:, 0] - own_group + groups
    turns = jnp.cumsum(shifts).astype(jnp.int32) % groups

    packed, gated_home, stay_state = pl.pallas_call(
        home_kernel,
        grid=(slots // 16,),
        in_specs=[
            pl.BlockSpec((4, 3, 16, width), lambda i: (0, 0, i, 0)),
            pl.BlockSpec((16, 3, 2, width), lambda i: (i, 0, 0, 0)),
            whole((3, 3, width)),
            pl.BlockSpec((16, MODES, width), lambda i: (i, 0, 0)),
            whole((MODES, width)),
            whole((MODES, width)),
            whole((1, width)),
            whole((3, slots)),
        ],
        out_specs=[
            pl.BlockSpec((8, 2 * MODES + 2 * KINDS, width), lambda i: (jnp.minimum(i, 3), 0, 0)),
            whole((slots + 48, width)),
            whole((16, MODES, width)),
        ],
        out_shape=[
            jax.ShapeDtypeStruct((groups, 2 * MODES + 2 * KINDS, width), BF16),
            jax.ShapeDtypeStruct((slots + 48, width), BF16),
            jax.ShapeDtypeStruct((16, MODES, width), F32),
        ],
        scratch_shapes=[pltpu.VMEM((16, width), F32)],
        compiler_params=pltpu.CompilerParams(vmem_limit_bytes=56 * 1024 * 1024),
        name="home_rows",
    )(qkv_kinds, fir_buffer, fir_taps, modal_state, poles, residues, skip_row, finished)

    n, own_cols = lax.axis_size("tensor"), norm_gain.shape[0]
    place = lax.axis_index("tensor").astype(jnp.int32)[None]
    far_weight = lax.dynamic_slice_in_dim(
        out_weight, ((place[0] + n // 2) % n) * own_cols, own_cols, 1
    )
    got = swap(packed)
    own_home = ring_sums(
        dot(gated_home, far_weight).astype(BF16), products(place, gated_home, out_weight, n)
    )
    got, own_home = lax.optimization_barrier((got, own_home))

    sent, gated_band, far = pl.pallas_call(
        band_kernel,
        in_specs=[
            pl.BlockSpec(memory_space=pltpu.SMEM),
            pl.BlockSpec(memory_space=pl.ANY),
        ]
        + [pl.BlockSpec(memory_space=pltpu.VMEM)] * 5,
        out_specs=[pl.BlockSpec(memory_space=pltpu.VMEM)] * 3,
        out_shape=[
            jax.ShapeDtypeStruct((groups, 2 * MODES + 16, width), BF16),
            jax.ShapeDtypeStruct((3 * moving, width), BF16),
            jax.ShapeDtypeStruct((3 * moving, own_cols), BF16),
        ],
        scratch_shapes=[
            pltpu.VMEM((6, moving, width), F32),
            pltpu.VMEM((3, 3, moving, width), F32),
            pltpu.VMEM((2, moving, width), F32),
            pltpu.VMEM((3, moving, width), F32),
            pltpu.VMEM((3, moving, width), F32),
            pltpu.VMEM((3, moving, width), F32),
            pltpu.VMEM(got.shape, BF16),
            pltpu.SemaphoreType.DMA((2,)),
        ],
        compiler_params=pltpu.CompilerParams(vmem_limit_bytes=40 * 1024 * 1024),
        name="band_rows",
    )(turns, got, fir_taps, poles, residues, skip_row, far_weight)

    own_band, back = ring_sums(far, products(place, gated_band, out_weight, n), sent)
    scales = row_scales([own_band, own_home])
    mixed_band = (own_band * scales[: 3 * moving] * norm_gain[None]).astype(BF16)
    mixed_band = jnp.transpose(mixed_band.reshape(3, groups, CAP, own_cols), (1, 0, 2, 3))
    back, mixed_band = lax.optimization_barrier((back, mixed_band))
    mixed_back = swap(mixed_band)
    final_state, final_lagged = pl.pallas_call(
        finish_kernel,
        grid=(slots // 16,),
        in_specs=[
            pl.BlockSpec((8, 2 * MODES + 16, width), lambda i: (jnp.minimum(i, 3), 0, 0)),
            pl.BlockSpec((2, 3, 16, width), lambda i: (1, 0, i, 0)),
            whole((16, MODES, width)),
            whole((3, slots)),
        ],
        out_specs=[
            pl.BlockSpec((16, MODES, width), lambda i: (i, 0, 0)),
            pl.BlockSpec((16, 3, 2, width), lambda i: (i, 0, 0, 0)),
        ],
        out_shape=[
            jax.ShapeDtypeStruct(modal_state.shape, F32),
            jax.ShapeDtypeStruct(fir_buffer.shape, BF16),
        ],
        compiler_params=pltpu.CompilerParams(vmem_limit_bytes=56 * 1024 * 1024),
        name="last_rows",
    )(back, qkv_kinds, stay_state, finished)

    mixed_later = jnp.transpose(mixed_back, (1, 0, 2, 3)).reshape(3, moving, own_cols)
    mixed_home = (own_home * scales[3 * moving :] * norm_gain[None]).astype(BF16)
    mixed_stay = mixed_home[slots:].reshape(3, 16, own_cols)
    mixed = jnp.concatenate(
        [mixed_home[None, :slots], jnp.concatenate([mixed_later, mixed_stay], axis=1)], axis=0
    )
    return (mixed, final_state, final_lagged)


def solution(mesh):
    return jax.shard_map(
        per_device,
        mesh=mesh,
        in_specs=(
            P(None, "dp", None, "tensor"),
            P("dp", None, None, "tensor"),
            P(None, None, "tensor"),
            P("dp", None, "tensor"),
            P(None, "tensor"),
            P(None, "tensor"),
            P("tensor"),
            P("tensor", None),
            P("tensor"),
            P(None, "dp"),
            P(None, "dp"),
        ),
        out_specs=(P(None, "dp", "tensor"), P("dp", None, "tensor"), P("dp", None, None, "tensor")),
        check_vma=False,
    )
```

```python
import jax
import jax.numpy as jnp
from jax import lax
from jax.experimental import pallas as pl
from jax.experimental.pallas import tpu as pltpu
from jax.sharding import PartitionSpec as P

CAP = 2
MODES = 16
KINDS = 16
F32, BF16 = jnp.float32, jnp.bfloat16


def dot(a, b):
    return jnp.dot(a, b, preferred_element_type=F32)


def wide(x, width):
    return jnp.concatenate([x] * (width // x.shape[-1]), axis=-1)


def home_kernel(qkv, fir, taps, state, poles, residues, skip, finished, packed, gated, stay_state, y_rows):
    block = pl.program_id(0)
    rows, width = 16, qkv.shape[-1]
    at = lax.broadcasted_iota(jnp.int32, (rows, finished.shape[1]), 0) + block * rows
    own = at == lax.broadcasted_iota(jnp.int32, at.shape, 1)
    alive = [
        jnp.broadcast_to(
            1.0 - jnp.sum(jnp.where(own, finished[t : t + 1].astype(F32), 0.0), axis=1, keepdims=True),
            (rows, width),
        )
        for t in range(3)
    ]
    alive0 = alive[0]
    q0 = [qkv[0, j].astype(F32) for j in range(3)]
    l0 = [fir[:, j].astype(F32)[:, 0] for j in range(3)]
    l1 = [fir[:, j].astype(F32)[:, 1] for j in range(3)]
    f = [
        taps[j, 0:1] * q0[j] + taps[j, 1:2] * l0[j] + taps[j, 2:3] * l1[j]
        for j in range(3)
    ]
    product = f[1] * f[2]
    modes = []
    for r in range(rows):
        s = poles[...] * state[r] + product[r : r + 1]
        y_rows[r : r + 1] = jnp.sum(residues[...] * s, axis=0, keepdims=True)
        modes.append(s * alive0[r : r + 1])
    gated[pl.ds(block * rows, rows)] = (f[0] * (y_rows[...] + skip[...] * product)).astype(BF16)

    @pl.when(block < 4)
    def _():
        for pair in range(rows // 2):
            both = jnp.concatenate([modes[2 * pair], modes[2 * pair + 1]], axis=0)
            packed[pair, 0 : 2 * MODES] = both.astype(BF16)
        sent = [(x * alive0).astype(BF16) for x in q0 + l0]
        sent += [qkv[t, j] for t in range(1, 4) for j in range(3)]
        half = width // 2
        sent.append(jnp.concatenate([alive[1][:, :half], alive[2][:, :half]], axis=-1).astype(BF16))
        stacked = jnp.concatenate(sent, axis=0)
        n = KINDS * rows
        r = lax.broadcasted_iota(jnp.int32, (n, n), 0)
        c = lax.broadcasted_iota(jnp.int32, (n, n), 1)
        source = ((r >> 1) & 15) * rows + (r >> 5) * 2 + (r & 1)
        order = jnp.where(c == source, 1.0, 0.0).astype(BF16)
        moved = dot(order, stacked).reshape(rows // 2, 2 * KINDS, width)
        packed[:, 2 * MODES :] = moved.astype(BF16)

    @pl.when(block == 4)
    def _():
        for r in range(rows):
            stay_state[r] = modes[r]
        lag0, lag1 = [x * alive0 for x in q0], [x * alive0 for x in l0]
        for t in range(1, 4):
            q = [qkv[t, j].astype(F32) for j in range(3)]
            g = [
                taps[j, 0:1] * q[j] + taps[j, 1:2] * lag0[j] + taps[j, 2:3] * lag1[j]
                for j in range(3)
            ]
            prod = g[1] * g[2]
            live = alive[t] if t < 3 else None
            for r in range(rows):
                s = poles[...] * stay_state[r] + prod[r : r + 1]
                y_rows[r : r + 1] = jnp.sum(residues[...] * s, axis=0, keepdims=True)
                stay_state[r] = s * live[r : r + 1] if t < 3 else s
            gated[64 + t * rows : 80 + t * rows] = (
                g[0] * (y_rows[...] + skip[...] * prod)
            ).astype(BF16)
            if t < 3:
                lag0, lag1 = [x * live for x in q], [x * live for x in lag0]


def band_kernel(
    turns, got_hbm, taps, poles, residues, skip, far_weight, sent, gated, far, *scratch
):
    lags, inputs, live, heads, products, y_rows, got, sems = scratch
    groups, _, width = got.shape
    rows = 2 * groups
    halves = [pl.ds(2 * MODES, 2 * KINDS), pl.ds(0, 2 * MODES)]
    fetches = [
        pltpu.make_async_copy(got_hbm.at[:, at], got.at[:, at], sems.at[i])
        for i, at in enumerate(halves)
    ]
    for fetch in fetches:
        fetch.start()
    fetches[0].wait()
    kinds = got[:, 2 * MODES :].reshape(groups * 2 * KINDS, width)

    def taken(first, count, turn):
        shape = (count * rows, groups * 2 * KINDS)
        r = lax.broadcasted_iota(jnp.int32, shape, 0)
        c = lax.broadcasted_iota(jnp.int32, shape, 1)
        group = (((r & (rows - 1)) >> 1) + turn) & (groups - 1)
        source = group * (2 * KINDS) + (first + r // rows) * 2 + (r & 1)
        order = jnp.where(c == source, 1.0, 0.0).astype(BF16)
        return dot(order, kinds).reshape(count, rows, width)

    lags[...] = taken(0, 6, 0)
    for t in range(3):
        inputs[t] = taken(6 + 3 * t, 3, turns[t])
    half = width // 2
    live[0] = wide(taken(15, 1, turns[0])[0, :, :half], width)
    live[1] = wide(taken(15, 1, turns[1])[0, :, half:], width)

    @pl.loop(0, rows // 8)
    def _(i):
        at = pl.ds(pl.multiple_of(i * 8, 8), 8)
        lag0 = [lags[j, at] for j in range(3)]
        lag1 = [lags[3 + j, at] for j in range(3)]
        for t in range(3):
            q = [inputs[t, j, at] for j in range(3)]
            f = [
                taps[j, 0:1] * q[j] + taps[j, 1:2] * lag0[j] + taps[j, 2:3] * lag1[j]
                for j in range(3)
            ]
            heads[t, at] = f[0]
            products[t, at] = f[1] * f[2]
            if t < 2:
                on = live[t, at]
                lag0, lag1 = [x * on for x in q], [x * on for x in lag0]
                if t == 1:
                    for j in range(3):
                        lags[j, at] = lag0[j]

    shape = (groups * 16, 3 * rows)
    r = lax.broadcasted_iota(jnp.int32, shape, 0)
    c = lax.broadcasted_iota(jnp.int32, shape, 1)
    group = ((r >> 4) - turns[2] + groups) & (groups - 1)
    source = ((r & 15) >> 1) * rows + group * 2 + (r & 1)
    order = jnp.where((c == source) & ((r & 15) < 6), 1.0, 0.0).astype(BF16)
    last = lags[0:3].reshape(3 * rows, width).astype(BF16)
    sent[:, 2 * MODES :] = dot(order, last).reshape(groups, 16, width).astype(BF16)

    fetches[1].wait()

    @pl.loop(0, groups)
    def _(g):
        final = []
        for side in range(2):
            row = pl.ds(g * 2 + side, 1)
            s = got[g, side * MODES : (side + 1) * MODES].astype(F32)
            for t in range(3):
                product = products[t, row]
                s = poles[...] * s + product
                y = jnp.sum(residues[...] * s, axis=0, keepdims=True)
                there = ((g + turns[t]) & (groups - 1)) * 2 + side
                y_rows[t, pl.ds(there, 1)] = heads[t, row] * (y + skip[...] * product)
                if t < 2:
                    s = s * live[t, row]
            final.append(s)
        end = (g + turns[2]) & (groups - 1)
        sent[end, 0 : 2 * MODES] = jnp.concatenate(final, axis=0).astype(BF16)

    gated[...] = y_rows[...].reshape(3 * rows, width).astype(BF16)
    far[...] = dot(gated[...], far_weight[...]).astype(BF16)


def products_kernel(place, gated, weight, part):
    part[0] = dot(gated[...], weight[...])


def products(gated, weight, aways):
    n = lax.axis_size("tensor")
    rows, width = gated.shape
    own_cols = weight.shape[1] // n
    places = (lax.axis_index("tensor") + jnp.array(aways, jnp.int32)) % n
    part = pl.pallas_call(
        products_kernel,
        grid_spec=pltpu.PrefetchScalarGridSpec(
            num_scalar_prefetch=1,
            grid=(len(aways),),
            in_specs=[
                whole((rows, width)),
                pl.BlockSpec((width, own_cols), lambda i, places: (0, places[i])),
            ],
            out_specs=pl.BlockSpec((1, rows, own_cols), lambda i, places: (i, 0, 0)),
        ),
        out_shape=jax.ShapeDtypeStruct((len(aways), rows, own_cols), F32),
        cost_estimate=pl.CostEstimate(
            flops=16 * rows * width * weight.shape[1], bytes_accessed=2 * weight.size, transcendentals=0
        ),
        compiler_params=pltpu.CompilerParams(vmem_limit_bytes=56 * 1024 * 1024),
        name="ring_products",
    )(places, gated, weight)
    return dict(zip(aways, part))


def finish_kernel(back, qkv, stay_state, finished, state, lagged):
    block = pl.program_id(0)
    rows, width = 16, qkv.shape[-1]

    def put(j, last):
        both = [qkv[1, j].astype(F32)[:, None], last[:, None]]
        lagged[:, j] = jnp.concatenate(both, axis=1).astype(BF16)

    @pl.when(block < 4)
    def _():
        n = back.shape[0]
        for b in range(n):
            for side in range(2):
                state[2 * b + side] = back[b, side * MODES : (side + 1) * MODES].astype(F32)
        shape = (3 * rows, n * 16)
        r = lax.broadcasted_iota(jnp.int32, shape, 0)
        c = lax.broadcasted_iota(jnp.int32, shape, 1)
        source = ((r & 15) >> 1) * 16 + (r >> 4) * 2 + (r & 1)
        order = jnp.where(c == source, 1.0, 0.0).astype(BF16)
        last = dot(order, back[:, 2 * MODES :].reshape(n * 16, width))
        for j in range(3):
            put(j, last[j * rows : (j + 1) * rows])

    @pl.when(block == 4)
    def _():
        state[...] = stay_state[...]
        at = lax.broadcasted_iota(jnp.int32, (rows, finished.shape[1]), 0) + block * rows
        own = at == lax.broadcasted_iota(jnp.int32, at.shape, 1)
        ended = jnp.where(own, finished[2:3].astype(F32), 0.0)
        alive = 1.0 - jnp.sum(ended, axis=1, keepdims=True)
        for j in range(3):
            put(j, qkv[0, j].astype(F32) * alive)


def whole(shape):
    return pl.BlockSpec(shape, lambda *_: (0,) * len(shape))


def swap(blocks):
    return lax.all_to_all(blocks, "dp", split_axis=0, concat_axis=0, tiled=True)


def ring_sums(far, gated, weight, block=None):
    n = lax.axis_size("tensor")
    half = far.shape[0] // 2

    def pass_on(right, left):
        right = lax.ppermute(right, "tensor", [(i, (i + 1) % n) for i in range(n)])
        left = lax.ppermute(left, "tensor", [(i, (i - 1) % n) for i in range(n)])
        return right, left

    right, left = pass_on(far[:half], far[half:])
    made = products(gated, weight, (3, -3, 2, -2))
    for away in range(n // 2 - 1, 0, -1):
        right, left, gated, block = lax.optimization_barrier((right, left, gated, block))
        ahead, behind = made[away], made[-away]
        if right.shape[0] == half:
            ahead = ahead.at[:half].add(right.astype(F32))
            behind = behind.at[half:].add(left.astype(F32))
        else:
            ahead, behind = ahead + right.astype(F32), behind + left.astype(F32)
        right, left = pass_on(ahead.astype(BF16), behind.astype(BF16))
        if away == 3:
            swapped = None if block is None else swap(block)
            block = None
        if away == 2:
            made |= products(gated, weight, (1, -1, 0))
    total = made[0] + right.astype(F32) + left.astype(F32)
    return lax.optimization_barrier((total, swapped))


def row_scales(own):
    n = lax.axis_size("tensor")
    squares = lax.psum(jnp.concatenate([jnp.sum(x * x, axis=1) for x in own]), "tensor")
    return lax.rsqrt(squares / (n * own[0].shape[1]) + 1e-05)[:, None]


def per_device(
    qkv,
    fir_buffer,
    fir_taps,
    modal_state,
    poles,
    residues,
    skip,
    out_weight,
    norm_gain,
    finished,
    dest_group,
):
    groups = lax.axis_size("dp")
    own_group = lax.axis_index("dp")
    slots, width = modal_state.shape[0], modal_state.shape[2]
    moving = groups * CAP
    qkv_kinds = jnp.transpose(qkv, (0, 2, 1, 3))
    skip_row = skip[None]
    shifts = lax.dynamic_slice_in_dim(dest_group, own_group * CAP, 1, 1)[:, 0] - own_group + groups
    turns = jnp.cumsum(shifts).astype(jnp.int32) % groups

    packed, gated_home, stay_state = pl.pallas_call(
        home_kernel,
        grid=(slots // 16,),
        in_specs=[
            pl.BlockSpec((4, 3, 16, width), lambda i: (0, 0, i, 0)),
            pl.BlockSpec((16, 3, 2, width), lambda i: (i, 0, 0, 0)),
            whole((3, 3, width)),
            pl.BlockSpec((16, MODES, width), lambda i: (i, 0, 0)),
            whole((MODES, width)),
            whole((MODES, width)),
            whole((1, width)),
            whole((3, slots)),
        ],
        out_specs=[
            pl.BlockSpec((8, 2 * MODES + 2 * KINDS, width), lambda i: (jnp.minimum(i, 3), 0, 0)),
            whole((slots + 48, width)),
            whole((16, MODES, width)),
        ],
        out_shape=[
            jax.ShapeDtypeStruct((groups, 2 * MODES + 2 * KINDS, width), BF16),
            jax.ShapeDtypeStruct((slots + 48, width), BF16),
            jax.ShapeDtypeStruct((16, MODES, width), F32),
        ],
        scratch_shapes=[pltpu.VMEM((16, width), F32)],
        compiler_params=pltpu.CompilerParams(vmem_limit_bytes=56 * 1024 * 1024),
        name="home_rows",
    )(qkv_kinds, fir_buffer, fir_taps, modal_state, poles, residues, skip_row, finished)

    n, own_cols = lax.axis_size("tensor"), norm_gain.shape[0]
    gated_home, later_weight = lax.optimization_barrier((gated_home, out_weight))
    far_place = (lax.axis_index("tensor") + n // 2) % n
    far_weight = lax.dynamic_slice_in_dim(later_weight, far_place * own_cols, own_cols, 1)
    got = swap(packed)
    own_home, _ = ring_sums(dot(gated_home, far_weight).astype(BF16), gated_home, out_weight)
    got, own_home = lax.optimization_barrier((got, own_home))

    sent, gated_band, far = pl.pallas_call(
        band_kernel,
        in_specs=[
            pl.BlockSpec(memory_space=pltpu.SMEM),
            pl.BlockSpec(memory_space=pl.ANY),
        ]
        + [pl.BlockSpec(memory_space=pltpu.VMEM)] * 5,
        out_specs=[pl.BlockSpec(memory_space=pltpu.VMEM)] * 3,
        out_shape=[
            jax.ShapeDtypeStruct((groups, 2 * MODES + 16, width), BF16),
            jax.ShapeDtypeStruct((3 * moving, width), BF16),
            jax.ShapeDtypeStruct((3 * moving, own_cols), BF16),
        ],
        scratch_shapes=[
            pltpu.VMEM((6, moving, width), F32),
            pltpu.VMEM((3, 3, moving, width), F32),
            pltpu.VMEM((2, moving, width), F32),
            pltpu.VMEM((3, moving, width), F32),
            pltpu.VMEM((3, moving, width), F32),
            pltpu.VMEM((3, moving, width), F32),
            pltpu.VMEM(got.shape, BF16),
            pltpu.SemaphoreType.DMA((2,)),
        ],
        compiler_params=pltpu.CompilerParams(vmem_limit_bytes=40 * 1024 * 1024),
        name="band_rows",
    )(turns, got, fir_taps, poles, residues, skip_row, far_weight)

    own_band, back = ring_sums(far, gated_band, out_weight, sent)
    scales = row_scales([own_band, own_home])
    mixed_band = (own_band * scales[: 3 * moving] * norm_gain[None]).astype(BF16)
    mixed_band = jnp.transpose(mixed_band.reshape(3, groups, CAP, own_cols), (1, 0, 2, 3))
    back, mixed_band = lax.optimization_barrier((back, mixed_band))
    mixed_back = swap(mixed_band)
    final_state, final_lagged = pl.pallas_call(
        finish_kernel,
        grid=(slots // 16,),
        in_specs=[
            pl.BlockSpec((8, 2 * MODES + 16, width), lambda i: (jnp.minimum(i, 3), 0, 0)),
            pl.BlockSpec((2, 3, 16, width), lambda i: (1, 0, i, 0)),
            whole((16, MODES, width)),
            whole((3, slots)),
        ],
        out_specs=[
            pl.BlockSpec((16, MODES, width), lambda i: (i, 0, 0)),
            pl.BlockSpec((16, 3, 2, width), lambda i: (i, 0, 0, 0)),
        ],
        out_shape=[
            jax.ShapeDtypeStruct(modal_state.shape, F32),
            jax.ShapeDtypeStruct(fir_buffer.shape, BF16),
        ],
        compiler_params=pltpu.CompilerParams(vmem_limit_bytes=56 * 1024 * 1024),
        name="last_rows",
    )(back, qkv_kinds, stay_state, finished)

    mixed_later = jnp.transpose(mixed_back, (1, 0, 2, 3)).reshape(3, moving, own_cols)
    mixed_home = (own_home * scales[3 * moving :] * norm_gain[None]).astype(BF16)
    mixed_stay = mixed_home[slots:].reshape(3, 16, own_cols)
    mixed = jnp.concatenate(
        [mixed_home[None, :slots], jnp.concatenate([mixed_later, mixed_stay], axis=1)], axis=0
    )
    return (mixed, final_state, final_lagged)


def solution(mesh):
    return jax.shard_map(
        per_device,
        mesh=mesh,
        in_specs=(
            P(None, "dp", None, "tensor"),
            P("dp", None, None, "tensor"),
            P(None, None, "tensor"),
            P("dp", None, "tensor"),
            P(None, "tensor"),
            P(None, "tensor"),
            P("tensor"),
            P("tensor", None),
            P("tensor"),
            P(None, "dp"),
            P(None, "dp"),
        ),
        out_specs=(P(None, "dp", "tensor"), P("dp", None, "tensor"), P("dp", None, None, "tensor")),
        check_vma=False,
    )
```

```python
import jax
import jax.numpy as jnp
from jax import lax
from jax.experimental import pallas as pl
from jax.experimental.pallas import tpu as pltpu
from jax.sharding import PartitionSpec as P

CAP = 2
MODES = 16
KINDS = 16
F32, BF16 = jnp.float32, jnp.bfloat16


def dot(a, b):
    return jnp.dot(a, b, preferred_element_type=F32)


def wide(x, width):
    return jnp.concatenate([x] * (width // x.shape[-1]), axis=-1)


def home_kernel(qkv_hbm, fir_hbm, state_hbm, taps, poles, residues, skip, finished, packed_hbm, *rest):
    gated, stay_state, qkv_all, fir_all, state_all, packed_all, y_rows, sems = rest
    rows, width = 16, qkv_hbm.shape[-1]
    blocks = qkv_hbm.shape[2] // rows

    def fetches(block):
        at = pl.ds(block * rows, rows)
        return [
            pltpu.make_async_copy(state_hbm.at[at], state_all.at[at], sems.at[0, block]),
            pltpu.make_async_copy(qkv_hbm.at[:, :, at], qkv_all.at[:, :, at], sems.at[1, block]),
            pltpu.make_async_copy(fir_hbm.at[at], fir_all.at[at], sems.at[2, block]),
        ]

    def store(block):
        at = pl.ds(block * (rows // 2), rows // 2)
        return pltpu.make_async_copy(packed_all.at[at], packed_hbm.at[at], sems.at[3, block])

    for block in range(blocks):
        for fetch in fetches(block):
            fetch.start()

    def first_step(block):
        for fetch in fetches(block):
            fetch.wait()
        start = pl.multiple_of(block * rows, rows)
        qkv = qkv_all.at[:, :, pl.ds(start, rows)]
        fir = fir_all.at[pl.ds(start, rows)]
        state = state_all.at[pl.ds(start, rows)]
        at = lax.broadcasted_iota(jnp.int32, (rows, finished.shape[1]), 0) + block * rows
        own = at == lax.broadcasted_iota(jnp.int32, at.shape, 1)
        alive = [
            jnp.broadcast_to(
                1.0 - jnp.sum(jnp.where(own, finished[t : t + 1].astype(F32), 0.0), axis=1, keepdims=True),
                (rows, width),
            )
            for t in range(3)
        ]
        alive0 = alive[0]
        q0 = [qkv[0, j].astype(F32) for j in range(3)]
        l0 = [fir[:, j].astype(F32)[:, 0] for j in range(3)]
        l1 = [fir[:, j].astype(F32)[:, 1] for j in range(3)]
        f = [
            taps[j, 0:1] * q0[j] + taps[j, 1:2] * l0[j] + taps[j, 2:3] * l1[j]
            for j in range(3)
        ]
        product = f[1] * f[2]
        modes = []
        for r in range(rows):
            s = poles[...] * state[r] + product[r : r + 1]
            y_rows[r : r + 1] = jnp.sum(residues[...] * s, axis=0, keepdims=True)
            modes.append(s * alive0[r : r + 1])
        gated[pl.ds(block * rows, rows)] = (f[0] * (y_rows[...] + skip[...] * product)).astype(BF16)
        return qkv, q0, l0, alive, modes

    @pl.loop(0, blocks - 1)
    def _(block):
        qkv, q0, l0, alive, modes = first_step(block)
        alive0 = alive[0]
        packed = packed_all.at[pl.ds(pl.multiple_of(block * (rows // 2), rows // 2), rows // 2)]
        for pair in range(rows // 2):
            both = jnp.concatenate([modes[2 * pair], modes[2 * pair + 1]], axis=0)
            packed[pair, 0 : 2 * MODES] = both.astype(BF16)
        sent = [(x * alive0).astype(BF16) for x in q0 + l0]
        sent += [qkv[t, j] for t in range(1, 4) for j in range(3)]
        half = width // 2
        sent.append(jnp.concatenate([alive[1][:, :half], alive[2][:, :half]], axis=-1).astype(BF16))
        stacked = jnp.concatenate(sent, axis=0)
        n = KINDS * rows
        r = lax.broadcasted_iota(jnp.int32, (n, n), 0)
        c = lax.broadcasted_iota(jnp.int32, (n, n), 1)
        source = ((r >> 1) & 15) * rows + (r >> 5) * 2 + (r & 1)
        order = jnp.where(c == source, 1.0, 0.0).astype(BF16)
        moved = dot(order, stacked).reshape(rows // 2, 2 * KINDS, width)
        packed[:, 2 * MODES :] = moved.astype(BF16)
        store(block).start()

    qkv, q0, l0, alive, modes = first_step(blocks - 1)
    alive0 = alive[0]
    for r in range(rows):
        stay_state[r] = modes[r]
    lag0, lag1 = [x * alive0 for x in q0], [x * alive0 for x in l0]
    for t in range(1, 4):
        q = [qkv[t, j].astype(F32) for j in range(3)]
        g = [
            taps[j, 0:1] * q[j] + taps[j, 1:2] * lag0[j] + taps[j, 2:3] * lag1[j]
            for j in range(3)
        ]
        prod = g[1] * g[2]
        live = alive[t] if t < 3 else None
        for r in range(rows):
            s = poles[...] * stay_state[r] + prod[r : r + 1]
            y_rows[r : r + 1] = jnp.sum(residues[...] * s, axis=0, keepdims=True)
            stay_state[r] = s * live[r : r + 1] if t < 3 else s
        gated[64 + t * rows : 80 + t * rows] = (
            g[0] * (y_rows[...] + skip[...] * prod)
        ).astype(BF16)
        if t < 3:
            lag0, lag1 = [x * live for x in q], [x * live for x in lag0]
    for block in range(blocks - 1):
        store(block).wait()


def band_kernel(
    turns, got_hbm, taps, poles, residues, skip, far_weight, ride, sent, gated, first, *scratch
):
    lags, inputs, live, heads, products, y_rows, got, sems = scratch
    groups, _, width = got.shape
    rows = 2 * groups
    halves = [pl.ds(2 * MODES, 2 * KINDS), pl.ds(0, 2 * MODES)]
    fetches = [
        pltpu.make_async_copy(got_hbm.at[:, at], got.at[:, at], sems.at[i])
        for i, at in enumerate(halves)
    ]
    for fetch in fetches:
        fetch.start()
    fetches[0].wait()
    kinds = got[:, 2 * MODES :].reshape(groups * 2 * KINDS, width)

    def taken(first, count, turn):
        shape = (count * rows, groups * 2 * KINDS)
        r = lax.broadcasted_iota(jnp.int32, shape, 0)
        c = lax.broadcasted_iota(jnp.int32, shape, 1)
        group = (((r & (rows - 1)) >> 1) + turn) & (groups - 1)
        source = group * (2 * KINDS) + (first + r // rows) * 2 + (r & 1)
        order = jnp.where(c == source, 1.0, 0.0).astype(BF16)
        return dot(order, kinds).reshape(count, rows, width)

    lags[...] = taken(0, 6, 0)
    for t in range(3):
        inputs[t] = taken(6 + 3 * t, 3, turns[t])
    half = width // 2
    live[0] = wide(taken(15, 1, turns[0])[0, :, :half], width)
    live[1] = wide(taken(15, 1, turns[1])[0, :, half:], width)

    @pl.loop(0, rows // 8)
    def _(i):
        at = pl.ds(pl.multiple_of(i * 8, 8), 8)
        lag0 = [lags[j, at] for j in range(3)]
        lag1 = [lags[3 + j, at] for j in range(3)]
        for t in range(3):
            q = [inputs[t, j, at] for j in range(3)]
            f = [
                taps[j, 0:1] * q[j] + taps[j, 1:2] * lag0[j] + taps[j, 2:3] * lag1[j]
                for j in range(3)
            ]
            heads[t, at] = f[0]
            products[t, at] = f[1] * f[2]
            if t < 2:
                on = live[t, at]
                lag0, lag1 = [x * on for x in q], [x * on for x in lag0]
                if t == 1:
                    for j in range(3):
                        lags[j, at] = lag0[j]

    shape = (groups * 16, 3 * rows)
    r = lax.broadcasted_iota(jnp.int32, shape, 0)
    c = lax.broadcasted_iota(jnp.int32, shape, 1)
    group = ((r >> 4) - turns[2] + groups) & (groups - 1)
    source = ((r & 15) >> 1) * rows + group * 2 + (r & 1)
    order = jnp.where((c == source) & ((r & 15) < 6), 1.0, 0.0).astype(BF16)
    last = lags[0:3].reshape(3 * rows, width).astype(BF16)
    sent[:, 2 * MODES :] = dot(order, last).reshape(groups, 16, width).astype(BF16)

    fetches[1].wait()

    @pl.loop(0, groups)
    def _(g):
        final = []
        for side in range(2):
            row = pl.ds(g * 2 + side, 1)
            s = got[g, side * MODES : (side + 1) * MODES].astype(F32)
            for t in range(3):
                product = products[t, row]
                s = poles[...] * s + product
                y = jnp.sum(residues[...] * s, axis=0, keepdims=True)
                there = ((g + turns[t]) & (groups - 1)) * 2 + side
                y_rows[t, pl.ds(there, 1)] = heads[t, row] * (y + skip[...] * product)
                if t < 2:
                    s = s * live[t, row]
            final.append(s)
        end = (g + turns[2]) & (groups - 1)
        sent[end, 0 : 2 * MODES] = jnp.concatenate(final, axis=0).astype(BF16)

    gated[...] = y_rows[...].reshape(3 * rows, width).astype(BF16)
    half = 3 * rows // 2
    for way in range(2):
        load = dot(gated[way * half : (way + 1) * half], far_weight[...])
        first[way, :half] = load.astype(BF16)
        first[way, half:] = ride[way]


def products_kernel(place, gated, weight, part):
    part[0] = dot(gated[...], weight[...])


def products(gated, weight, aways):
    n = lax.axis_size("tensor")
    rows, width = gated.shape
    own_cols = weight.shape[1] // n
    places = (lax.axis_index("tensor") + jnp.array(aways, jnp.int32)) % n
    part = pl.pallas_call(
        products_kernel,
        grid_spec=pltpu.PrefetchScalarGridSpec(
            num_scalar_prefetch=1,
            grid=(len(aways),),
            in_specs=[
                whole((rows, width)),
                pl.BlockSpec((width, own_cols), lambda i, places: (0, places[i])),
            ],
            out_specs=pl.BlockSpec((1, rows, own_cols), lambda i, places: (i, 0, 0)),
        ),
        out_shape=jax.ShapeDtypeStruct((len(aways), rows, own_cols), F32),
        cost_estimate=pl.CostEstimate(
            flops=16 * rows * width * weight.shape[1], bytes_accessed=2 * weight.size, transcendentals=0
        ),
        compiler_params=pltpu.CompilerParams(vmem_limit_bytes=56 * 1024 * 1024),
        name="ring_products",
    )(places, gated, weight)
    return dict(zip(aways, part))


def finish_kernel(back, qkv, stay_state, finished, state, lagged):
    block = pl.program_id(0)
    rows, width = 16, qkv.shape[-1]

    def put(j, last):
        both = [qkv[1, j].astype(F32)[:, None], last[:, None]]
        lagged[:, j] = jnp.concatenate(both, axis=1).astype(BF16)

    @pl.when(block < 4)
    def _():
        n = back.shape[0]
        for b in range(n):
            for side in range(2):
                state[2 * b + side] = back[b, side * MODES : (side + 1) * MODES].astype(F32)
        shape = (3 * rows, n * 16)
        r = lax.broadcasted_iota(jnp.int32, shape, 0)
        c = lax.broadcasted_iota(jnp.int32, shape, 1)
        source = ((r & 15) >> 1) * 16 + (r >> 4) * 2 + (r & 1)
        order = jnp.where(c == source, 1.0, 0.0).astype(BF16)
        last = dot(order, back[:, 2 * MODES :].reshape(n * 16, width))
        for j in range(3):
            put(j, last[j * rows : (j + 1) * rows])

    @pl.when(block == 4)
    def _():
        state[...] = stay_state[...]
        at = lax.broadcasted_iota(jnp.int32, (rows, finished.shape[1]), 0) + block * rows
        own = at == lax.broadcasted_iota(jnp.int32, at.shape, 1)
        ended = jnp.where(own, finished[2:3].astype(F32), 0.0)
        alive = 1.0 - jnp.sum(ended, axis=1, keepdims=True)
        for j in range(3):
            put(j, qkv[0, j].astype(F32) * alive)


def whole(shape):
    return pl.BlockSpec(shape, lambda *_: (0,) * len(shape))


def swap(blocks):
    return lax.all_to_all(blocks, "dp", split_axis=0, concat_axis=0, tiled=True)


def pass_on(right, left):
    n = lax.axis_size("tensor")
    right = lax.ppermute(right, "tensor", [(i, (i + 1) % n) for i in range(n)])
    left = lax.ppermute(left, "tensor", [(i, (i - 1) % n) for i in range(n)])
    return right, left


def joined(made, away, right, left):
    ahead, behind = made[away], made[-away]
    half = right.shape[0]
    if half < ahead.shape[0]:
        ahead = ahead.at[:half].add(right.astype(F32))
        behind = behind.at[half:].add(left.astype(F32))
    else:
        ahead, behind = ahead + right.astype(F32), behind + left.astype(F32)
    return ahead.astype(BF16), behind.astype(BF16)


def row_scales(own):
    n = lax.axis_size("tensor")
    squares = lax.psum(jnp.concatenate([jnp.sum(x * x, axis=1) for x in own]), "tensor")
    return lax.rsqrt(squares / (n * own[0].shape[1]) + 1e-05)[:, None]


def per_device(
    qkv,
    fir_buffer,
    fir_taps,
    modal_state,
    poles,
    residues,
    skip,
    out_weight,
    norm_gain,
    finished,
    dest_group,
):
    groups = lax.axis_size("dp")
    own_group = lax.axis_index("dp")
    slots, width = modal_state.shape[0], modal_state.shape[2]
    moving = groups * CAP
    qkv_kinds = jnp.transpose(qkv, (0, 2, 1, 3))
    skip_row = skip[None]
    shifts = lax.dynamic_slice_in_dim(dest_group, own_group * CAP, 1, 1)[:, 0] - own_group + groups
    turns = jnp.cumsum(shifts).astype(jnp.int32) % groups

    packed, gated_home, stay_state = pl.pallas_call(
        home_kernel,
        in_specs=[pl.BlockSpec(memory_space=pl.ANY)] * 3
        + [pl.BlockSpec(memory_space=pltpu.VMEM)] * 5,
        out_specs=[pl.BlockSpec(memory_space=pl.ANY)]
        + [pl.BlockSpec(memory_space=pltpu.VMEM)] * 2,
        out_shape=[
            jax.ShapeDtypeStruct((groups, 2 * MODES + 2 * KINDS, width), BF16),
            jax.ShapeDtypeStruct((slots + 48, width), BF16),
            jax.ShapeDtypeStruct((16, MODES, width), F32),
        ],
        scratch_shapes=[
            pltpu.VMEM(qkv_kinds.shape, BF16),
            pltpu.VMEM(fir_buffer.shape, BF16),
            pltpu.VMEM(modal_state.shape, F32),
            pltpu.VMEM((groups, 2 * MODES + 2 * KINDS, width), BF16),
            pltpu.VMEM((16, width), F32),
            pltpu.SemaphoreType.DMA((4, slots // 16)),
        ],
        compiler_params=pltpu.CompilerParams(vmem_limit_bytes=56 * 1024 * 1024),
        name="home_rows",
    )(qkv_kinds, fir_buffer, modal_state, fir_taps, poles, residues, skip_row, finished)

    n, own_cols = lax.axis_size("tensor"), norm_gain.shape[0]
    gated_home, later_weight = lax.optimization_barrier((gated_home, out_weight))
    far_place = (lax.axis_index("tensor") + n // 2) % n
    far_weight = lax.dynamic_slice_in_dim(later_weight, far_place * own_cols, own_cols, 1)
    got = swap(packed)
    far = dot(gated_home, far_weight).astype(BF16)
    half = far.shape[0] // 2
    right, left = pass_on(far[:half], far[half:])
    made = products(gated_home, out_weight, (3, -3, 2, -2))
    right, left = lax.optimization_barrier((right, left))
    right, left, gated_home = lax.optimization_barrier((*pass_on(*joined(made, 3, right, left)), gated_home))
    right, left = pass_on(*joined(made, 2, right, left))
    made = products(gated_home, out_weight, (1, -1, 0))
    right, left = lax.optimization_barrier((right, left))
    ride = jnp.stack(joined(made, 1, right, left))
    got, ride, own_home = lax.optimization_barrier((got, ride, made[0]))

    sent, gated_band, first = pl.pallas_call(
        band_kernel,
        in_specs=[
            pl.BlockSpec(memory_space=pltpu.SMEM),
            pl.BlockSpec(memory_space=pl.ANY),
        ]
        + [pl.BlockSpec(memory_space=pltpu.VMEM)] * 6,
        out_specs=[pl.BlockSpec(memory_space=pltpu.VMEM)] * 3,
        out_shape=[
            jax.ShapeDtypeStruct((groups, 2 * MODES + 16, width), BF16),
            jax.ShapeDtypeStruct((3 * moving, width), BF16),
            jax.ShapeDtypeStruct((2, 3 * moving // 2 + slots + 48, own_cols), BF16),
        ],
        scratch_shapes=[
            pltpu.VMEM((6, moving, width), F32),
            pltpu.VMEM((3, 3, moving, width), F32),
            pltpu.VMEM((2, moving, width), F32),
            pltpu.VMEM((3, moving, width), F32),
            pltpu.VMEM((3, moving, width), F32),
            pltpu.VMEM((3, moving, width), F32),
            pltpu.VMEM(got.shape, BF16),
            pltpu.SemaphoreType.DMA((2,)),
        ],
        compiler_params=pltpu.CompilerParams(vmem_limit_bytes=40 * 1024 * 1024),
        name="band_rows",
    )(turns, got, fir_taps, poles, residues, skip_row, far_weight, ride)

    half = 3 * moving // 2
    right, left = pass_on(first[0], first[1])
    made = products(gated_band, out_weight, (3, -3, 2, -2))
    right, left, gated_band, sent = lax.optimization_barrier((right, left, gated_band, sent))
    own_home = own_home + right[half:].astype(F32) + left[half:].astype(F32)
    right, left = pass_on(*joined(made, 3, right[:half], left[:half]))
    back = swap(sent)
    right, left, gated_band = lax.optimization_barrier((right, left, gated_band))
    right, left = pass_on(*joined(made, 2, right, left))
    made = products(gated_band, out_weight, (1, -1, 0))
    right, left = lax.optimization_barrier((right, left))
    right, left = pass_on(*joined(made, 1, right, left))
    right, left = lax.optimization_barrier((right, left))
    own_band = made[0] + right.astype(F32) + left.astype(F32)
    own_band, back = lax.optimization_barrier((own_band, back))
    scales = row_scales([own_band, own_home])
    mixed_band = (own_band * scales[: 3 * moving] * norm_gain[None]).astype(BF16)
    mixed_band = jnp.transpose(mixed_band.reshape(3, groups, CAP, own_cols), (1, 0, 2, 3))
    back, mixed_band = lax.optimization_barrier((back, mixed_band))
    mixed_back = swap(mixed_band)
    final_state, final_lagged = pl.pallas_call(
        finish_kernel,
        grid=(slots // 16,),
        in_specs=[
            pl.BlockSpec((8, 2 * MODES + 16, width), lambda i: (jnp.minimum(i, 3), 0, 0)),
            pl.BlockSpec((2, 3, 16, width), lambda i: (1, 0, i, 0)),
            whole((16, MODES, width)),
            whole((3, slots)),
        ],
        out_specs=[
            pl.BlockSpec((16, MODES, width), lambda i: (i, 0, 0)),
            pl.BlockSpec((16, 3, 2, width), lambda i: (i, 0, 0, 0)),
        ],
        out_shape=[
            jax.ShapeDtypeStruct(modal_state.shape, F32),
            jax.ShapeDtypeStruct(fir_buffer.shape, BF16),
        ],
        compiler_params=pltpu.CompilerParams(vmem_limit_bytes=56 * 1024 * 1024),
        name="last_rows",
    )(back, qkv_kinds, stay_state, finished)

    mixed_later = jnp.transpose(mixed_back, (1, 0, 2, 3)).reshape(3, moving, own_cols)
    mixed_home = (own_home * scales[3 * moving :] * norm_gain[None]).astype(BF16)
    mixed_stay = mixed_home[slots:].reshape(3, 16, own_cols)
    mixed = jnp.concatenate(
        [mixed_home[None, :slots], jnp.concatenate([mixed_later, mixed_stay], axis=1)], axis=0
    )
    return (mixed, final_state, final_lagged)


def solution(mesh):
    return jax.shard_map(
        per_device,
        mesh=mesh,
        in_specs=(
            P(None, "dp", None, "tensor"),
            P("dp", None, None, "tensor"),
            P(None, None, "tensor"),
            P("dp", None, "tensor"),
            P(None, "tensor"),
            P(None, "tensor"),
            P("tensor"),
            P("tensor", None),
            P("tensor"),
            P(None, "dp"),
            P(None, "dp"),
        ),
        out_specs=(P(None, "dp", "tensor"), P("dp", None, "tensor"), P("dp", None, None, "tensor")),
        check_vma=False,
    )
```

```python
import jax
import jax.numpy as jnp
from jax import lax
from jax.experimental import pallas as pl
from jax.experimental.pallas import tpu as pltpu
from jax.sharding import PartitionSpec as P

CAP = 2
MODES = 16
KINDS = 16
F32, BF16 = jnp.float32, jnp.bfloat16


def dot(a, b):
    return jnp.dot(a, b, preferred_element_type=F32)


def wide(x, width):
    return jnp.concatenate([x] * (width // x.shape[-1]), axis=-1)


def home_kernel(qkv_hbm, fir_hbm, state_hbm, taps, poles, residues, skip, finished, packed_hbm, *rest):
    gated, stay_state, qkv_all, fir_all, state_all, packed_all, y_rows, sems = rest
    rows, width = 16, qkv_hbm.shape[-1]
    blocks = qkv_hbm.shape[2] // rows

    def fetches(block):
        at = pl.ds(block * rows, rows)
        return [
            pltpu.make_async_copy(state_hbm.at[at], state_all.at[at], sems.at[0, block]),
            pltpu.make_async_copy(qkv_hbm.at[:, :, at], qkv_all.at[:, :, at], sems.at[1, block]),
            pltpu.make_async_copy(fir_hbm.at[at], fir_all.at[at], sems.at[2, block]),
        ]

    def store(block):
        at = pl.ds(block * (rows // 2), rows // 2)
        return pltpu.make_async_copy(packed_all.at[at], packed_hbm.at[at], sems.at[3, block])

    for block in range(blocks):
        for fetch in fetches(block):
            fetch.start()

    def first_step(block):
        for fetch in fetches(block):
            fetch.wait()
        start = pl.multiple_of(block * rows, rows)
        qkv = qkv_all.at[:, :, pl.ds(start, rows)]
        fir = fir_all.at[pl.ds(start, rows)]
        state = state_all.at[pl.ds(start, rows)]
        at = lax.broadcasted_iota(jnp.int32, (rows, finished.shape[1]), 0) + block * rows
        own = at == lax.broadcasted_iota(jnp.int32, at.shape, 1)
        alive = [
            jnp.broadcast_to(
                1.0 - jnp.sum(jnp.where(own, finished[t : t + 1].astype(F32), 0.0), axis=1, keepdims=True),
                (rows, width),
            )
            for t in range(3)
        ]
        alive0 = alive[0]
        q0 = [qkv[0, j].astype(F32) for j in range(3)]
        l0 = [fir[:, j].astype(F32)[:, 0] for j in range(3)]
        l1 = [fir[:, j].astype(F32)[:, 1] for j in range(3)]
        f = [
            taps[j, 0:1] * q0[j] + taps[j, 1:2] * l0[j] + taps[j, 2:3] * l1[j]
            for j in range(3)
        ]
        product = f[1] * f[2]
        modes = []
        for r in range(rows):
            s = poles[...] * state[r] + product[r : r + 1]
            y_rows[r : r + 1] = jnp.sum(residues[...] * s, axis=0, keepdims=True)
            modes.append(s * alive0[r : r + 1])
        gated[pl.ds(block * rows, rows)] = (f[0] * (y_rows[...] + skip[...] * product)).astype(BF16)
        return qkv, q0, l0, alive, modes

    @pl.loop(0, blocks - 1)
    def _(block):
        qkv, q0, l0, alive, modes = first_step(block)
        alive0 = alive[0]
        packed = packed_all.at[pl.ds(pl.multiple_of(block * (rows // 2), rows // 2), rows // 2)]
        for pair in range(rows // 2):
            both = jnp.concatenate([modes[2 * pair], modes[2 * pair + 1]], axis=0)
            packed[pair, 0 : 2 * MODES] = both.astype(BF16)
        sent = [(x * alive0).astype(BF16) for x in q0 + l0]
        sent += [qkv[t, j] for t in range(1, 4) for j in range(3)]
        half = width // 2
        sent.append(jnp.concatenate([alive[1][:, :half], alive[2][:, :half]], axis=-1).astype(BF16))
        stacked = jnp.concatenate(sent, axis=0)
        n = KINDS * rows
        r = lax.broadcasted_iota(jnp.int32, (n, n), 0)
        c = lax.broadcasted_iota(jnp.int32, (n, n), 1)
        source = ((r >> 1) & 15) * rows + (r >> 5) * 2 + (r & 1)
        order = jnp.where(c == source, 1.0, 0.0).astype(BF16)
        moved = dot(order, stacked).reshape(rows // 2, 2 * KINDS, width)
        packed[:, 2 * MODES :] = moved.astype(BF16)
        store(block).start()

    qkv, q0, l0, alive, modes = first_step(blocks - 1)
    alive0 = alive[0]
    for r in range(rows):
        stay_state[r] = modes[r]
    lag0, lag1 = [x * alive0 for x in q0], [x * alive0 for x in l0]
    for t in range(1, 4):
        q = [qkv[t, j].astype(F32) for j in range(3)]
        g = [
            taps[j, 0:1] * q[j] + taps[j, 1:2] * lag0[j] + taps[j, 2:3] * lag1[j]
            for j in range(3)
        ]
        prod = g[1] * g[2]
        live = alive[t] if t < 3 else None
        for r in range(rows):
            s = poles[...] * stay_state[r] + prod[r : r + 1]
            y_rows[r : r + 1] = jnp.sum(residues[...] * s, axis=0, keepdims=True)
            stay_state[r] = s * live[r : r + 1] if t < 3 else s
        gated[64 + t * rows : 80 + t * rows] = (
            g[0] * (y_rows[...] + skip[...] * prod)
        ).astype(BF16)
        if t < 3:
            lag0, lag1 = [x * live for x in q], [x * live for x in lag0]
    for block in range(blocks - 1):
        store(block).wait()


def band_kernel(
    turns, got_hbm, taps, poles, residues, skip, far_weight, ride, sent, gated, first_right, first_left, *scratch
):
    lags, inputs, live, heads, products, y_rows, got, sems = scratch
    groups, _, width = got.shape
    rows = 2 * groups
    halves = [pl.ds(2 * MODES, 2 * KINDS), pl.ds(0, 2 * MODES)]
    fetches = [
        pltpu.make_async_copy(got_hbm.at[:, at], got.at[:, at], sems.at[i])
        for i, at in enumerate(halves)
    ]
    for fetch in fetches:
        fetch.start()
    fetches[0].wait()
    kinds = got[:, 2 * MODES :].reshape(groups * 2 * KINDS, width)

    def taken(first, count, turn):
        shape = (count * rows, groups * 2 * KINDS)
        r = lax.broadcasted_iota(jnp.int32, shape, 0)
        c = lax.broadcasted_iota(jnp.int32, shape, 1)
        group = (((r & (rows - 1)) >> 1) + turn) & (groups - 1)
        source = group * (2 * KINDS) + (first + r // rows) * 2 + (r & 1)
        order = jnp.where(c == source, 1.0, 0.0).astype(BF16)
        return dot(order, kinds).reshape(count, rows, width)

    lags[...] = taken(0, 6, 0)
    for t in range(3):
        inputs[t] = taken(6 + 3 * t, 3, turns[t])
    half = width // 2
    live[0] = wide(taken(15, 1, turns[0])[0, :, :half], width)
    live[1] = wide(taken(15, 1, turns[1])[0, :, half:], width)

    @pl.loop(0, rows // 8)
    def _(i):
        at = pl.ds(pl.multiple_of(i * 8, 8), 8)
        lag0 = [lags[j, at] for j in range(3)]
        lag1 = [lags[3 + j, at] for j in range(3)]
        for t in range(3):
            q = [inputs[t, j, at] for j in range(3)]
            f = [
                taps[j, 0:1] * q[j] + taps[j, 1:2] * lag0[j] + taps[j, 2:3] * lag1[j]
                for j in range(3)
            ]
            heads[t, at] = f[0]
            products[t, at] = f[1] * f[2]
            if t < 2:
                on = live[t, at]
                lag0, lag1 = [x * on for x in q], [x * on for x in lag0]
                if t == 1:
                    for j in range(3):
                        lags[j, at] = lag0[j]

    shape = (groups * 16, 3 * rows)
    r = lax.broadcasted_iota(jnp.int32, shape, 0)
    c = lax.broadcasted_iota(jnp.int32, shape, 1)
    group = ((r >> 4) - turns[2] + groups) & (groups - 1)
    source = ((r & 15) >> 1) * rows + group * 2 + (r & 1)
    order = jnp.where((c == source) & ((r & 15) < 6), 1.0, 0.0).astype(BF16)
    last = lags[0:3].reshape(3 * rows, width).astype(BF16)
    sent[:, 2 * MODES :] = dot(order, last).reshape(groups, 16, width).astype(BF16)

    fetches[1].wait()

    @pl.loop(0, groups)
    def _(g):
        final = []
        for side in range(2):
            row = pl.ds(g * 2 + side, 1)
            s = got[g, side * MODES : (side + 1) * MODES].astype(F32)
            for t in range(3):
                product = products[t, row]
                s = poles[...] * s + product
                y = jnp.sum(residues[...] * s, axis=0, keepdims=True)
                there = ((g + turns[t]) & (groups - 1)) * 2 + side
                y_rows[t, pl.ds(there, 1)] = heads[t, row] * (y + skip[...] * product)
                if t < 2:
                    s = s * live[t, row]
            final.append(s)
        end = (g + turns[2]) & (groups - 1)
        sent[end, 0 : 2 * MODES] = jnp.concatenate(final, axis=0).astype(BF16)

    gated[...] = y_rows[...].reshape(3 * rows, width).astype(BF16)
    half = 3 * rows // 2
    for way, first in enumerate((first_right, first_left)):
        load = dot(gated[way * half : (way + 1) * half], far_weight[...])
        first[:half] = load.astype(BF16)
        first[half:] = ride[way]


def products_kernel(place, gated, weight, part):
    part[0] = dot(gated[...], weight[...])


def products(place, gated, weight, aways):
    n = lax.axis_size("tensor")
    rows, width = gated.shape
    own_cols = weight.shape[1] // n
    assert aways == tuple((aways[0] - i // 2) * (1 - 2 * (i % 2)) for i in range(len(aways)))

    def column(i, place):
        return 0, (place[0] + n + (aways[0] - i // 2) * (1 - 2 * (i % 2))) % n

    part = pl.pallas_call(
        products_kernel,
        grid_spec=pltpu.PrefetchScalarGridSpec(
            num_scalar_prefetch=1,
            grid=(len(aways),),
            in_specs=[
                whole((rows, width)),
                pl.BlockSpec((width, own_cols), column),
            ],
            out_specs=pl.BlockSpec((1, rows, own_cols), lambda i, place: (i, 0, 0)),
        ),
        out_shape=jax.ShapeDtypeStruct((len(aways), rows, own_cols), F32),
        cost_estimate=pl.CostEstimate(
            flops=16 * rows * width * weight.shape[1], bytes_accessed=2 * weight.size, transcendentals=0
        ),
        compiler_params=pltpu.CompilerParams(vmem_limit_bytes=56 * 1024 * 1024),
        name="ring_products",
    )(place, gated, weight)
    return dict(zip(aways, part))


def finish_kernel(back, qkv, stay_state, finished, state, lagged):
    block = pl.program_id(0)
    rows, width = 16, qkv.shape[-1]

    def put(j, last):
        both = [qkv[1, j].astype(F32)[:, None], last[:, None]]
        lagged[:, j] = jnp.concatenate(both, axis=1).astype(BF16)

    @pl.when(block < 4)
    def _():
        n = back.shape[0]
        for b in range(n):
            for side in range(2):
                state[2 * b + side] = back[b, side * MODES : (side + 1) * MODES].astype(F32)
        shape = (3 * rows, n * 16)
        r = lax.broadcasted_iota(jnp.int32, shape, 0)
        c = lax.broadcasted_iota(jnp.int32, shape, 1)
        source = ((r & 15) >> 1) * 16 + (r >> 4) * 2 + (r & 1)
        order = jnp.where(c == source, 1.0, 0.0).astype(BF16)
        last = dot(order, back[:, 2 * MODES :].reshape(n * 16, width))
        for j in range(3):
            put(j, last[j * rows : (j + 1) * rows])

    @pl.when(block == 4)
    def _():
        state[...] = stay_state[...]
        at = lax.broadcasted_iota(jnp.int32, (rows, finished.shape[1]), 0) + block * rows
        own = at == lax.broadcasted_iota(jnp.int32, at.shape, 1)
        ended = jnp.where(own, finished[2:3].astype(F32), 0.0)
        alive = 1.0 - jnp.sum(ended, axis=1, keepdims=True)
        for j in range(3):
            put(j, qkv[0, j].astype(F32) * alive)


def whole(shape):
    return pl.BlockSpec(shape, lambda *_: (0,) * len(shape))


def swap(blocks):
    return lax.all_to_all(blocks, "dp", split_axis=0, concat_axis=0, tiled=True)


def pass_on(right, left):
    n = lax.axis_size("tensor")
    right = lax.ppermute(right, "tensor", [(i, (i + 1) % n) for i in range(n)])
    left = lax.ppermute(left, "tensor", [(i, (i - 1) % n) for i in range(n)])
    return right, left


def joined(made, away, right, left):
    ahead, behind = made[away], made[-away]
    half = right.shape[0]
    if half < ahead.shape[0]:
        ahead = ahead.at[:half].add(right.astype(F32))
        behind = behind.at[half:].add(left.astype(F32))
    else:
        ahead, behind = ahead + right.astype(F32), behind + left.astype(F32)
    return ahead.astype(BF16), behind.astype(BF16)


def row_scales(own):
    n = lax.axis_size("tensor")
    squares = jnp.concatenate([jnp.sum(x * x, axis=1) for x in own])

    def sent_on(x, away):
        return lax.ppermute(x, "tensor", [(i, (i + away) % n) for i in range(n)])

    near = [sent_on(squares, away) for away in (1, -1, 2)]
    squares = squares + near[0] + near[1] + near[2]
    squares = squares + sent_on(squares, 4)
    return lax.rsqrt(squares / (n * own[0].shape[1]) + 1e-05)[:, None]


def per_device(
    qkv,
    fir_buffer,
    fir_taps,
    modal_state,
    poles,
    residues,
    skip,
    out_weight,
    norm_gain,
    finished,
    dest_group,
):
    groups = lax.axis_size("dp")
    own_group = lax.axis_index("dp")
    slots, width = modal_state.shape[0], modal_state.shape[2]
    moving = groups * CAP
    qkv_kinds = jnp.transpose(qkv, (0, 2, 1, 3))
    skip_row = skip[None]
    shifts = lax.dynamic_slice_in_dim(dest_group, own_group * CAP, 1, 1)[:, 0] - own_group + groups
    turns = jnp.cumsum(shifts).astype(jnp.int32) % groups

    packed, gated_home, stay_state = pl.pallas_call(
        home_kernel,
        in_specs=[pl.BlockSpec(memory_space=pl.ANY)] * 3
        + [pl.BlockSpec(memory_space=pltpu.VMEM)] * 5,
        out_specs=[pl.BlockSpec(memory_space=pl.ANY)]
        + [pl.BlockSpec(memory_space=pltpu.VMEM)] * 2,
        out_shape=[
            jax.ShapeDtypeStruct((groups, 2 * MODES + 2 * KINDS, width), BF16),
            jax.ShapeDtypeStruct((slots + 48, width), BF16),
            jax.ShapeDtypeStruct((16, MODES, width), F32),
        ],
        scratch_shapes=[
            pltpu.VMEM(qkv_kinds.shape, BF16),
            pltpu.VMEM(fir_buffer.shape, BF16),
            pltpu.VMEM(modal_state.shape, F32),
            pltpu.VMEM((groups, 2 * MODES + 2 * KINDS, width), BF16),
            pltpu.VMEM((16, width), F32),
            pltpu.SemaphoreType.DMA((4, slots // 16)),
        ],
        compiler_params=pltpu.CompilerParams(vmem_limit_bytes=56 * 1024 * 1024),
        name="home_rows",
    )(qkv_kinds, fir_buffer, modal_state, fir_taps, poles, residues, skip_row, finished)

    n, own_cols = lax.axis_size("tensor"), norm_gain.shape[0]
    gated_home, later_weight = lax.optimization_barrier((gated_home, out_weight))
    place = lax.axis_index("tensor").astype(jnp.int32)[None]
    far_place = (place[0] + n // 2) % n
    far_weight = lax.dynamic_slice_in_dim(later_weight, far_place * own_cols, own_cols, 1)
    got = swap(packed)
    far = dot(gated_home, far_weight).astype(BF16)
    half = far.shape[0] // 2
    right, left = pass_on(far[:half], far[half:])
    made = products(place, gated_home, out_weight, (3, -3, 2, -2))
    right, left = lax.optimization_barrier((right, left))
    right, left, gated_home = lax.optimization_barrier((*pass_on(*joined(made, 3, right, left)), gated_home))
    right, left = pass_on(*joined(made, 2, right, left))
    made = products(place, gated_home, out_weight, (1, -1, 0))
    right, left = lax.optimization_barrier((right, left))
    ride = jnp.stack(joined(made, 1, right, left))
    got, ride, own_home = lax.optimization_barrier((got, ride, made[0]))

    sent, gated_band, right, left = pl.pallas_call(
        band_kernel,
        in_specs=[
            pl.BlockSpec(memory_space=pltpu.SMEM),
            pl.BlockSpec(memory_space=pl.ANY),
        ]
        + [pl.BlockSpec(memory_space=pltpu.VMEM)] * 6,
        out_specs=[pl.BlockSpec(memory_space=pltpu.VMEM)] * 4,
        out_shape=[
            jax.ShapeDtypeStruct((groups, 2 * MODES + 16, width), BF16),
            jax.ShapeDtypeStruct((3 * moving, width), BF16),
            jax.ShapeDtypeStruct((3 * moving // 2 + slots + 48, own_cols), BF16),
            jax.ShapeDtypeStruct((3 * moving // 2 + slots + 48, own_cols), BF16),
        ],
        scratch_shapes=[
            pltpu.VMEM((6, moving, width), F32),
            pltpu.VMEM((3, 3, moving, width), F32),
            pltpu.VMEM((2, moving, width), F32),
            pltpu.VMEM((3, moving, width), F32),
            pltpu.VMEM((3, moving, width), F32),
            pltpu.VMEM((3, moving, width), F32),
            pltpu.VMEM(got.shape, BF16),
            pltpu.SemaphoreType.DMA((2,)),
        ],
        compiler_params=pltpu.CompilerParams(vmem_limit_bytes=40 * 1024 * 1024),
        name="band_rows",
    )(turns, got, fir_taps, poles, residues, skip_row, far_weight, ride)

    half = 3 * moving // 2
    right, left = pass_on(right, left)
    made = products(place, gated_band, out_weight, (3, -3, 2, -2))
    right, left, gated_band, sent = lax.optimization_barrier((right, left, gated_band, sent))
    own_home = own_home + right[half:].astype(F32) + left[half:].astype(F32)
    right, left = pass_on(*joined(made, 3, right[:half], left[:half]))
    back = swap(sent)
    right, left, gated_band = lax.optimization_barrier((right, left, gated_band))
    right, left = pass_on(*joined(made, 2, right, left))
    made = products(place, gated_band, out_weight, (1, -1, 0))
    right, left = lax.optimization_barrier((right, left))
    right, left = pass_on(*joined(made, 1, right, left))
    right, left = lax.optimization_barrier((right, left))
    own_band = made[0] + right.astype(F32) + left.astype(F32)
    own_band, back = lax.optimization_barrier((own_band, back))
    scales = row_scales([own_band, own_home])
    mixed_band = (own_band * scales[: 3 * moving] * norm_gain[None]).astype(BF16)
    mixed_band = jnp.transpose(mixed_band.reshape(3, groups, CAP, own_cols), (1, 0, 2, 3))
    back, mixed_band = lax.optimization_barrier((back, mixed_band))
    mixed_back = swap(mixed_band)
    final_state, final_lagged = pl.pallas_call(
        finish_kernel,
        grid=(slots // 16,),
        in_specs=[
            pl.BlockSpec((8, 2 * MODES + 16, width), lambda i: (jnp.minimum(i, 3), 0, 0)),
            pl.BlockSpec((2, 3, 16, width), lambda i: (1, 0, i, 0)),
            whole((16, MODES, width)),
            whole((3, slots)),
        ],
        out_specs=[
            pl.BlockSpec((16, MODES, width), lambda i: (i, 0, 0)),
            pl.BlockSpec((16, 3, 2, width), lambda i: (i, 0, 0, 0)),
        ],
        out_shape=[
            jax.ShapeDtypeStruct(modal_state.shape, F32),
            jax.ShapeDtypeStruct(fir_buffer.shape, BF16),
        ],
        compiler_params=pltpu.CompilerParams(vmem_limit_bytes=56 * 1024 * 1024),
        name="last_rows",
    )(back, qkv_kinds, stay_state, finished)

    mixed_later = jnp.transpose(mixed_back, (1, 0, 2, 3)).reshape(3, moving, own_cols)
    mixed_home = (own_home * scales[3 * moving :] * norm_gain[None]).astype(BF16)
    mixed_stay = mixed_home[slots:].reshape(3, 16, own_cols)
    mixed = jnp.concatenate(
        [mixed_home[None, :slots], jnp.concatenate([mixed_later, mixed_stay], axis=1)], axis=0
    )
    return (mixed, final_state, final_lagged)


def solution(mesh):
    return jax.shard_map(
        per_device,
        mesh=mesh,
        in_specs=(
            P(None, "dp", None, "tensor"),
            P("dp", None, None, "tensor"),
            P(None, None, "tensor"),
            P("dp", None, "tensor"),
            P(None, "tensor"),
            P(None, "tensor"),
            P("tensor"),
            P("tensor", None),
            P("tensor"),
            P(None, "dp"),
            P(None, "dp"),
        ),
        out_specs=(P(None, "dp", "tensor"), P("dp", None, "tensor"), P("dp", None, None, "tensor")),
        check_vma=False,
    )
```

```python
import jax
import jax.numpy as jnp
from jax import lax
from jax.experimental import pallas as pl
from jax.experimental.pallas import tpu as pltpu
from jax.sharding import PartitionSpec as P

CAP = 2
MODES = 16
KINDS = 16
F32, BF16 = jnp.float32, jnp.bfloat16


def dot(a, b):
    return jnp.dot(a, b, preferred_element_type=F32)


def wide(x, width):
    return jnp.concatenate([x] * (width // x.shape[-1]), axis=-1)


def home_kernel(qkv_hbm, fir_hbm, state_hbm, taps, poles, residues, skip, finished, packed_hbm, *rest):
    gated, stay_state, qkv_all, fir_all, state_all, packed_all, y_rows, sems = rest
    rows, width = 16, qkv_hbm.shape[-1]
    blocks = qkv_hbm.shape[2] // rows

    def fetches(block):
        at = pl.ds(block * rows, rows)
        return [
            pltpu.make_async_copy(state_hbm.at[at], state_all.at[at], sems.at[0, block]),
            pltpu.make_async_copy(qkv_hbm.at[:, :, at], qkv_all.at[:, :, at], sems.at[1, block]),
            pltpu.make_async_copy(fir_hbm.at[at], fir_all.at[at], sems.at[2, block]),
        ]

    def store(block):
        at = pl.ds(block * (rows // 2), rows // 2)
        return pltpu.make_async_copy(packed_all.at[at], packed_hbm.at[at], sems.at[3, block])

    for block in range(blocks):
        for fetch in fetches(block):
            fetch.start()

    def first_step(block):
        for fetch in fetches(block):
            fetch.wait()
        start = pl.multiple_of(block * rows, rows)
        qkv = qkv_all.at[:, :, pl.ds(start, rows)]
        fir = fir_all.at[pl.ds(start, rows)]
        state = state_all.at[pl.ds(start, rows)]
        at = lax.broadcasted_iota(jnp.int32, (rows, finished.shape[1]), 0) + block * rows
        own = at == lax.broadcasted_iota(jnp.int32, at.shape, 1)
        alive = [
            jnp.broadcast_to(
                1.0 - jnp.sum(jnp.where(own, finished[t : t + 1].astype(F32), 0.0), axis=1, keepdims=True),
                (rows, width),
            )
            for t in range(3)
        ]
        alive0 = alive[0]
        q0 = [qkv[0, j].astype(F32) for j in range(3)]
        l0 = [fir[:, j].astype(F32)[:, 0] for j in range(3)]
        l1 = [fir[:, j].astype(F32)[:, 1] for j in range(3)]
        f = [
            taps[j, 0:1] * q0[j] + taps[j, 1:2] * l0[j] + taps[j, 2:3] * l1[j]
            for j in range(3)
        ]
        product = f[1] * f[2]
        modes = []
        for r in range(rows):
            s = poles[...] * state[r] + product[r : r + 1]
            y_rows[r : r + 1] = jnp.sum(residues[...] * s, axis=0, keepdims=True)
            modes.append(s * alive0[r : r + 1])
        gated[pl.ds(block * rows, rows)] = (f[0] * (y_rows[...] + skip[...] * product)).astype(BF16)
        return qkv, q0, l0, alive, modes

    @pl.loop(0, blocks - 1)
    def _(block):
        qkv, q0, l0, alive, modes = first_step(block)
        alive0 = alive[0]
        packed = packed_all.at[pl.ds(pl.multiple_of(block * (rows // 2), rows // 2), rows // 2)]
        for pair in range(rows // 2):
            both = jnp.concatenate([modes[2 * pair], modes[2 * pair + 1]], axis=0)
            packed[pair, 0 : 2 * MODES] = both.astype(BF16)
        sent = [(x * alive0).astype(BF16) for x in q0 + l0]
        sent += [qkv[t, j] for t in range(1, 4) for j in range(3)]
        half = width // 2
        sent.append(jnp.concatenate([alive[1][:, :half], alive[2][:, :half]], axis=-1).astype(BF16))
        stacked = jnp.concatenate(sent, axis=0)
        n = KINDS * rows
        r = lax.broadcasted_iota(jnp.int32, (n, n), 0)
        c = lax.broadcasted_iota(jnp.int32, (n, n), 1)
        source = ((r >> 1) & 15) * rows + (r >> 5) * 2 + (r & 1)
        order = jnp.where(c == source, 1.0, 0.0).astype(BF16)
        moved = dot(order, stacked).reshape(rows // 2, 2 * KINDS, width)
        packed[:, 2 * MODES :] = moved.astype(BF16)
        store(block).start()

    qkv, q0, l0, alive, modes = first_step(blocks - 1)
    alive0 = alive[0]
    for r in range(rows):
        stay_state[r] = modes[r]
    lag0, lag1 = [x * alive0 for x in q0], [x * alive0 for x in l0]
    for t in range(1, 4):
        q = [qkv[t, j].astype(F32) for j in range(3)]
        g = [
            taps[j, 0:1] * q[j] + taps[j, 1:2] * lag0[j] + taps[j, 2:3] * lag1[j]
            for j in range(3)
        ]
        prod = g[1] * g[2]
        live = alive[t] if t < 3 else None
        for r in range(rows):
            s = poles[...] * stay_state[r] + prod[r : r + 1]
            y_rows[r : r + 1] = jnp.sum(residues[...] * s, axis=0, keepdims=True)
            stay_state[r] = s * live[r : r + 1] if t < 3 else s
        gated[64 + t * rows : 80 + t * rows] = (
            g[0] * (y_rows[...] + skip[...] * prod)
        ).astype(BF16)
        if t < 3:
            lag0, lag1 = [x * live for x in q], [x * live for x in lag0]
    for block in range(blocks - 1):
        store(block).wait()


def band_kernel(
    turns, got_hbm, taps, poles, residues, skip, far_weight, ride, sent, gated, first_right, first_left, *scratch
):
    lags, inputs, live, heads, products, y_rows, got, sems = scratch
    groups, _, width = got.shape
    rows = 2 * groups
    halves = [pl.ds(2 * MODES, 2 * KINDS), pl.ds(0, 2 * MODES)]
    fetches = [
        pltpu.make_async_copy(got_hbm.at[:, at], got.at[:, at], sems.at[i])
        for i, at in enumerate(halves)
    ]
    for fetch in fetches:
        fetch.start()
    fetches[0].wait()
    kinds = got[:, 2 * MODES :].reshape(groups * 2 * KINDS, width)

    def taken(first, count, turn):
        shape = (count * rows, groups * 2 * KINDS)
        r = lax.broadcasted_iota(jnp.int32, shape, 0)
        c = lax.broadcasted_iota(jnp.int32, shape, 1)
        group = (((r & (rows - 1)) >> 1) + turn) & (groups - 1)
        source = group * (2 * KINDS) + (first + r // rows) * 2 + (r & 1)
        order = jnp.where(c == source, 1.0, 0.0).astype(BF16)
        return dot(order, kinds).reshape(count, rows, width)

    lags[...] = taken(0, 6, 0)
    for t in range(3):
        inputs[t] = taken(6 + 3 * t, 3, turns[t])
    half = width // 2
    live[0] = wide(taken(15, 1, turns[0])[0, :, :half], width)
    live[1] = wide(taken(15, 1, turns[1])[0, :, half:], width)

    @pl.loop(0, rows // 8)
    def _(i):
        at = pl.ds(pl.multiple_of(i * 8, 8), 8)
        lag0 = [lags[j, at] for j in range(3)]
        lag1 = [lags[3 + j, at] for j in range(3)]
        for t in range(3):
            q = [inputs[t, j, at] for j in range(3)]
            f = [
                taps[j, 0:1] * q[j] + taps[j, 1:2] * lag0[j] + taps[j, 2:3] * lag1[j]
                for j in range(3)
            ]
            heads[t, at] = f[0]
            products[t, at] = f[1] * f[2]
            if t < 2:
                on = live[t, at]
                lag0, lag1 = [x * on for x in q], [x * on for x in lag0]
                if t == 1:
                    for j in range(3):
                        lags[j, at] = lag0[j]

    shape = (groups * 16, 3 * rows)
    r = lax.broadcasted_iota(jnp.int32, shape, 0)
    c = lax.broadcasted_iota(jnp.int32, shape, 1)
    group = ((r >> 4) - turns[2] + groups) & (groups - 1)
    source = ((r & 15) >> 1) * rows + group * 2 + (r & 1)
    order = jnp.where((c == source) & ((r & 15) < 6), 1.0, 0.0).astype(BF16)
    last = lags[0:3].reshape(3 * rows, width).astype(BF16)
    sent[:, 2 * MODES :] = dot(order, last).reshape(groups, 16, width).astype(BF16)

    fetches[1].wait()

    @pl.loop(0, groups)
    def _(g):
        final = []
        for side in range(2):
            row = pl.ds(g * 2 + side, 1)
            s = got[g, side * MODES : (side + 1) * MODES].astype(F32)
            for t in range(3):
                product = products[t, row]
                s = poles[...] * s + product
                y = jnp.sum(residues[...] * s, axis=0, keepdims=True)
                there = ((g + turns[t]) & (groups - 1)) * 2 + side
                y_rows[t, pl.ds(there, 1)] = heads[t, row] * (y + skip[...] * product)
                if t < 2:
                    s = s * live[t, row]
            final.append(s)
        end = (g + turns[2]) & (groups - 1)
        sent[end, 0 : 2 * MODES] = jnp.concatenate(final, axis=0).astype(BF16)

    gated[...] = y_rows[...].reshape(3 * rows, width).astype(BF16)
    half = 3 * rows // 2
    for way, first in enumerate((first_right, first_left)):
        load = dot(gated[way * half : (way + 1) * half], far_weight[...])
        first[:half] = load.astype(BF16)
        first[half:] = ride[way]


def products_kernel(place, gated, weight, part):
    part[0] = dot(gated[...], weight[...])


def products(place, gated, weight, aways):
    n = lax.axis_size("tensor")
    rows, width = gated.shape
    own_cols = weight.shape[1] // n
    assert aways == tuple((aways[0] - i // 2) * (1 - 2 * (i % 2)) for i in range(len(aways)))

    def column(i, place):
        return 0, (place[0] + n + (aways[0] - i // 2) * (1 - 2 * (i % 2))) % n

    part = pl.pallas_call(
        products_kernel,
        grid_spec=pltpu.PrefetchScalarGridSpec(
            num_scalar_prefetch=1,
            grid=(len(aways),),
            in_specs=[
                whole((rows, width)),
                pl.BlockSpec((width, own_cols), column),
            ],
            out_specs=pl.BlockSpec((1, rows, own_cols), lambda i, place: (i, 0, 0)),
        ),
        out_shape=jax.ShapeDtypeStruct((len(aways), rows, own_cols), F32),
        cost_estimate=pl.CostEstimate(
            flops=16 * rows * width * weight.shape[1], bytes_accessed=2 * weight.size, transcendentals=0
        ),
        compiler_params=pltpu.CompilerParams(vmem_limit_bytes=52 * 1024 * 1024),
        name="ring_products",
    )(place, gated, weight)
    return dict(zip(aways, part))


def finish_kernel(back, qkv, stay_state, finished, state, lagged):
    block = pl.program_id(0)
    rows, width = 16, qkv.shape[-1]

    def put(j, last):
        both = [qkv[1, j].astype(F32)[:, None], last[:, None]]
        lagged[:, j] = jnp.concatenate(both, axis=1).astype(BF16)

    @pl.when(block < 4)
    def _():
        n = back.shape[0]
        for b in range(n):
            for side in range(2):
                state[2 * b + side] = back[b, side * MODES : (side + 1) * MODES].astype(F32)
        shape = (3 * rows, n * 16)
        r = lax.broadcasted_iota(jnp.int32, shape, 0)
        c = lax.broadcasted_iota(jnp.int32, shape, 1)
        source = ((r & 15) >> 1) * 16 + (r >> 4) * 2 + (r & 1)
        order = jnp.where(c == source, 1.0, 0.0).astype(BF16)
        last = dot(order, back[:, 2 * MODES :].reshape(n * 16, width))
        for j in range(3):
            put(j, last[j * rows : (j + 1) * rows])

    @pl.when(block == 4)
    def _():
        state[...] = stay_state[...]
        at = lax.broadcasted_iota(jnp.int32, (rows, finished.shape[1]), 0) + block * rows
        own = at == lax.broadcasted_iota(jnp.int32, at.shape, 1)
        ended = jnp.where(own, finished[2:3].astype(F32), 0.0)
        alive = 1.0 - jnp.sum(ended, axis=1, keepdims=True)
        for j in range(3):
            put(j, qkv[0, j].astype(F32) * alive)


def whole(shape):
    return pl.BlockSpec(shape, lambda *_: (0,) * len(shape))


def swap(blocks):
    return lax.all_to_all(blocks, "dp", split_axis=0, concat_axis=0, tiled=True)


def pass_on(right, left):
    n = lax.axis_size("tensor")
    right = lax.ppermute(right, "tensor", [(i, (i + 1) % n) for i in range(n)])
    left = lax.ppermute(left, "tensor", [(i, (i - 1) % n) for i in range(n)])
    return right, left


def joined(made, away, right, left):
    ahead, behind = made[away], made[-away]
    half = right.shape[0]
    if half < ahead.shape[0]:
        ahead = ahead.at[:half].add(right.astype(F32))
        behind = behind.at[half:].add(left.astype(F32))
    else:
        ahead, behind = ahead + right.astype(F32), behind + left.astype(F32)
    return ahead.astype(BF16), behind.astype(BF16)


def row_scales(own):
    n = lax.axis_size("tensor")
    squares = jnp.concatenate([jnp.sum(x * x, axis=1) for x in own])

    def sent_on(x, away):
        return lax.ppermute(x, "tensor", [(i, (i + away) % n) for i in range(n)])

    four = squares + (sent_on(squares, 1) + sent_on(squares, -1)) + sent_on(squares, 2)
    squares = sent_on(four, 2) + sent_on(four, -2)
    return lax.rsqrt(squares / (n * own[0].shape[1]) + 1e-05)[:, None]


def per_device(
    qkv,
    fir_buffer,
    fir_taps,
    modal_state,
    poles,
    residues,
    skip,
    out_weight,
    norm_gain,
    finished,
    dest_group,
):
    groups = lax.axis_size("dp")
    own_group = lax.axis_index("dp")
    slots, width = modal_state.shape[0], modal_state.shape[2]
    moving = groups * CAP
    qkv_kinds = jnp.transpose(qkv, (0, 2, 1, 3))
    skip_row = skip[None]
    shifts = lax.dynamic_slice_in_dim(dest_group, own_group * CAP, 1, 1)[:, 0] - own_group + groups
    turns = jnp.cumsum(shifts).astype(jnp.int32) % groups

    packed, gated_home, stay_state = pl.pallas_call(
        home_kernel,
        in_specs=[pl.BlockSpec(memory_space=pl.ANY)] * 3
        + [pl.BlockSpec(memory_space=pltpu.VMEM)] * 5,
        out_specs=[pl.BlockSpec(memory_space=pl.ANY)]
        + [pl.BlockSpec(memory_space=pltpu.VMEM)] * 2,
        out_shape=[
            jax.ShapeDtypeStruct((groups, 2 * MODES + 2 * KINDS, width), BF16),
            jax.ShapeDtypeStruct((slots + 48, width), BF16),
            jax.ShapeDtypeStruct((16, MODES, width), F32),
        ],
        scratch_shapes=[
            pltpu.VMEM(qkv_kinds.shape, BF16),
            pltpu.VMEM(fir_buffer.shape, BF16),
            pltpu.VMEM(modal_state.shape, F32),
            pltpu.VMEM((groups, 2 * MODES + 2 * KINDS, width), BF16),
            pltpu.VMEM((16, width), F32),
            pltpu.SemaphoreType.DMA((4, slots // 16)),
        ],
        compiler_params=pltpu.CompilerParams(vmem_limit_bytes=56 * 1024 * 1024),
        name="home_rows",
    )(qkv_kinds, fir_buffer, modal_state, fir_taps, poles, residues, skip_row, finished)

    n, own_cols = lax.axis_size("tensor"), norm_gain.shape[0]
    gated_home, later_weight = lax.optimization_barrier((gated_home, out_weight))
    place = lax.axis_index("tensor").astype(jnp.int32)[None]
    far_place = (place[0] + n // 2) % n
    far_weight = lax.dynamic_slice_in_dim(later_weight, far_place * own_cols, own_cols, 1)
    got = swap(packed)
    far = dot(gated_home, far_weight).astype(BF16)
    half = far.shape[0] // 2
    right, left = pass_on(far[:half], far[half:])
    made = products(place, gated_home, out_weight, (3, -3, 2, -2))
    right, left = lax.optimization_barrier((right, left))
    right, left, gated_home = lax.optimization_barrier((*pass_on(*joined(made, 3, right, left)), gated_home))
    right, left = pass_on(*joined(made, 2, right, left))
    made = products(place, gated_home, out_weight, (1, -1, 0))
    right, left = lax.optimization_barrier((right, left))
    ride = jnp.stack(joined(made, 1, right, left))
    got, ride, own_home = lax.optimization_barrier((got, ride, made[0]))

    sent, gated_band, right, left = pl.pallas_call(
        band_kernel,
        in_specs=[
            pl.BlockSpec(memory_space=pltpu.SMEM),
            pl.BlockSpec(memory_space=pl.ANY),
        ]
        + [pl.BlockSpec(memory_space=pltpu.VMEM)] * 6,
        out_specs=[pl.BlockSpec(memory_space=pltpu.VMEM)] * 4,
        out_shape=[
            jax.ShapeDtypeStruct((groups, 2 * MODES + 16, width), BF16),
            jax.ShapeDtypeStruct((3 * moving, width), BF16),
            jax.ShapeDtypeStruct((3 * moving // 2 + slots + 48, own_cols), BF16),
            jax.ShapeDtypeStruct((3 * moving // 2 + slots + 48, own_cols), BF16),
        ],
        scratch_shapes=[
            pltpu.VMEM((6, moving, width), F32),
            pltpu.VMEM((3, 3, moving, width), F32),
            pltpu.VMEM((2, moving, width), F32),
            pltpu.VMEM((3, moving, width), F32),
            pltpu.VMEM((3, moving, width), F32),
            pltpu.VMEM((3, moving, width), F32),
            pltpu.VMEM(got.shape, BF16),
            pltpu.SemaphoreType.DMA((2,)),
        ],
        compiler_params=pltpu.CompilerParams(vmem_limit_bytes=40 * 1024 * 1024),
        name="band_rows",
    )(turns, got, fir_taps, poles, residues, skip_row, far_weight, ride)

    half = 3 * moving // 2
    right, left = pass_on(right, left)
    made = products(place, gated_band, out_weight, (3, -3, 2, -2))
    right, left, gated_band, sent = lax.optimization_barrier((right, left, gated_band, sent))
    own_home = own_home + right[half:].astype(F32) + left[half:].astype(F32)
    right, left = pass_on(*joined(made, 3, right[:half], left[:half]))
    back = swap(sent)
    right, left, gated_band = lax.optimization_barrier((right, left, gated_band))
    right, left = pass_on(*joined(made, 2, right, left))
    made = products(place, gated_band, out_weight, (1, -1, 0))
    right, left = lax.optimization_barrier((right, left))
    right, left = pass_on(*joined(made, 1, right, left))
    right, left = lax.optimization_barrier((right, left))
    own_band = made[0] + right.astype(F32) + left.astype(F32)
    own_band, back = lax.optimization_barrier((own_band, back))
    scales = row_scales([own_band, own_home])
    mixed_band = (own_band * scales[: 3 * moving] * norm_gain[None]).astype(BF16)
    mixed_band = jnp.transpose(mixed_band.reshape(3, groups, CAP, own_cols), (1, 0, 2, 3))
    back, mixed_band = lax.optimization_barrier((back, mixed_band))
    mixed_back = swap(mixed_band)
    final_state, final_lagged = pl.pallas_call(
        finish_kernel,
        grid=(slots // 16,),
        in_specs=[
            pl.BlockSpec((8, 2 * MODES + 16, width), lambda i: (jnp.minimum(i, 3), 0, 0)),
            pl.BlockSpec((2, 3, 16, width), lambda i: (1, 0, i, 0)),
            whole((16, MODES, width)),
            whole((3, slots)),
        ],
        out_specs=[
            pl.BlockSpec((16, MODES, width), lambda i: (i, 0, 0)),
            pl.BlockSpec((16, 3, 2, width), lambda i: (i, 0, 0, 0)),
        ],
        out_shape=[
            jax.ShapeDtypeStruct(modal_state.shape, F32),
            jax.ShapeDtypeStruct(fir_buffer.shape, BF16),
        ],
        compiler_params=pltpu.CompilerParams(vmem_limit_bytes=56 * 1024 * 1024),
        name="last_rows",
    )(back, qkv_kinds, stay_state, finished)

    mixed_later = jnp.transpose(mixed_back, (1, 0, 2, 3)).reshape(3, moving, own_cols)
    mixed_home = (own_home * scales[3 * moving :] * norm_gain[None]).astype(BF16)
    mixed_stay = mixed_home[slots:].reshape(3, 16, own_cols)
    mixed = jnp.concatenate(
        [mixed_home[None, :slots], jnp.concatenate([mixed_later, mixed_stay], axis=1)], axis=0
    )
    return (mixed, final_state, final_lagged)


def solution(mesh):
    return jax.shard_map(
        per_device,
        mesh=mesh,
        in_specs=(
            P(None, "dp", None, "tensor"),
            P("dp", None, None, "tensor"),
            P(None, None, "tensor"),
            P("dp", None, "tensor"),
            P(None, "tensor"),
            P(None, "tensor"),
            P("tensor"),
            P("tensor", None),
            P("tensor"),
            P(None, "dp"),
            P(None, "dp"),
        ),
        out_specs=(P(None, "dp", "tensor"), P("dp", None, "tensor"), P("dp", None, None, "tensor")),
        check_vma=False,
    )
```

```python
import jax
import jax.numpy as jnp
from jax import lax
from jax.experimental import pallas as pl
from jax.experimental.pallas import tpu as pltpu
from jax.sharding import PartitionSpec as P

CAP = 2
MODES = 16
KINDS = 16
F32, BF16 = jnp.float32, jnp.bfloat16


def dot(a, b):
    return jnp.dot(a, b, preferred_element_type=F32)


def wide(x, width):
    return jnp.concatenate([x] * (width // x.shape[-1]), axis=-1)


def home_kernel(qkv_hbm, fir_hbm, state_hbm, taps, poles, residues, skip, finished, packed_hbm, *rest):
    gated, stay_state, qkv_all, fir_all, state_all, packed_all, y_rows, sems = rest
    rows, width = 16, qkv_hbm.shape[-1]
    blocks = qkv_hbm.shape[2] // rows

    def fetches(block):
        at = pl.ds(block * rows, rows)
        return [
            pltpu.make_async_copy(state_hbm.at[at], state_all.at[at], sems.at[0, block]),
            pltpu.make_async_copy(qkv_hbm.at[:, :, at], qkv_all.at[:, :, at], sems.at[1, block]),
            pltpu.make_async_copy(fir_hbm.at[at], fir_all.at[at], sems.at[2, block]),
        ]

    def store(block):
        at = pl.ds(block * (rows // 2), rows // 2)
        return pltpu.make_async_copy(packed_all.at[at], packed_hbm.at[at], sems.at[3, block])

    for block in range(blocks):
        for fetch in fetches(block):
            fetch.start()

    def first_step(block):
        for fetch in fetches(block):
            fetch.wait()
        start = pl.multiple_of(block * rows, rows)
        qkv = qkv_all.at[:, :, pl.ds(start, rows)]
        fir = fir_all.at[pl.ds(start, rows)]
        state = state_all.at[pl.ds(start, rows)]
        at = lax.broadcasted_iota(jnp.int32, (rows, finished.shape[1]), 0) + block * rows
        own = at == lax.broadcasted_iota(jnp.int32, at.shape, 1)
        alive = [
            jnp.broadcast_to(
                1.0 - jnp.sum(jnp.where(own, finished[t : t + 1].astype(F32), 0.0), axis=1, keepdims=True),
                (rows, width),
            )
            for t in range(3)
        ]
        alive0 = alive[0]
        q0 = [qkv[0, j].astype(F32) for j in range(3)]
        l0 = [fir[:, j].astype(F32)[:, 0] for j in range(3)]
        l1 = [fir[:, j].astype(F32)[:, 1] for j in range(3)]
        f = [
            taps[j, 0:1] * q0[j] + taps[j, 1:2] * l0[j] + taps[j, 2:3] * l1[j]
            for j in range(3)
        ]
        product = f[1] * f[2]
        modes = []
        for r in range(rows):
            s = poles[...] * state[r] + product[r : r + 1]
            y_rows[r : r + 1] = jnp.sum(residues[...] * s, axis=0, keepdims=True)
            modes.append(s * alive0[r : r + 1])
        gated[pl.ds(block * rows, rows)] = (f[0] * (y_rows[...] + skip[...] * product)).astype(BF16)
        return qkv, q0, l0, alive, modes

    @pl.loop(0, blocks - 1)
    def _(block):
        qkv, q0, l0, alive, modes = first_step(block)
        alive0 = alive[0]
        packed = packed_all.at[pl.ds(pl.multiple_of(block * (rows // 2), rows // 2), rows // 2)]
        for pair in range(rows // 2):
            both = jnp.concatenate([modes[2 * pair], modes[2 * pair + 1]], axis=0)
            packed[pair, 0 : 2 * MODES] = both.astype(BF16)
        sent = [(x * alive0).astype(BF16) for x in q0 + l0]
        sent += [qkv[t, j] for t in range(1, 4) for j in range(3)]
        half = width // 2
        sent.append(jnp.concatenate([alive[1][:, :half], alive[2][:, :half]], axis=-1).astype(BF16))
        stacked = jnp.concatenate(sent, axis=0)
        n = KINDS * rows
        r = lax.broadcasted_iota(jnp.int32, (n, n), 0)
        c = lax.broadcasted_iota(jnp.int32, (n, n), 1)
        source = ((r >> 1) & 15) * rows + (r >> 5) * 2 + (r & 1)
        order = jnp.where(c == source, 1.0, 0.0).astype(BF16)
        moved = dot(order, stacked).reshape(rows // 2, 2 * KINDS, width)
        packed[:, 2 * MODES :] = moved.astype(BF16)
        store(block).start()

    qkv, q0, l0, alive, modes = first_step(blocks - 1)
    alive0 = alive[0]
    for r in range(rows):
        stay_state[r] = modes[r]
    lag0, lag1 = [x * alive0 for x in q0], [x * alive0 for x in l0]
    for t in range(1, 4):
        q = [qkv[t, j].astype(F32) for j in range(3)]
        g = [
            taps[j, 0:1] * q[j] + taps[j, 1:2] * lag0[j] + taps[j, 2:3] * lag1[j]
            for j in range(3)
        ]
        prod = g[1] * g[2]
        live = alive[t] if t < 3 else None
        for r in range(rows):
            s = poles[...] * stay_state[r] + prod[r : r + 1]
            y_rows[r : r + 1] = jnp.sum(residues[...] * s, axis=0, keepdims=True)
            stay_state[r] = s * live[r : r + 1] if t < 3 else s
        gated[64 + t * rows : 80 + t * rows] = (
            g[0] * (y_rows[...] + skip[...] * prod)
        ).astype(BF16)
        if t < 3:
            lag0, lag1 = [x * live for x in q], [x * live for x in lag0]
    for block in range(blocks - 1):
        store(block).wait()


def band_kernel(
    turns, got, taps, poles, residues, skip, far_weight, ride, sent, gated, first_right, first_left, *scratch
):
    lags, inputs, live, heads, products, y_rows, kinds = scratch
    groups, _, width = got.shape
    rows = 2 * groups

    n = 16 * KINDS
    r = lax.broadcasted_iota(jnp.int32, (n, n), 0)
    c = lax.broadcasted_iota(jnp.int32, (n, n), 1)
    source = ((r >> 1) & 7) * (2 * KINDS) + (r >> 4) * 2 + (r & 1)
    order = jnp.where(c == source, 1.0, 0.0).astype(BF16)
    for g in range(0, groups, 8):
        part = dot(order, got[g : g + 8, 2 * MODES :].reshape(n, width)).reshape(KINDS, 16, width)
        lags[:, 2 * g : 2 * g + 16] = part[:6]
        kinds[:, 2 * g : 2 * g + 16] = part[6:].astype(BF16)

    r = lax.broadcasted_iota(jnp.int32, (rows, rows), 0)
    c = lax.broadcasted_iota(jnp.int32, (rows, rows), 1)
    half = width // 2
    for t in range(3):
        turn = jnp.where(c == ((r + 2 * turns[t]) & (rows - 1)), 1.0, 0.0).astype(BF16)
        for j in range(3):
            inputs[t, j] = dot(turn, kinds[3 * t + j])
        if t < 2:
            live[t] = wide(dot(turn, kinds[9, :, t * half : (t + 1) * half]), width)

    @pl.loop(0, rows // 8)
    def _(i):
        at = pl.ds(pl.multiple_of(i * 8, 8), 8)
        lag0 = [lags[j, at] for j in range(3)]
        lag1 = [lags[3 + j, at] for j in range(3)]
        for t in range(3):
            q = [inputs[t, j, at] for j in range(3)]
            f = [
                taps[j, 0:1] * q[j] + taps[j, 1:2] * lag0[j] + taps[j, 2:3] * lag1[j]
                for j in range(3)
            ]
            heads[t, at] = f[0]
            products[t, at] = f[1] * f[2]
            if t < 2:
                on = live[t, at]
                lag0, lag1 = [x * on for x in q], [x * on for x in lag0]
                if t == 1:
                    for j in range(3):
                        lags[j, at] = lag0[j]

    shape = (groups * 16, 3 * rows)
    r = lax.broadcasted_iota(jnp.int32, shape, 0)
    c = lax.broadcasted_iota(jnp.int32, shape, 1)
    group = ((r >> 4) - turns[2] + groups) & (groups - 1)
    source = ((r & 15) >> 1) * rows + group * 2 + (r & 1)
    order = jnp.where((c == source) & ((r & 15) < 6), 1.0, 0.0).astype(BF16)
    last = lags[0:3].reshape(3 * rows, width).astype(BF16)
    sent[:, 2 * MODES :] = dot(order, last).reshape(groups, 16, width).astype(BF16)

    @pl.loop(0, groups)
    def _(g):
        final = []
        for side in range(2):
            row = pl.ds(g * 2 + side, 1)
            s = got[g, side * MODES : (side + 1) * MODES].astype(F32)
            for t in range(3):
                product = products[t, row]
                s = poles[...] * s + product
                y = jnp.sum(residues[...] * s, axis=0, keepdims=True)
                there = ((g + turns[t]) & (groups - 1)) * 2 + side
                y_rows[t, pl.ds(there, 1)] = heads[t, row] * (y + skip[...] * product)
                if t < 2:
                    s = s * live[t, row]
            final.append(s)
        end = (g + turns[2]) & (groups - 1)
        sent[end, 0 : 2 * MODES] = jnp.concatenate(final, axis=0).astype(BF16)

    gated[...] = y_rows[...].reshape(3 * rows, width).astype(BF16)
    half = 3 * rows // 2
    for way, first in enumerate((first_right, first_left)):
        load = dot(gated[way * half : (way + 1) * half], far_weight[...])
        first[:half] = load.astype(BF16)
        first[half:] = ride[way]


def products_kernel(place, gated, weight, part):
    part[0] = dot(gated[...], weight[...])


def products(place, gated, weight, aways):
    n = lax.axis_size("tensor")
    rows, width = gated.shape
    own_cols = weight.shape[1] // n
    assert aways == tuple((aways[0] - i // 2) * (1 - 2 * (i % 2)) for i in range(len(aways)))

    def column(i, place):
        return 0, (place[0] + n + (aways[0] - i // 2) * (1 - 2 * (i % 2))) % n

    part = pl.pallas_call(
        products_kernel,
        grid_spec=pltpu.PrefetchScalarGridSpec(
            num_scalar_prefetch=1,
            grid=(len(aways),),
            in_specs=[
                whole((rows, width)),
                pl.BlockSpec((width, own_cols), column),
            ],
            out_specs=pl.BlockSpec((1, rows, own_cols), lambda i, place: (i, 0, 0)),
        ),
        out_shape=jax.ShapeDtypeStruct((len(aways), rows, own_cols), F32),
        cost_estimate=pl.CostEstimate(
            flops=16 * rows * width * weight.shape[1], bytes_accessed=2 * weight.size, transcendentals=0
        ),
        compiler_params=pltpu.CompilerParams(vmem_limit_bytes=52 * 1024 * 1024),
        name="ring_products",
    )(place, gated, weight)
    return dict(zip(aways, part))


def finish_kernel(back, qkv, stay_state, finished, state, lagged):
    block = pl.program_id(0)
    rows, width = 16, qkv.shape[-1]

    def put(j, last):
        both = [qkv[1, j].astype(F32)[:, None], last[:, None]]
        lagged[:, j] = jnp.concatenate(both, axis=1).astype(BF16)

    @pl.when(block < 4)
    def _():
        n = back.shape[0]
        for b in range(n):
            for side in range(2):
                state[2 * b + side] = back[b, side * MODES : (side + 1) * MODES].astype(F32)
        shape = (3 * rows, n * 16)
        r = lax.broadcasted_iota(jnp.int32, shape, 0)
        c = lax.broadcasted_iota(jnp.int32, shape, 1)
        source = ((r & 15) >> 1) * 16 + (r >> 4) * 2 + (r & 1)
        order = jnp.where(c == source, 1.0, 0.0).astype(BF16)
        last = dot(order, back[:, 2 * MODES :].reshape(n * 16, width))
        for j in range(3):
            put(j, last[j * rows : (j + 1) * rows])

    @pl.when(block == 4)
    def _():
        state[...] = stay_state[...]
        at = lax.broadcasted_iota(jnp.int32, (rows, finished.shape[1]), 0) + block * rows
        own = at == lax.broadcasted_iota(jnp.int32, at.shape, 1)
        ended = jnp.where(own, finished[2:3].astype(F32), 0.0)
        alive = 1.0 - jnp.sum(ended, axis=1, keepdims=True)
        for j in range(3):
            put(j, qkv[0, j].astype(F32) * alive)


def whole(shape):
    return pl.BlockSpec(shape, lambda *_: (0,) * len(shape))


def swap(blocks):
    return lax.all_to_all(blocks, "dp", split_axis=0, concat_axis=0, tiled=True)


def pass_on(right, left):
    n = lax.axis_size("tensor")
    right = lax.ppermute(right, "tensor", [(i, (i + 1) % n) for i in range(n)])
    left = lax.ppermute(left, "tensor", [(i, (i - 1) % n) for i in range(n)])
    return right, left


def joined(made, away, right, left):
    ahead, behind = made[away], made[-away]
    half = right.shape[0]
    if half < ahead.shape[0]:
        ahead = ahead.at[:half].add(right.astype(F32))
        behind = behind.at[half:].add(left.astype(F32))
    else:
        ahead, behind = ahead + right.astype(F32), behind + left.astype(F32)
    return ahead.astype(BF16), behind.astype(BF16)


def row_scales(own, back):
    n = lax.axis_size("tensor")
    squares = jnp.concatenate([jnp.sum(x * x, axis=1) for x in own])

    def sent_on(x, away):
        return lax.ppermute(x, "tensor", [(i, (i + away) % n) for i in range(n)])

    below = squares + sent_on(squares, 1)
    three = below + sent_on(squares, -1)
    three, below, back = lax.optimization_barrier((three, below, back))
    squares = three + (sent_on(three, 3) + sent_on(below, -3))
    return lax.rsqrt(squares / (n * own[0].shape[1]) + 1e-05)[:, None], back


def per_device(
    qkv,
    fir_buffer,
    fir_taps,
    modal_state,
    poles,
    residues,
    skip,
    out_weight,
    norm_gain,
    finished,
    dest_group,
):
    groups = lax.axis_size("dp")
    own_group = lax.axis_index("dp")
    slots, width = modal_state.shape[0], modal_state.shape[2]
    moving = groups * CAP
    qkv_kinds = jnp.transpose(qkv, (0, 2, 1, 3))
    skip_row = skip[None]
    shifts = lax.dynamic_slice_in_dim(dest_group, own_group * CAP, 1, 1)[:, 0] - own_group + groups
    turns = jnp.cumsum(shifts).astype(jnp.int32) % groups

    packed, gated_home, stay_state = pl.pallas_call(
        home_kernel,
        in_specs=[pl.BlockSpec(memory_space=pl.ANY)] * 3
        + [pl.BlockSpec(memory_space=pltpu.VMEM)] * 5,
        out_specs=[pl.BlockSpec(memory_space=pl.ANY)]
        + [pl.BlockSpec(memory_space=pltpu.VMEM)] * 2,
        out_shape=[
            jax.ShapeDtypeStruct((groups, 2 * MODES + 2 * KINDS, width), BF16),
            jax.ShapeDtypeStruct((slots + 48, width), BF16),
            jax.ShapeDtypeStruct((16, MODES, width), F32),
        ],
        scratch_shapes=[
            pltpu.VMEM(qkv_kinds.shape, BF16),
            pltpu.VMEM(fir_buffer.shape, BF16),
            pltpu.VMEM(modal_state.shape, F32),
            pltpu.VMEM((groups, 2 * MODES + 2 * KINDS, width), BF16),
            pltpu.VMEM((16, width), F32),
            pltpu.SemaphoreType.DMA((4, slots // 16)),
        ],
        compiler_params=pltpu.CompilerParams(vmem_limit_bytes=56 * 1024 * 1024),
        name="home_rows",
    )(qkv_kinds, fir_buffer, modal_state, fir_taps, poles, residues, skip_row, finished)

    n, own_cols = lax.axis_size("tensor"), norm_gain.shape[0]
    gated_home, later_weight = lax.optimization_barrier((gated_home, out_weight))
    place = lax.axis_index("tensor").astype(jnp.int32)[None]
    far_place = (place[0] + n // 2) % n
    far_weight = lax.dynamic_slice_in_dim(later_weight, far_place * own_cols, own_cols, 1)
    got = swap(packed)
    far = dot(gated_home, far_weight).astype(BF16)
    half = far.shape[0] // 2
    right, left = pass_on(far[:half], far[half:])
    made = products(place, gated_home, out_weight, (3, -3, 2, -2))
    right, left = lax.optimization_barrier((right, left))
    right, left, gated_home = lax.optimization_barrier((*pass_on(*joined(made, 3, right, left)), gated_home))
    right, left = pass_on(*joined(made, 2, right, left))
    made = products(place, gated_home, out_weight, (1, -1, 0))
    right, left = lax.optimization_barrier((right, left))
    ride = jnp.stack(joined(made, 1, right, left))
    got, ride, own_home = lax.optimization_barrier((got, ride, made[0]))

    sent, gated_band, right, left = pl.pallas_call(
        band_kernel,
        in_specs=[
            pl.BlockSpec(memory_space=pltpu.SMEM),
        ]
        + [pl.BlockSpec(memory_space=pltpu.VMEM)] * 7,
        out_specs=[pl.BlockSpec(memory_space=pltpu.VMEM)] * 4,
        out_shape=[
            jax.ShapeDtypeStruct((groups, 2 * MODES + 16, width), BF16),
            jax.ShapeDtypeStruct((3 * moving, width), BF16),
            jax.ShapeDtypeStruct((3 * moving // 2 + slots + 48, own_cols), BF16),
            jax.ShapeDtypeStruct((3 * moving // 2 + slots + 48, own_cols), BF16),
        ],
        scratch_shapes=[
            pltpu.VMEM((6, moving, width), F32),
            pltpu.VMEM((3, 3, moving, width), F32),
            pltpu.VMEM((2, moving, width), F32),
            pltpu.VMEM((3, moving, width), F32),
            pltpu.VMEM((3, moving, width), F32),
            pltpu.VMEM((3, moving, width), F32),
            pltpu.VMEM((KINDS - 6, moving, width), BF16),
        ],
        compiler_params=pltpu.CompilerParams(vmem_limit_bytes=40 * 1024 * 1024),
        name="band_rows",
    )(turns, got, fir_taps, poles, residues, skip_row, far_weight, ride)

    half = 3 * moving // 2
    right, left = pass_on(right, left)
    made = products(place, gated_band, out_weight, (3, -3, 2, -2))
    right, left, gated_band, sent = lax.optimization_barrier((right, left, gated_band, sent))
    own_home = own_home + right[half:].astype(F32) + left[half:].astype(F32)
    right, left = pass_on(*joined(made, 3, right[:half], left[:half]))
    back = swap(sent)
    right, left, gated_band = lax.optimization_barrier((right, left, gated_band))
    right, left = pass_on(*joined(made, 2, right, left))
    made = products(place, gated_band, out_weight, (1, -1, 0))
    right, left = lax.optimization_barrier((right, left))
    right, left = pass_on(*joined(made, 1, right, left))
    right, left = lax.optimization_barrier((right, left))
    own_band = made[0] + right.astype(F32) + left.astype(F32)
    scales, back = row_scales([own_band, own_home], back)
    mixed_band = (own_band * scales[: 3 * moving] * norm_gain[None]).astype(BF16)
    mixed_band = jnp.transpose(mixed_band.reshape(3, groups, CAP, own_cols), (1, 0, 2, 3))
    back, mixed_band = lax.optimization_barrier((back, mixed_band))
    mixed_back = swap(mixed_band)
    final_state, final_lagged = pl.pallas_call(
        finish_kernel,
        grid=(slots // 16,),
        in_specs=[
            pl.BlockSpec((8, 2 * MODES + 16, width), lambda i: (jnp.minimum(i, 3), 0, 0)),
            pl.BlockSpec((2, 3, 16, width), lambda i: (1, 0, i, 0)),
            whole((16, MODES, width)),
            whole((3, slots)),
        ],
        out_specs=[
            pl.BlockSpec((16, MODES, width), lambda i: (i, 0, 0)),
            pl.BlockSpec((16, 3, 2, width), lambda i: (i, 0, 0, 0)),
        ],
        out_shape=[
            jax.ShapeDtypeStruct(modal_state.shape, F32),
            jax.ShapeDtypeStruct(fir_buffer.shape, BF16),
        ],
        compiler_params=pltpu.CompilerParams(vmem_limit_bytes=56 * 1024 * 1024),
        name="last_rows",
    )(back, qkv_kinds, stay_state, finished)

    mixed_later = jnp.transpose(mixed_back, (1, 0, 2, 3)).reshape(3, moving, own_cols)
    mixed_home = (own_home * scales[3 * moving :] * norm_gain[None]).astype(BF16)
    mixed_stay = mixed_home[slots:].reshape(3, 16, own_cols)
    mixed = jnp.concatenate(
        [mixed_home[None, :slots], jnp.concatenate([mixed_later, mixed_stay], axis=1)], axis=0
    )
    return (mixed, final_state, final_lagged)


def solution(mesh):
    return jax.shard_map(
        per_device,
        mesh=mesh,
        in_specs=(
            P(None, "dp", None, "tensor"),
            P("dp", None, None, "tensor"),
            P(None, None, "tensor"),
            P("dp", None, "tensor"),
            P(None, "tensor"),
            P(None, "tensor"),
            P("tensor"),
            P("tensor", None),
            P("tensor"),
            P(None, "dp"),
            P(None, "dp"),
        ),
        out_specs=(P(None, "dp", "tensor"), P("dp", None, "tensor"), P("dp", None, None, "tensor")),
        check_vma=False,
    )
```

```python
import jax
import jax.numpy as jnp
from jax import lax
from jax.experimental import pallas as pl
from jax.experimental.pallas import tpu as pltpu
from jax.sharding import PartitionSpec as P

CAP = 2
MODES = 16
KINDS = 16
F32, BF16 = jnp.float32, jnp.bfloat16


def dot(a, b):
    return jnp.dot(a, b, preferred_element_type=F32)


def wide(x, width):
    return jnp.concatenate([x] * (width // x.shape[-1]), axis=-1)


def going_on(finished, block, rows, width):
    at = lax.broadcasted_iota(jnp.int32, (rows, finished.shape[1]), 0) + block * rows
    own = at == lax.broadcasted_iota(jnp.int32, at.shape, 1)
    ended = [
        jnp.sum(jnp.where(own, finished[t : t + 1].astype(F32), 0.0), axis=1, keepdims=True)
        for t in range(3)
    ]
    return [jnp.broadcast_to(1.0 - x, (rows, width)) for x in ended]


def home_kernel(qkv_hbm, fir_hbm, state_hbm, taps, poles, residues, skip, finished, packed_hbm, *rest):
    gated, stay_state, qkv_all, fir_all, state_all, packed_all, y_rows, sems = rest
    rows, width = 16, qkv_hbm.shape[-1]
    blocks = qkv_hbm.shape[2] // rows

    def fetches(block):
        at = pl.ds(block * rows, rows)
        return [
            pltpu.make_async_copy(state_hbm.at[at], state_all.at[at], sems.at[0, block]),
            pltpu.make_async_copy(qkv_hbm.at[:, :, at], qkv_all.at[:, :, at], sems.at[1, block]),
            pltpu.make_async_copy(fir_hbm.at[at], fir_all.at[at], sems.at[2, block]),
        ]

    def store(block):
        at = pl.ds(block * (rows // 2), rows // 2)
        return pltpu.make_async_copy(packed_all.at[at], packed_hbm.at[at], sems.at[3, block])

    for block in range(blocks):
        for fetch in fetches(block):
            fetch.start()

    def first_step(block):
        for fetch in fetches(block):
            fetch.wait()
        start = pl.multiple_of(block * rows, rows)
        qkv = qkv_all.at[:, :, pl.ds(start, rows)]
        fir = fir_all.at[pl.ds(start, rows)]
        state = state_all.at[pl.ds(start, rows)]
        alive = going_on(finished, block, rows, width)
        alive0 = alive[0]
        q0 = [qkv[0, j].astype(F32) for j in range(3)]
        l0 = [fir[:, j].astype(F32)[:, 0] for j in range(3)]
        l1 = [fir[:, j].astype(F32)[:, 1] for j in range(3)]
        f = [
            taps[j, 0:1] * q0[j] + taps[j, 1:2] * l0[j] + taps[j, 2:3] * l1[j]
            for j in range(3)
        ]
        product = f[1] * f[2]
        modes = []
        for r in range(rows):
            s = poles[...] * state[r] + product[r : r + 1]
            y_rows[r : r + 1] = jnp.sum(residues[...] * s, axis=0, keepdims=True)
            modes.append(s * alive0[r : r + 1])
        gated[pl.ds(block * rows, rows)] = (f[0] * (y_rows[...] + skip[...] * product)).astype(BF16)
        return qkv, q0, l0, alive, modes

    @pl.loop(0, blocks - 1)
    def _(block):
        qkv, q0, l0, alive, modes = first_step(block)
        alive0 = alive[0]
        packed = packed_all.at[pl.ds(pl.multiple_of(block * (rows // 2), rows // 2), rows // 2)]
        for pair in range(rows // 2):
            both = jnp.concatenate([modes[2 * pair], modes[2 * pair + 1]], axis=0)
            packed[pair, 0 : 2 * MODES] = both.astype(BF16)
        sent = [(x * alive0).astype(BF16) for x in q0 + l0]
        sent += [qkv[t, j] for t in range(1, 4) for j in range(3)]
        half = width // 2
        sent.append(jnp.concatenate([alive[1][:, :half], alive[2][:, :half]], axis=-1).astype(BF16))
        stacked = jnp.concatenate(sent, axis=0)
        n = KINDS * rows
        r = lax.broadcasted_iota(jnp.int32, (n, n), 0)
        c = lax.broadcasted_iota(jnp.int32, (n, n), 1)
        source = ((r >> 1) & 15) * rows + (r >> 5) * 2 + (r & 1)
        order = jnp.where(c == source, 1.0, 0.0).astype(BF16)
        moved = dot(order, stacked).reshape(rows // 2, 2 * KINDS, width)
        packed[:, 2 * MODES :] = moved.astype(BF16)
        store(block).start()

    modes = first_step(blocks - 1)[-1]
    for r in range(rows):
        stay_state[r] = modes[r]
    for block in range(blocks - 1):
        store(block).wait()


def stay_kernel(gated, qkv, fir, state, taps, poles, residues, skip, finished, all_gated, stay_state, y_rows):
    rows, width = 16, qkv.shape[-1]
    first = gated.shape[0]
    all_gated[:first] = gated[...]
    alive = going_on(finished, first // rows - 1, rows, width)
    lag0 = [qkv[0, j].astype(F32) * alive[0] for j in range(3)]
    lag1 = [fir[:, j].astype(F32)[:, 0] * alive[0] for j in range(3)]
    for t in range(1, 4):
        q = [qkv[t, j].astype(F32) for j in range(3)]
        f = [
            taps[j, 0:1] * q[j] + taps[j, 1:2] * lag0[j] + taps[j, 2:3] * lag1[j]
            for j in range(3)
        ]
        product = f[1] * f[2]
        for r in range(rows):
            s = poles[...] * (state if t == 1 else stay_state)[r] + product[r : r + 1]
            y_rows[r : r + 1] = jnp.sum(residues[...] * s, axis=0, keepdims=True)
            stay_state[r] = s * alive[t][r : r + 1] if t < 3 else s
        at = first + (t - 1) * rows
        all_gated[at : at + rows] = (f[0] * (y_rows[...] + skip[...] * product)).astype(BF16)
        if t < 3:
            lag0, lag1 = [x * alive[t] for x in q], [x * alive[t] for x in lag0]


def band_kernel(
    turns, got, taps, poles, residues, skip, far_weight, ride, sent, gated, first_right, first_left, *scratch
):
    lags, inputs, live, heads, products, y_rows, kinds = scratch
    groups, _, width = got.shape
    rows = 2 * groups

    n = 16 * KINDS
    r = lax.broadcasted_iota(jnp.int32, (n, n), 0)
    c = lax.broadcasted_iota(jnp.int32, (n, n), 1)
    source = ((r >> 1) & 7) * (2 * KINDS) + (r >> 4) * 2 + (r & 1)
    order = jnp.where(c == source, 1.0, 0.0).astype(BF16)
    for g in range(0, groups, 8):
        part = dot(order, got[g : g + 8, 2 * MODES :].reshape(n, width)).reshape(KINDS, 16, width)
        lags[:, 2 * g : 2 * g + 16] = part[:6]
        kinds[:, 2 * g : 2 * g + 16] = part[6:].astype(BF16)

    r = lax.broadcasted_iota(jnp.int32, (rows, rows), 0)
    c = lax.broadcasted_iota(jnp.int32, (rows, rows), 1)
    half = width // 2
    for t in range(3):
        turn = jnp.where(c == ((r + 2 * turns[t]) & (rows - 1)), 1.0, 0.0).astype(BF16)
        for j in range(3):
            inputs[t, j] = dot(turn, kinds[3 * t + j])
        if t < 2:
            live[t] = wide(dot(turn, kinds[9, :, t * half : (t + 1) * half]), width)

    @pl.loop(0, rows // 8)
    def _(i):
        at = pl.ds(pl.multiple_of(i * 8, 8), 8)
        lag0 = [lags[j, at] for j in range(3)]
        lag1 = [lags[3 + j, at] for j in range(3)]
        for t in range(3):
            q = [inputs[t, j, at] for j in range(3)]
            f = [
                taps[j, 0:1] * q[j] + taps[j, 1:2] * lag0[j] + taps[j, 2:3] * lag1[j]
                for j in range(3)
            ]
            heads[t, at] = f[0]
            products[t, at] = f[1] * f[2]
            if t < 2:
                on = live[t, at]
                lag0, lag1 = [x * on for x in q], [x * on for x in lag0]
                if t == 1:
                    for j in range(3):
                        lags[j, at] = lag0[j]

    shape = (groups * 16, 3 * rows)
    r = lax.broadcasted_iota(jnp.int32, shape, 0)
    c = lax.broadcasted_iota(jnp.int32, shape, 1)
    group = ((r >> 4) - turns[2] + groups) & (groups - 1)
    source = ((r & 15) >> 1) * rows + group * 2 + (r & 1)
    order = jnp.where((c == source) & ((r & 15) < 6), 1.0, 0.0).astype(BF16)
    last = lags[0:3].reshape(3 * rows, width).astype(BF16)
    sent[:, 2 * MODES :] = dot(order, last).reshape(groups, 16, width).astype(BF16)

    @pl.loop(0, groups)
    def _(g):
        final = []
        for side in range(2):
            row = pl.ds(g * 2 + side, 1)
            s = got[g, side * MODES : (side + 1) * MODES].astype(F32)
            for t in range(3):
                product = products[t, row]
                s = poles[...] * s + product
                y = jnp.sum(residues[...] * s, axis=0, keepdims=True)
                there = ((g + turns[t]) & (groups - 1)) * 2 + side
                y_rows[t, pl.ds(there, 1)] = heads[t, row] * (y + skip[...] * product)
                if t < 2:
                    s = s * live[t, row]
            final.append(s)
        end = (g + turns[2]) & (groups - 1)
        sent[end, 0 : 2 * MODES] = jnp.concatenate(final, axis=0).astype(BF16)

    gated[...] = y_rows[...].reshape(3 * rows, width).astype(BF16)
    half = 3 * rows // 2
    for way, first in enumerate((first_right, first_left)):
        load = dot(gated[way * half : (way + 1) * half], far_weight[...])
        first[:half] = load.astype(BF16)
        first[half:] = ride[way]


def products_kernel(place, gated, weight, part):
    part[0] = dot(gated[...], weight[...])


def products(place, gated, weight, aways):
    n = lax.axis_size("tensor")
    rows, width = gated.shape
    own_cols = weight.shape[1] // n
    assert aways == tuple((aways[0] - i // 2) * (1 - 2 * (i % 2)) for i in range(len(aways)))

    def column(i, place):
        return 0, (place[0] + n + (aways[0] - i // 2) * (1 - 2 * (i % 2))) % n

    part = pl.pallas_call(
        products_kernel,
        grid_spec=pltpu.PrefetchScalarGridSpec(
            num_scalar_prefetch=1,
            grid=(len(aways),),
            in_specs=[
                whole((rows, width)),
                pl.BlockSpec((width, own_cols), column),
            ],
            out_specs=pl.BlockSpec((1, rows, own_cols), lambda i, place: (i, 0, 0)),
        ),
        out_shape=jax.ShapeDtypeStruct((len(aways), rows, own_cols), F32),
        cost_estimate=pl.CostEstimate(
            flops=16 * rows * width * weight.shape[1], bytes_accessed=2 * weight.size, transcendentals=0
        ),
        compiler_params=pltpu.CompilerParams(vmem_limit_bytes=52 * 1024 * 1024),
        name="ring_products",
    )(place, gated, weight)
    return dict(zip(aways, part))


def finish_kernel(back, qkv, stay_state, finished, state, lagged):
    block = pl.program_id(0)
    rows, width = 16, qkv.shape[-1]

    def put(j, last):
        both = [qkv[1, j].astype(F32)[:, None], last[:, None]]
        lagged[:, j] = jnp.concatenate(both, axis=1).astype(BF16)

    @pl.when(block < 4)
    def _():
        n = back.shape[0]
        for b in range(n):
            for side in range(2):
                state[2 * b + side] = back[b, side * MODES : (side + 1) * MODES].astype(F32)
        shape = (3 * rows, n * 16)
        r = lax.broadcasted_iota(jnp.int32, shape, 0)
        c = lax.broadcasted_iota(jnp.int32, shape, 1)
        source = ((r & 15) >> 1) * 16 + (r >> 4) * 2 + (r & 1)
        order = jnp.where(c == source, 1.0, 0.0).astype(BF16)
        last = dot(order, back[:, 2 * MODES :].reshape(n * 16, width))
        for j in range(3):
            put(j, last[j * rows : (j + 1) * rows])

    @pl.when(block == 4)
    def _():
        state[...] = stay_state[...]
        at = lax.broadcasted_iota(jnp.int32, (rows, finished.shape[1]), 0) + block * rows
        own = at == lax.broadcasted_iota(jnp.int32, at.shape, 1)
        ended = jnp.where(own, finished[2:3].astype(F32), 0.0)
        alive = 1.0 - jnp.sum(ended, axis=1, keepdims=True)
        for j in range(3):
            put(j, qkv[0, j].astype(F32) * alive)


def whole(shape):
    return pl.BlockSpec(shape, lambda *_: (0,) * len(shape))


def swap(blocks):
    return lax.all_to_all(blocks, "dp", split_axis=0, concat_axis=0, tiled=True)


def pass_on(right, left):
    n = lax.axis_size("tensor")
    right = lax.ppermute(right, "tensor", [(i, (i + 1) % n) for i in range(n)])
    left = lax.ppermute(left, "tensor", [(i, (i - 1) % n) for i in range(n)])
    return right, left


def joined(made, away, right, left):
    ahead, behind = made[away], made[-away]
    half = right.shape[0]
    if half < ahead.shape[0]:
        ahead = ahead.at[:half].add(right.astype(F32))
        behind = behind.at[half:].add(left.astype(F32))
    else:
        ahead, behind = ahead + right.astype(F32), behind + left.astype(F32)
    return ahead.astype(BF16), behind.astype(BF16)


def row_scales(own, back):
    n = lax.axis_size("tensor")
    squares = jnp.concatenate([jnp.sum(x * x, axis=1) for x in own])

    def sent_on(x, away):
        return lax.ppermute(x, "tensor", [(i, (i + away) % n) for i in range(n)])

    four = squares + (sent_on(squares, 1) + sent_on(squares, -1)) + sent_on(squares, 2)
    four, back = lax.optimization_barrier((four, back))
    squares = sent_on(four, 2) + sent_on(four, -2)
    return lax.rsqrt(squares / (n * own[0].shape[1]) + 1e-05)[:, None], back


def per_device(
    qkv,
    fir_buffer,
    fir_taps,
    modal_state,
    poles,
    residues,
    skip,
    out_weight,
    norm_gain,
    finished,
    dest_group,
):
    groups = lax.axis_size("dp")
    own_group = lax.axis_index("dp")
    slots, width = modal_state.shape[0], modal_state.shape[2]
    moving = groups * CAP
    qkv_kinds = jnp.transpose(qkv, (0, 2, 1, 3))
    skip_row = skip[None]
    shifts = lax.dynamic_slice_in_dim(dest_group, own_group * CAP, 1, 1)[:, 0] - own_group + groups
    turns = jnp.cumsum(shifts).astype(jnp.int32) % groups

    packed, gated_first, stay_first = pl.pallas_call(
        home_kernel,
        in_specs=[pl.BlockSpec(memory_space=pl.ANY)] * 3
        + [pl.BlockSpec(memory_space=pltpu.VMEM)] * 5,
        out_specs=[pl.BlockSpec(memory_space=pl.ANY)]
        + [pl.BlockSpec(memory_space=pltpu.VMEM)] * 2,
        out_shape=[
            jax.ShapeDtypeStruct((groups, 2 * MODES + 2 * KINDS, width), BF16),
            jax.ShapeDtypeStruct((slots, width), BF16),
            jax.ShapeDtypeStruct((16, MODES, width), F32),
        ],
        scratch_shapes=[
            pltpu.VMEM(qkv_kinds.shape, BF16),
            pltpu.VMEM(fir_buffer.shape, BF16),
            pltpu.VMEM(modal_state.shape, F32),
            pltpu.VMEM((groups, 2 * MODES + 2 * KINDS, width), BF16),
            pltpu.VMEM((16, width), F32),
            pltpu.SemaphoreType.DMA((4, slots // 16)),
        ],
        compiler_params=pltpu.CompilerParams(vmem_limit_bytes=56 * 1024 * 1024),
        name="home_rows",
    )(qkv_kinds, fir_buffer, modal_state, fir_taps, poles, residues, skip_row, finished)

    n, own_cols = lax.axis_size("tensor"), norm_gain.shape[0]
    last = slots // 16 - 1
    gated_home, stay_state = pl.pallas_call(
        stay_kernel,
        grid=(1,),
        in_specs=[
            whole((slots, width)),
            pl.BlockSpec((4, 3, 16, width), lambda i: (0, 0, last, 0)),
            pl.BlockSpec((16, 3, 2, width), lambda i: (last, 0, 0, 0)),
            whole((16, MODES, width)),
            whole((3, 3, width)),
            whole((MODES, width)),
            whole((MODES, width)),
            whole((1, width)),
            whole((3, slots)),
        ],
        out_specs=[whole((slots + 48, width)), whole((16, MODES, width))],
        out_shape=[
            jax.ShapeDtypeStruct((slots + 48, width), BF16),
            jax.ShapeDtypeStruct((16, MODES, width), F32),
        ],
        scratch_shapes=[pltpu.VMEM((16, width), F32)],
        compiler_params=pltpu.CompilerParams(vmem_limit_bytes=56 * 1024 * 1024),
        name="stay_rows",
    )(gated_first, qkv_kinds, fir_buffer, stay_first, fir_taps, poles, residues, skip_row, finished)

    gated_home, later_weight = lax.optimization_barrier((gated_home, out_weight))
    place = lax.axis_index("tensor").astype(jnp.int32)[None]
    far_place = (place[0] + n // 2) % n
    far_weight = lax.dynamic_slice_in_dim(later_weight, far_place * own_cols, own_cols, 1)
    got = swap(packed)
    far = dot(gated_home, far_weight).astype(BF16)
    half = far.shape[0] // 2
    right, left = pass_on(far[:half], far[half:])
    made = products(place, gated_home, out_weight, (3, -3, 2, -2))
    right, left = lax.optimization_barrier((right, left))
    right, left, gated_home = lax.optimization_barrier((*pass_on(*joined(made, 3, right, left)), gated_home))
    right, left = pass_on(*joined(made, 2, right, left))
    made = products(place, gated_home, out_weight, (1, -1, 0))
    right, left = lax.optimization_barrier((right, left))
    ride = jnp.stack(joined(made, 1, right, left))
    got, ride, own_home = lax.optimization_barrier((got, ride, made[0]))

    sent, gated_band, right, left = pl.pallas_call(
        band_kernel,
        in_specs=[
            pl.BlockSpec(memory_space=pltpu.SMEM),
        ]
        + [pl.BlockSpec(memory_space=pltpu.VMEM)] * 7,
        out_specs=[pl.BlockSpec(memory_space=pltpu.VMEM)] * 4,
        out_shape=[
            jax.ShapeDtypeStruct((groups, 2 * MODES + 16, width), BF16),
            jax.ShapeDtypeStruct((3 * moving, width), BF16),
            jax.ShapeDtypeStruct((3 * moving // 2 + slots + 48, own_cols), BF16),
            jax.ShapeDtypeStruct((3 * moving // 2 + slots + 48, own_cols), BF16),
        ],
        scratch_shapes=[
            pltpu.VMEM((6, moving, width), F32),
            pltpu.VMEM((3, 3, moving, width), F32),
            pltpu.VMEM((2, moving, width), F32),
            pltpu.VMEM((3, moving, width), F32),
            pltpu.VMEM((3, moving, width), F32),
            pltpu.VMEM((3, moving, width), F32),
            pltpu.VMEM((KINDS - 6, moving, width), BF16),
        ],
        compiler_params=pltpu.CompilerParams(vmem_limit_bytes=40 * 1024 * 1024),
        name="band_rows",
    )(turns, got, fir_taps, poles, residues, skip_row, far_weight, ride)

    half = 3 * moving // 2
    right, left = pass_on(right, left)
    made = products(place, gated_band, out_weight, (3, -3, 2, -2))
    right, left, gated_band, sent = lax.optimization_barrier((right, left, gated_band, sent))
    own_home = own_home + right[half:].astype(F32) + left[half:].astype(F32)
    right, left = pass_on(*joined(made, 3, right[:half], left[:half]))
    back = swap(sent)
    right, left, gated_band = lax.optimization_barrier((right, left, gated_band))
    right, left = pass_on(*joined(made, 2, right, left))
    made = products(place, gated_band, out_weight, (1, -1, 0))
    right, left = lax.optimization_barrier((right, left))
    right, left = pass_on(*joined(made, 1, right, left))
    right, left = lax.optimization_barrier((right, left))
    own_band = made[0] + right.astype(F32) + left.astype(F32)
    scales, back = row_scales([own_band, own_home], back)
    mixed_band = (own_band * scales[: 3 * moving] * norm_gain[None]).astype(BF16)
    mixed_band = jnp.transpose(mixed_band.reshape(3, groups, CAP, own_cols), (1, 0, 2, 3))
    back, mixed_band = lax.optimization_barrier((back, mixed_band))
    mixed_back = swap(mixed_band)
    final_state, final_lagged = pl.pallas_call(
        finish_kernel,
        grid=(slots // 16,),
        in_specs=[
            pl.BlockSpec((8, 2 * MODES + 16, width), lambda i: (jnp.minimum(i, 3), 0, 0)),
            pl.BlockSpec((2, 3, 16, width), lambda i: (1, 0, i, 0)),
            whole((16, MODES, width)),
            whole((3, slots)),
        ],
        out_specs=[
            pl.BlockSpec((16, MODES, width), lambda i: (i, 0, 0)),
            pl.BlockSpec((16, 3, 2, width), lambda i: (i, 0, 0, 0)),
        ],
        out_shape=[
            jax.ShapeDtypeStruct(modal_state.shape, F32),
            jax.ShapeDtypeStruct(fir_buffer.shape, BF16),
        ],
        compiler_params=pltpu.CompilerParams(vmem_limit_bytes=56 * 1024 * 1024),
        name="last_rows",
    )(back, qkv_kinds, stay_state, finished)

    mixed_later = jnp.transpose(mixed_back, (1, 0, 2, 3)).reshape(3, moving, own_cols)
    mixed_home = (own_home * scales[3 * moving :] * norm_gain[None]).astype(BF16)
    mixed_stay = mixed_home[slots:].reshape(3, 16, own_cols)
    mixed = jnp.concatenate(
        [mixed_home[None, :slots], jnp.concatenate([mixed_later, mixed_stay], axis=1)], axis=0
    )
    return (mixed, final_state, final_lagged)


def solution(mesh):
    return jax.shard_map(
        per_device,
        mesh=mesh,
        in_specs=(
            P(None, "dp", None, "tensor"),
            P("dp", None, None, "tensor"),
            P(None, None, "tensor"),
            P("dp", None, "tensor"),
            P(None, "tensor"),
            P(None, "tensor"),
            P("tensor"),
            P("tensor", None),
            P("tensor"),
            P(None, "dp"),
            P(None, "dp"),
        ),
        out_specs=(P(None, "dp", "tensor"), P("dp", None, "tensor"), P("dp", None, None, "tensor")),
        check_vma=False,
    )
```

```python
import jax
import jax.numpy as jnp
from jax import lax
from jax.experimental import pallas as pl
from jax.experimental.pallas import tpu as pltpu
from jax.sharding import PartitionSpec as P

CAP = 2
MODES = 16
KINDS = 16
F32, BF16 = jnp.float32, jnp.bfloat16


def dot(a, b):
    return jnp.dot(a, b, preferred_element_type=F32)


def wide(x, width):
    return jnp.concatenate([x] * (width // x.shape[-1]), axis=-1)


def home_kernel(qkv_hbm, fir_hbm, state_hbm, taps, poles, residues, skip, finished, packed_hbm, *rest):
    gated, stay_state, qkv_all, fir_all, state_all, packed_all, y_rows, sems = rest
    rows, width = 16, qkv_hbm.shape[-1]
    blocks = qkv_hbm.shape[2] // rows

    def fetches(block):
        at = pl.ds(block * rows, rows)
        return [
            pltpu.make_async_copy(state_hbm.at[at], state_all.at[at], sems.at[0, block]),
            pltpu.make_async_copy(qkv_hbm.at[:, :, at], qkv_all.at[:, :, at], sems.at[1, block]),
            pltpu.make_async_copy(fir_hbm.at[at], fir_all.at[at], sems.at[2, block]),
        ]

    def store(block):
        at = pl.ds(block * (rows // 2), rows // 2)
        return pltpu.make_async_copy(packed_all.at[at], packed_hbm.at[at], sems.at[3, block])

    for block in range(2):
        for fetch in fetches(block):
            fetch.start()

    def first_step(block):
        @pl.when(block + 2 < blocks)
        def _():
            for fetch in fetches(block + 2):
                fetch.start()

        for fetch in fetches(block):
            fetch.wait()
        start = pl.multiple_of(block * rows, rows)
        qkv = qkv_all.at[:, :, pl.ds(start, rows)]
        fir = fir_all.at[pl.ds(start, rows)]
        state = state_all.at[pl.ds(start, rows)]
        at = lax.broadcasted_iota(jnp.int32, (rows, finished.shape[1]), 0) + block * rows
        own = at == lax.broadcasted_iota(jnp.int32, at.shape, 1)
        alive = [
            jnp.broadcast_to(
                1.0 - jnp.sum(jnp.where(own, finished[t : t + 1].astype(F32), 0.0), axis=1, keepdims=True),
                (rows, width),
            )
            for t in range(3)
        ]
        alive0 = alive[0]
        q0 = [qkv[0, j].astype(F32) for j in range(3)]
        l0 = [fir[:, j].astype(F32)[:, 0] for j in range(3)]
        l1 = [fir[:, j].astype(F32)[:, 1] for j in range(3)]
        f = [
            taps[j, 0:1] * q0[j] + taps[j, 1:2] * l0[j] + taps[j, 2:3] * l1[j]
            for j in range(3)
        ]
        product = f[1] * f[2]
        modes = []
        for r in range(rows):
            s = poles[...] * state[r] + product[r : r + 1]
            y_rows[r : r + 1] = jnp.sum(residues[...] * s, axis=0, keepdims=True)
            modes.append(s * alive0[r : r + 1])
        gated[pl.ds(block * rows, rows)] = (f[0] * (y_rows[...] + skip[...] * product)).astype(BF16)
        return qkv, q0, l0, alive, modes

    @pl.loop(0, blocks - 1)
    def _(block):
        qkv, q0, l0, alive, modes = first_step(block)
        alive0 = alive[0]
        packed = packed_all.at[pl.ds(pl.multiple_of(block * (rows // 2), rows // 2), rows // 2)]
        for pair in range(rows // 2):
            both = jnp.concatenate([modes[2 * pair], modes[2 * pair + 1]], axis=0)
            packed[pair, 0 : 2 * MODES] = both.astype(BF16)
        sent = [(x * alive0).astype(BF16) for x in q0 + l0]
        sent += [qkv[t, j] for t in range(1, 4) for j in range(3)]
        half = width // 2
        sent.append(jnp.concatenate([alive[1][:, :half], alive[2][:, :half]], axis=-1).astype(BF16))
        stacked = jnp.concatenate(sent, axis=0)
        n = KINDS * rows
        r = lax.broadcasted_iota(jnp.int32, (n, n), 0)
        c = lax.broadcasted_iota(jnp.int32, (n, n), 1)
        source = ((r >> 1) & 15) * rows + (r >> 5) * 2 + (r & 1)
        order = jnp.where(c == source, 1.0, 0.0).astype(BF16)
        moved = dot(order, stacked).reshape(rows // 2, 2 * KINDS, width)
        packed[:, 2 * MODES :] = moved.astype(BF16)
        store(block).start()

    qkv, q0, l0, alive, modes = first_step(blocks - 1)
    alive0 = alive[0]
    for r in range(rows):
        stay_state[r] = modes[r]
    lag0, lag1 = [x * alive0 for x in q0], [x * alive0 for x in l0]
    for t in range(1, 4):
        q = [qkv[t, j].astype(F32) for j in range(3)]
        g = [
            taps[j, 0:1] * q[j] + taps[j, 1:2] * lag0[j] + taps[j, 2:3] * lag1[j]
            for j in range(3)
        ]
        prod = g[1] * g[2]
        live = alive[t] if t < 3 else None
        for r in range(rows):
            s = poles[...] * stay_state[r] + prod[r : r + 1]
            y_rows[r : r + 1] = jnp.sum(residues[...] * s, axis=0, keepdims=True)
            stay_state[r] = s * live[r : r + 1] if t < 3 else s
        gated[64 + t * rows : 80 + t * rows] = (
            g[0] * (y_rows[...] + skip[...] * prod)
        ).astype(BF16)
        if t < 3:
            lag0, lag1 = [x * live for x in q], [x * live for x in lag0]
    for block in range(blocks - 1):
        store(block).wait()


def band_kernel(
    turns, got, taps, poles, residues, skip, far_weight, ride, sent, gated, first_right, first_left, *scratch
):
    lags, inputs, live, heads, products, y_rows, kinds = scratch
    groups, _, width = got.shape
    rows = 2 * groups

    n = 16 * KINDS
    r = lax.broadcasted_iota(jnp.int32, (n, n), 0)
    c = lax.broadcasted_iota(jnp.int32, (n, n), 1)
    source = ((r >> 1) & 7) * (2 * KINDS) + (r >> 4) * 2 + (r & 1)
    order = jnp.where(c == source, 1.0, 0.0).astype(BF16)
    for g in range(0, groups, 8):
        part = dot(order, got[g : g + 8, 2 * MODES :].reshape(n, width)).reshape(KINDS, 16, width)
        lags[:, 2 * g : 2 * g + 16] = part[:6]
        kinds[:, 2 * g : 2 * g + 16] = part[6:].astype(BF16)

    r = lax.broadcasted_iota(jnp.int32, (rows, rows), 0)
    c = lax.broadcasted_iota(jnp.int32, (rows, rows), 1)
    half = width // 2
    for t in range(3):
        turn = jnp.where(c == ((r + 2 * turns[t]) & (rows - 1)), 1.0, 0.0).astype(BF16)
        for j in range(3):
            inputs[t, j] = dot(turn, kinds[3 * t + j])
        if t < 2:
            live[t] = wide(dot(turn, kinds[9, :, t * half : (t + 1) * half]), width)

    @pl.loop(0, rows // 8)
    def _(i):
        at = pl.ds(pl.multiple_of(i * 8, 8), 8)
        lag0 = [lags[j, at] for j in range(3)]
        lag1 = [lags[3 + j, at] for j in range(3)]
        for t in range(3):
            q = [inputs[t, j, at] for j in range(3)]
            f = [
                taps[j, 0:1] * q[j] + taps[j, 1:2] * lag0[j] + taps[j, 2:3] * lag1[j]
                for j in range(3)
            ]
            heads[t, at] = f[0]
            products[t, at] = f[1] * f[2]
            if t < 2:
                on = live[t, at]
                lag0, lag1 = [x * on for x in q], [x * on for x in lag0]
                if t == 1:
                    for j in range(3):
                        lags[j, at] = lag0[j]

    shape = (groups * 16, 3 * rows)
    r = lax.broadcasted_iota(jnp.int32, shape, 0)
    c = lax.broadcasted_iota(jnp.int32, shape, 1)
    group = ((r >> 4) - turns[2] + groups) & (groups - 1)
    source = ((r & 15) >> 1) * rows + group * 2 + (r & 1)
    order = jnp.where((c == source) & ((r & 15) < 6), 1.0, 0.0).astype(BF16)
    last = lags[0:3].reshape(3 * rows, width).astype(BF16)
    sent[:, 2 * MODES :] = dot(order, last).reshape(groups, 16, width).astype(BF16)

    @pl.loop(0, groups)
    def _(g):
        final = []
        for side in range(2):
            row = pl.ds(g * 2 + side, 1)
            s = got[g, side * MODES : (side + 1) * MODES].astype(F32)
            for t in range(3):
                product = products[t, row]
                s = poles[...] * s + product
                y = jnp.sum(residues[...] * s, axis=0, keepdims=True)
                there = ((g + turns[t]) & (groups - 1)) * 2 + side
                y_rows[t, pl.ds(there, 1)] = heads[t, row] * (y + skip[...] * product)
                if t < 2:
                    s = s * live[t, row]
            final.append(s)
        end = (g + turns[2]) & (groups - 1)
        sent[end, 0 : 2 * MODES] = jnp.concatenate(final, axis=0).astype(BF16)

    gated[...] = y_rows[...].reshape(3 * rows, width).astype(BF16)
    half = 3 * rows // 2
    for way, first in enumerate((first_right, first_left)):
        load = dot(gated[way * half : (way + 1) * half], far_weight[...])
        first[:half] = load.astype(BF16)
        first[half:] = ride[way]


def products_kernel(place, gated, weight, part):
    part[0] = dot(gated[...], weight[...])


def products(place, gated, weight, aways):
    n = lax.axis_size("tensor")
    rows, width = gated.shape
    own_cols = weight.shape[1] // n
    assert aways == tuple((aways[0] - i // 2) * (1 - 2 * (i % 2)) for i in range(len(aways)))

    def column(i, place):
        return 0, (place[0] + n + (aways[0] - i // 2) * (1 - 2 * (i % 2))) % n

    part = pl.pallas_call(
        products_kernel,
        grid_spec=pltpu.PrefetchScalarGridSpec(
            num_scalar_prefetch=1,
            grid=(len(aways),),
            in_specs=[
                whole((rows, width)),
                pl.BlockSpec((width, own_cols), column),
            ],
            out_specs=pl.BlockSpec((1, rows, own_cols), lambda i, place: (i, 0, 0)),
        ),
        out_shape=jax.ShapeDtypeStruct((len(aways), rows, own_cols), F32),
        cost_estimate=pl.CostEstimate(
            flops=16 * rows * width * weight.shape[1], bytes_accessed=2 * weight.size, transcendentals=0
        ),
        compiler_params=pltpu.CompilerParams(vmem_limit_bytes=52 * 1024 * 1024),
        name="ring_products",
    )(place, gated, weight)
    return dict(zip(aways, part))


def finish_kernel(back_hbm, qkv_hbm, stay_hbm, finished, state_hbm, lagged_hbm, *rest):
    back_all, qkv_all, state_all, lagged_all, sems = rest
    rows, width = 16, qkv_hbm.shape[-1]
    blocks = qkv_hbm.shape[2] // rows
    n = rows // 2

    def qkv_fetch(block):
        at = pl.ds(block * rows, rows)
        return pltpu.make_async_copy(qkv_hbm.at[2:4, :, at], qkv_all.at[:, :, at], sems.at[0, block])

    def back_fetch(block):
        at = pl.ds(block * n, n)
        return pltpu.make_async_copy(back_hbm.at[at], back_all.at[at], sems.at[1, block])

    def stores(block):
        at = pl.ds(block * rows, rows)
        return [
            pltpu.make_async_copy(state_all.at[at], state_hbm.at[at], sems.at[2, block]),
            pltpu.make_async_copy(lagged_all.at[at], lagged_hbm.at[at], sems.at[3, block]),
        ]

    for block in range(blocks):
        qkv_fetch(block).start()
        if block < blocks - 1:
            back_fetch(block).start()
    last_at = pl.ds((blocks - 1) * rows, rows)
    stay = pltpu.make_async_copy(stay_hbm, state_all.at[last_at], sems.at[1, blocks - 1])
    stay.start()

    def put(block, j, last):
        at = pl.ds(pl.multiple_of(block * rows, rows), rows)
        both = [qkv_all[1, j, at].astype(F32)[:, None], last[:, None]]
        lagged_all[at, j] = jnp.concatenate(both, axis=1).astype(BF16)

    r = lax.broadcasted_iota(jnp.int32, (3 * rows, n * 16), 0)
    c = lax.broadcasted_iota(jnp.int32, (3 * rows, n * 16), 1)
    source = ((r & 15) >> 1) * 16 + (r >> 4) * 2 + (r & 1)
    order = jnp.where(c == source, 1.0, 0.0).astype(BF16)

    @pl.loop(0, blocks - 1)
    def _(block):
        qkv_fetch(block).wait()
        back_fetch(block).wait()
        back = back_all.at[pl.ds(pl.multiple_of(block * n, n), n)]
        for b in range(n):
            for side in range(2):
                part = back[b, side * MODES : (side + 1) * MODES].astype(F32)
                state_all[block * rows + 2 * b + side] = part
        last = dot(order, back[:, 2 * MODES :].reshape(n * 16, width))
        for j in range(3):
            put(block, j, last[j * rows : (j + 1) * rows])
        for store in stores(block):
            store.start()

    qkv_fetch(blocks - 1).wait()
    stay.wait()
    at = lax.broadcasted_iota(jnp.int32, (rows, finished.shape[1]), 0) + (blocks - 1) * rows
    own = at == lax.broadcasted_iota(jnp.int32, at.shape, 1)
    ended = jnp.where(own, finished[2:3].astype(F32), 0.0)
    alive = 1.0 - jnp.sum(ended, axis=1, keepdims=True)
    for j in range(3):
        put(blocks - 1, j, qkv_all[0, j, last_at].astype(F32) * alive)
    for store in stores(blocks - 1):
        store.start()
    for block in range(blocks):
        for store in stores(block):
            store.wait()


def whole(shape):
    return pl.BlockSpec(shape, lambda *_: (0,) * len(shape))


def swap(blocks):
    return lax.all_to_all(blocks, "dp", split_axis=0, concat_axis=0, tiled=True)


def pass_on(right, left):
    n = lax.axis_size("tensor")
    right = lax.ppermute(right, "tensor", [(i, (i + 1) % n) for i in range(n)])
    left = lax.ppermute(left, "tensor", [(i, (i - 1) % n) for i in range(n)])
    return right, left


def joined(made, away, right, left):
    ahead, behind = made[away], made[-away]
    half = right.shape[0]
    if half < ahead.shape[0]:
        ahead = ahead.at[:half].add(right.astype(F32))
        behind = behind.at[half:].add(left.astype(F32))
    else:
        ahead, behind = ahead + right.astype(F32), behind + left.astype(F32)
    return ahead.astype(BF16), behind.astype(BF16)


def row_scales(own, back):
    n = lax.axis_size("tensor")
    squares = jnp.concatenate([jnp.sum(x * x, axis=1) for x in own])

    def sent_on(x, away):
        return lax.ppermute(x, "tensor", [(i, (i + away) % n) for i in range(n)])

    below = squares + sent_on(squares, 1)
    three = below + sent_on(squares, -1)
    three, below, back = lax.optimization_barrier((three, below, back))
    squares = three + (sent_on(three, 3) + sent_on(below, -3))
    return lax.rsqrt(squares / (n * own[0].shape[1]) + 1e-05)[:, None], back


def per_device(
    qkv,
    fir_buffer,
    fir_taps,
    modal_state,
    poles,
    residues,
    skip,
    out_weight,
    norm_gain,
    finished,
    dest_group,
):
    groups = lax.axis_size("dp")
    own_group = lax.axis_index("dp")
    slots, width = modal_state.shape[0], modal_state.shape[2]
    moving = groups * CAP
    qkv_kinds = jnp.transpose(qkv, (0, 2, 1, 3))
    skip_row = skip[None]
    shifts = lax.dynamic_slice_in_dim(dest_group, own_group * CAP, 1, 1)[:, 0] - own_group + groups
    turns = jnp.cumsum(shifts).astype(jnp.int32) % groups

    packed, gated_home, stay_state = pl.pallas_call(
        home_kernel,
        in_specs=[pl.BlockSpec(memory_space=pl.ANY)] * 3
        + [pl.BlockSpec(memory_space=pltpu.VMEM)] * 5,
        out_specs=[pl.BlockSpec(memory_space=pl.ANY)]
        + [pl.BlockSpec(memory_space=pltpu.VMEM)] * 2,
        out_shape=[
            jax.ShapeDtypeStruct((groups, 2 * MODES + 2 * KINDS, width), BF16),
            jax.ShapeDtypeStruct((slots + 48, width), BF16),
            jax.ShapeDtypeStruct((16, MODES, width), F32),
        ],
        scratch_shapes=[
            pltpu.VMEM(qkv_kinds.shape, BF16),
            pltpu.VMEM(fir_buffer.shape, BF16),
            pltpu.VMEM(modal_state.shape, F32),
            pltpu.VMEM((groups, 2 * MODES + 2 * KINDS, width), BF16),
            pltpu.VMEM((16, width), F32),
            pltpu.SemaphoreType.DMA((4, slots // 16)),
        ],
        compiler_params=pltpu.CompilerParams(vmem_limit_bytes=56 * 1024 * 1024),
        name="home_rows",
    )(qkv_kinds, fir_buffer, modal_state, fir_taps, poles, residues, skip_row, finished)

    n, own_cols = lax.axis_size("tensor"), norm_gain.shape[0]
    gated_home, later_weight = lax.optimization_barrier((gated_home, out_weight))
    place = lax.axis_index("tensor").astype(jnp.int32)[None]
    far_place = (place[0] + n // 2) % n
    far_weight = lax.dynamic_slice_in_dim(later_weight, far_place * own_cols, own_cols, 1)
    got = swap(packed)
    far = dot(gated_home, far_weight).astype(BF16)
    half = far.shape[0] // 2
    right, left = pass_on(far[:half], far[half:])
    made = products(place, gated_home, out_weight, (3, -3, 2, -2))
    right, left = lax.optimization_barrier((right, left))
    right, left, gated_home = lax.optimization_barrier((*pass_on(*joined(made, 3, right, left)), gated_home))
    right, left = pass_on(*joined(made, 2, right, left))
    made = products(place, gated_home, out_weight, (1, -1, 0))
    right, left = lax.optimization_barrier((right, left))
    ride = jnp.stack(joined(made, 1, right, left))
    got, ride, own_home = lax.optimization_barrier((got, ride, made[0]))

    sent, gated_band, right, left = pl.pallas_call(
        band_kernel,
        in_specs=[
            pl.BlockSpec(memory_space=pltpu.SMEM),
        ]
        + [pl.BlockSpec(memory_space=pltpu.VMEM)] * 7,
        out_specs=[pl.BlockSpec(memory_space=pltpu.VMEM)] * 4,
        out_shape=[
            jax.ShapeDtypeStruct((groups, 2 * MODES + 16, width), BF16),
            jax.ShapeDtypeStruct((3 * moving, width), BF16),
            jax.ShapeDtypeStruct((3 * moving // 2 + slots + 48, own_cols), BF16),
            jax.ShapeDtypeStruct((3 * moving // 2 + slots + 48, own_cols), BF16),
        ],
        scratch_shapes=[
            pltpu.VMEM((6, moving, width), F32),
            pltpu.VMEM((3, 3, moving, width), F32),
            pltpu.VMEM((2, moving, width), F32),
            pltpu.VMEM((3, moving, width), F32),
            pltpu.VMEM((3, moving, width), F32),
            pltpu.VMEM((3, moving, width), F32),
            pltpu.VMEM((KINDS - 6, moving, width), BF16),
        ],
        compiler_params=pltpu.CompilerParams(vmem_limit_bytes=40 * 1024 * 1024),
        name="band_rows",
    )(turns, got, fir_taps, poles, residues, skip_row, far_weight, ride)

    half = 3 * moving // 2
    right, left = pass_on(right, left)
    made = products(place, gated_band, out_weight, (3, -3, 2, -2))
    right, left, gated_band, sent = lax.optimization_barrier((right, left, gated_band, sent))
    own_home = own_home + right[half:].astype(F32) + left[half:].astype(F32)
    right, left = pass_on(*joined(made, 3, right[:half], left[:half]))
    back = swap(sent)
    right, left, gated_band = lax.optimization_barrier((right, left, gated_band))
    right, left = pass_on(*joined(made, 2, right, left))
    made = products(place, gated_band, out_weight, (1, -1, 0))
    right, left = lax.optimization_barrier((right, left))
    right, left = pass_on(*joined(made, 1, right, left))
    right, left = lax.optimization_barrier((right, left))
    own_band = made[0] + right.astype(F32) + left.astype(F32)
    scales, back = row_scales([own_band, own_home], back)
    mixed_band = (own_band * scales[: 3 * moving] * norm_gain[None]).astype(BF16)
    mixed_band = jnp.transpose(mixed_band.reshape(3, groups, CAP, own_cols), (1, 0, 2, 3))
    back, mixed_band = lax.optimization_barrier((back, mixed_band))
    mixed_back = swap(mixed_band)
    final_state, final_lagged = pl.pallas_call(
        finish_kernel,
        in_specs=[pl.BlockSpec(memory_space=pl.ANY)] * 3 + [pl.BlockSpec(memory_space=pltpu.VMEM)],
        out_specs=[pl.BlockSpec(memory_space=pl.ANY)] * 2,
        out_shape=[
            jax.ShapeDtypeStruct(modal_state.shape, F32),
            jax.ShapeDtypeStruct(fir_buffer.shape, BF16),
        ],
        scratch_shapes=[
            pltpu.VMEM(back.shape, BF16),
            pltpu.VMEM((2, 3, slots, width), BF16),
            pltpu.VMEM(modal_state.shape, F32),
            pltpu.VMEM(fir_buffer.shape, BF16),
            pltpu.SemaphoreType.DMA((4, slots // 16)),
        ],
        compiler_params=pltpu.CompilerParams(vmem_limit_bytes=56 * 1024 * 1024),
        name="last_rows",
    )(back, qkv_kinds, stay_state, finished)

    mixed_later = jnp.transpose(mixed_back, (1, 0, 2, 3)).reshape(3, moving, own_cols)
    mixed_home = (own_home * scales[3 * moving :] * norm_gain[None]).astype(BF16)
    mixed_stay = mixed_home[slots:].reshape(3, 16, own_cols)
    mixed = jnp.concatenate(
        [mixed_home[None, :slots], jnp.concatenate([mixed_later, mixed_stay], axis=1)], axis=0
    )
    return (mixed, final_state, final_lagged)


def solution(mesh):
    return jax.shard_map(
        per_device,
        mesh=mesh,
        in_specs=(
            P(None, "dp", None, "tensor"),
            P("dp", None, None, "tensor"),
            P(None, None, "tensor"),
            P("dp", None, "tensor"),
            P(None, "tensor"),
            P(None, "tensor"),
            P("tensor"),
            P("tensor", None),
            P("tensor"),
            P(None, "dp"),
            P(None, "dp"),
        ),
        out_specs=(P(None, "dp", "tensor"), P("dp", None, "tensor"), P("dp", None, None, "tensor")),
        check_vma=False,
    )
```

```python
import jax
import jax.numpy as jnp
from jax import lax
from jax.experimental import pallas as pl
from jax.experimental.pallas import tpu as pltpu
from jax.sharding import PartitionSpec as P

CAP = 2
MODES = 16
KINDS = 16
F32, BF16 = jnp.float32, jnp.bfloat16


def dot(a, b):
    return jnp.dot(a, b, preferred_element_type=F32)


def wide(x, width):
    return jnp.concatenate([x] * (width // x.shape[-1]), axis=-1)


def home_kernel(qkv_hbm, fir_hbm, state_hbm, *rest):
    small_hbm, (packed_hbm, gated_hbm, stay_hbm), rest = rest[:5], rest[5:8], rest[8:]
    small_all, (gated, stay_state, qkv_all, fir_all, state_all, packed_all, y_rows, sems) = rest[:5], rest[5:]
    rows, width = 16, qkv_hbm.shape[-1]
    blocks = qkv_hbm.shape[2] // rows

    def fetches(block):
        at = pl.ds(block * rows, rows)
        return [
            pltpu.make_async_copy(state_hbm.at[at], state_all.at[at], sems.at[0, block]),
            pltpu.make_async_copy(qkv_hbm.at[:, :, at], qkv_all.at[:, :, at], sems.at[1, block]),
            pltpu.make_async_copy(fir_hbm.at[at], fir_all.at[at], sems.at[2, block]),
        ]

    def store(block):
        at = pl.ds(block * (rows // 2), rows // 2)
        return pltpu.make_async_copy(packed_all.at[at], packed_hbm.at[at], sems.at[3, block])

    small = [
        pltpu.make_async_copy(source, target, sems.at[4, i])
        for i, (source, target) in enumerate(zip(small_hbm, small_all))
    ]
    for fetch in small:
        fetch.start()
    for block in (blocks - 1, *range(blocks - 1)):
        for fetch in fetches(block):
            fetch.start()
    for fetch in small:
        fetch.wait()
    taps, poles, residues, skip, finished = small_all

    def first_step(block):
        for fetch in fetches(block):
            fetch.wait()
        start = pl.multiple_of(block * rows, rows)
        qkv = qkv_all.at[:, :, pl.ds(start, rows)]
        fir = fir_all.at[pl.ds(start, rows)]
        state = state_all.at[pl.ds(start, rows)]
        at = lax.broadcasted_iota(jnp.int32, (rows, finished.shape[1]), 0) + block * rows
        own = at == lax.broadcasted_iota(jnp.int32, at.shape, 1)
        alive = [
            jnp.broadcast_to(
                1.0 - jnp.sum(jnp.where(own, finished[t : t + 1].astype(F32), 0.0), axis=1, keepdims=True),
                (rows, width),
            )
            for t in range(3)
        ]
        alive0 = alive[0]
        q0 = [qkv[0, j].astype(F32) for j in range(3)]
        l0 = [fir[:, j].astype(F32)[:, 0] for j in range(3)]
        l1 = [fir[:, j].astype(F32)[:, 1] for j in range(3)]
        f = [
            taps[j, 0:1] * q0[j] + taps[j, 1:2] * l0[j] + taps[j, 2:3] * l1[j]
            for j in range(3)
        ]
        product = f[1] * f[2]
        modes = []
        for r in range(rows):
            s = poles[...] * state[r] + product[r : r + 1]
            y_rows[r : r + 1] = jnp.sum(residues[...] * s, axis=0, keepdims=True)
            modes.append(s * alive0[r : r + 1])
        gated[pl.ds(block * rows, rows)] = (f[0] * (y_rows[...] + skip[...] * product)).astype(BF16)
        return qkv, q0, l0, alive, modes

    qkv, q0, l0, alive, modes = first_step(blocks - 1)
    alive0 = alive[0]
    for r in range(rows):
        stay_state[r] = modes[r]
    lag0, lag1 = [x * alive0 for x in q0], [x * alive0 for x in l0]
    for t in range(1, 4):
        q = [qkv[t, j].astype(F32) for j in range(3)]
        g = [
            taps[j, 0:1] * q[j] + taps[j, 1:2] * lag0[j] + taps[j, 2:3] * lag1[j]
            for j in range(3)
        ]
        prod = g[1] * g[2]
        live = alive[t] if t < 3 else None
        for r in range(rows):
            s = poles[...] * stay_state[r] + prod[r : r + 1]
            y_rows[r : r + 1] = jnp.sum(residues[...] * s, axis=0, keepdims=True)
            stay_state[r] = s * live[r : r + 1] if t < 3 else s
        gated[64 + t * rows : 80 + t * rows] = (
            g[0] * (y_rows[...] + skip[...] * prod)
        ).astype(BF16)
        if t < 3:
            lag0, lag1 = [x * live for x in q], [x * live for x in lag0]
    stay_store = pltpu.make_async_copy(stay_state, stay_hbm, sems.at[3, blocks - 1])
    stay_store.start()

    @pl.loop(0, blocks - 1)
    def _(block):
        qkv, q0, l0, alive, modes = first_step(block)
        alive0 = alive[0]
        packed = packed_all.at[pl.ds(pl.multiple_of(block * (rows // 2), rows // 2), rows // 2)]
        for pair in range(rows // 2):
            both = jnp.concatenate([modes[2 * pair], modes[2 * pair + 1]], axis=0)
            packed[pair, 0 : 2 * MODES] = both.astype(BF16)
        sent = [(x * alive0).astype(BF16) for x in q0 + l0]
        sent += [qkv[t, j] for t in range(1, 4) for j in range(3)]
        half = width // 2
        sent.append(jnp.concatenate([alive[1][:, :half], alive[2][:, :half]], axis=-1).astype(BF16))
        stacked = jnp.concatenate(sent, axis=0)
        n = KINDS * rows
        r = lax.broadcasted_iota(jnp.int32, (n, n), 0)
        c = lax.broadcasted_iota(jnp.int32, (n, n), 1)
        source = ((r >> 1) & 15) * rows + (r >> 5) * 2 + (r & 1)
        order = jnp.where(c == source, 1.0, 0.0).astype(BF16)
        moved = dot(order, stacked).reshape(rows // 2, 2 * KINDS, width)
        packed[:, 2 * MODES :] = moved.astype(BF16)
        store(block).start()

    gated_store = pltpu.make_async_copy(gated, gated_hbm, sems.at[5, 0])
    gated_store.start()
    stay_store.wait()
    for block in range(blocks - 1):
        store(block).wait()
    gated_store.wait()


def band_kernel(
    turns, got, taps, poles, residues, skip, far_weight, ride, sent_hbm, gated, first_right, first_left, *scratch
):
    lags, inputs, live, heads, products, y_rows, kinds, sent, sem = scratch
    groups, _, width = got.shape
    rows = 2 * groups

    n = 16 * KINDS
    r = lax.broadcasted_iota(jnp.int32, (n, n), 0)
    c = lax.broadcasted_iota(jnp.int32, (n, n), 1)
    source = ((r >> 1) & 7) * (2 * KINDS) + (r >> 4) * 2 + (r & 1)
    order = jnp.where(c == source, 1.0, 0.0).astype(BF16)
    for g in range(0, groups, 8):
        part = dot(order, got[g : g + 8, 2 * MODES :].reshape(n, width)).reshape(KINDS, 16, width)
        lags[:, 2 * g : 2 * g + 16] = part[:6]
        kinds[:, 2 * g : 2 * g + 16] = part[6:].astype(BF16)

    r = lax.broadcasted_iota(jnp.int32, (rows, rows), 0)
    c = lax.broadcasted_iota(jnp.int32, (rows, rows), 1)
    half = width // 2
    for t in range(3):
        turn = jnp.where(c == ((r + 2 * turns[t]) & (rows - 1)), 1.0, 0.0).astype(BF16)
        for j in range(3):
            inputs[t, j] = dot(turn, kinds[3 * t + j])
        if t < 2:
            live[t] = wide(dot(turn, kinds[9, :, t * half : (t + 1) * half]), width)

    @pl.loop(0, rows // 8)
    def _(i):
        at = pl.ds(pl.multiple_of(i * 8, 8), 8)
        lag0 = [lags[j, at] for j in range(3)]
        lag1 = [lags[3 + j, at] for j in range(3)]
        for t in range(3):
            q = [inputs[t, j, at] for j in range(3)]
            f = [
                taps[j, 0:1] * q[j] + taps[j, 1:2] * lag0[j] + taps[j, 2:3] * lag1[j]
                for j in range(3)
            ]
            heads[t, at] = f[0]
            products[t, at] = f[1] * f[2]
            if t < 2:
                on = live[t, at]
                lag0, lag1 = [x * on for x in q], [x * on for x in lag0]
                if t == 1:
                    for j in range(3):
                        lags[j, at] = lag0[j]

    shape = (groups * 16, 3 * rows)
    r = lax.broadcasted_iota(jnp.int32, shape, 0)
    c = lax.broadcasted_iota(jnp.int32, shape, 1)
    group = ((r >> 4) - turns[2] + groups) & (groups - 1)
    source = ((r & 15) >> 1) * rows + group * 2 + (r & 1)
    order = jnp.where((c == source) & ((r & 15) < 6), 1.0, 0.0).astype(BF16)
    last = lags[0:3].reshape(3 * rows, width).astype(BF16)
    sent[:, 2 * MODES :] = dot(order, last).reshape(groups, 16, width).astype(BF16)

    @pl.loop(0, groups)
    def _(g):
        final = []
        for side in range(2):
            row = pl.ds(g * 2 + side, 1)
            s = got[g, side * MODES : (side + 1) * MODES].astype(F32)
            for t in range(3):
                product = products[t, row]
                s = poles[...] * s + product
                y = jnp.sum(residues[...] * s, axis=0, keepdims=True)
                there = ((g + turns[t]) & (groups - 1)) * 2 + side
                y_rows[t, pl.ds(there, 1)] = heads[t, row] * (y + skip[...] * product)
                if t < 2:
                    s = s * live[t, row]
            final.append(s)
        end = (g + turns[2]) & (groups - 1)
        sent[end, 0 : 2 * MODES] = jnp.concatenate(final, axis=0).astype(BF16)

    store = pltpu.make_async_copy(sent, sent_hbm, sem)
    store.start()
    gated[...] = y_rows[...].reshape(3 * rows, width).astype(BF16)
    half = 3 * rows // 2
    for way, first in enumerate((first_right, first_left)):
        load = dot(gated[way * half : (way + 1) * half], far_weight[...])
        first[:half] = load.astype(BF16)
        first[half:] = ride[way]
    store.wait()


def products_kernel(place, gated, weight, part):
    part[0] = dot(gated[...], weight[...])


def products(place, gated, weight, aways):
    n = lax.axis_size("tensor")
    rows, width = gated.shape
    own_cols = weight.shape[1] // n
    assert aways == tuple((aways[0] - i // 2) * (1 - 2 * (i % 2)) for i in range(len(aways)))

    def column(i, place):
        return 0, (place[0] + n + (aways[0] - i // 2) * (1 - 2 * (i % 2))) % n

    part = pl.pallas_call(
        products_kernel,
        grid_spec=pltpu.PrefetchScalarGridSpec(
            num_scalar_prefetch=1,
            grid=(len(aways),),
            in_specs=[
                whole((rows, width)),
                pl.BlockSpec((width, own_cols), column),
            ],
            out_specs=pl.BlockSpec((1, rows, own_cols), lambda i, place: (i, 0, 0)),
        ),
        out_shape=jax.ShapeDtypeStruct((len(aways), rows, own_cols), F32),
        cost_estimate=pl.CostEstimate(
            flops=16 * rows * width * weight.shape[1], bytes_accessed=2 * weight.size, transcendentals=0
        ),
        compiler_params=pltpu.CompilerParams(vmem_limit_bytes=52 * 1024 * 1024),
        name="ring_products",
    )(place, gated, weight)
    return dict(zip(aways, part))


def finish_kernel(back_hbm, qkv_hbm, stay_hbm, finished, state_hbm, lagged_hbm, *rest):
    back_all, qkv_all, state_all, lagged_all, sems = rest
    rows, width = 16, qkv_hbm.shape[-1]
    blocks = qkv_hbm.shape[2] // rows
    n = rows // 2

    def qkv_fetch(block):
        at = pl.ds(block * rows, rows)
        return pltpu.make_async_copy(qkv_hbm.at[2:4, :, at], qkv_all.at[:, :, at], sems.at[0, block])

    def back_fetch(block):
        at = pl.ds(block * n, n)
        return pltpu.make_async_copy(back_hbm.at[at], back_all.at[at], sems.at[1, block])

    def stores(block):
        at = pl.ds(block * rows, rows)
        return [
            pltpu.make_async_copy(state_all.at[at], state_hbm.at[at], sems.at[2, block]),
            pltpu.make_async_copy(lagged_all.at[at], lagged_hbm.at[at], sems.at[3, block]),
        ]

    for block in range(blocks):
        qkv_fetch(block).start()
        if block < blocks - 1:
            back_fetch(block).start()
    last_at = pl.ds((blocks - 1) * rows, rows)
    stay = pltpu.make_async_copy(stay_hbm, state_all.at[last_at], sems.at[1, blocks - 1])
    stay.start()

    def put(block, j, last):
        at = pl.ds(pl.multiple_of(block * rows, rows), rows)
        both = [qkv_all[1, j, at].astype(F32)[:, None], last[:, None]]
        lagged_all[at, j] = jnp.concatenate(both, axis=1).astype(BF16)

    r = lax.broadcasted_iota(jnp.int32, (3 * rows, n * 16), 0)
    c = lax.broadcasted_iota(jnp.int32, (3 * rows, n * 16), 1)
    source = ((r & 15) >> 1) * 16 + (r >> 4) * 2 + (r & 1)
    order = jnp.where(c == source, 1.0, 0.0).astype(BF16)

    @pl.loop(0, blocks - 1)
    def _(block):
        qkv_fetch(block).wait()
        back_fetch(block).wait()
        back = back_all.at[pl.ds(pl.multiple_of(block * n, n), n)]
        for b in range(n):
            for side in range(2):
                part = back[b, side * MODES : (side + 1) * MODES].astype(F32)
                state_all[block * rows + 2 * b + side] = part
        last = dot(order, back[:, 2 * MODES :].reshape(n * 16, width))
        for j in range(3):
            put(block, j, last[j * rows : (j + 1) * rows])
        for store in stores(block):
            store.start()

    qkv_fetch(blocks - 1).wait()
    stay.wait()
    at = lax.broadcasted_iota(jnp.int32, (rows, finished.shape[1]), 0) + (blocks - 1) * rows
    own = at == lax.broadcasted_iota(jnp.int32, at.shape, 1)
    ended = jnp.where(own, finished[2:3].astype(F32), 0.0)
    alive = 1.0 - jnp.sum(ended, axis=1, keepdims=True)
    for j in range(3):
        put(blocks - 1, j, qkv_all[0, j, last_at].astype(F32) * alive)
    for store in stores(blocks - 1):
        store.start()
    for block in range(blocks):
        for store in stores(block):
            store.wait()


def whole(shape):
    return pl.BlockSpec(shape, lambda *_: (0,) * len(shape))


def swap(blocks):
    return lax.all_to_all(blocks, "dp", split_axis=0, concat_axis=0, tiled=True)


def pass_on(right, left):
    n = lax.axis_size("tensor")
    right = lax.ppermute(right, "tensor", [(i, (i + 1) % n) for i in range(n)])
    left = lax.ppermute(left, "tensor", [(i, (i - 1) % n) for i in range(n)])
    return right, left


def joined(made, away, right, left):
    ahead, behind = made[away], made[-away]
    half = right.shape[0]
    if half < ahead.shape[0]:
        ahead = ahead.at[:half].add(right.astype(F32))
        behind = behind.at[half:].add(left.astype(F32))
    else:
        ahead, behind = ahead + right.astype(F32), behind + left.astype(F32)
    return ahead.astype(BF16), behind.astype(BF16)


def row_scales(own, back):
    n = lax.axis_size("tensor")
    squares = jnp.concatenate([jnp.sum(x * x, axis=1) for x in own])

    def sent_on(x, away):
        return lax.ppermute(x, "tensor", [(i, (i + away) % n) for i in range(n)])

    below = squares + sent_on(squares, 1)
    three = below + sent_on(squares, -1)
    three, below, back = lax.optimization_barrier((three, below, back))
    squares = three + (sent_on(three, 3) + sent_on(below, -3))
    return lax.rsqrt(squares / (n * own[0].shape[1]) + 1e-05)[:, None], back


def per_device(
    qkv,
    fir_buffer,
    fir_taps,
    modal_state,
    poles,
    residues,
    skip,
    out_weight,
    norm_gain,
    finished,
    dest_group,
):
    groups = lax.axis_size("dp")
    own_group = lax.axis_index("dp")
    slots, width = modal_state.shape[0], modal_state.shape[2]
    moving = groups * CAP
    qkv_kinds = jnp.transpose(qkv, (0, 2, 1, 3))
    skip_row = skip[None]
    shifts = lax.dynamic_slice_in_dim(dest_group, own_group * CAP, 1, 1)[:, 0] - own_group + groups
    turns = jnp.cumsum(shifts).astype(jnp.int32) % groups

    packed, gated_home, stay_state = pl.pallas_call(
        home_kernel,
        in_specs=[pl.BlockSpec(memory_space=pl.ANY)] * 8,
        out_specs=[pl.BlockSpec(memory_space=pl.ANY)] * 3,
        out_shape=[
            jax.ShapeDtypeStruct((groups, 2 * MODES + 2 * KINDS, width), BF16),
            jax.ShapeDtypeStruct((slots + 48, width), BF16),
            jax.ShapeDtypeStruct((16, MODES, width), F32),
        ],
        scratch_shapes=[
            pltpu.VMEM(fir_taps.shape, F32),
            pltpu.VMEM(poles.shape, F32),
            pltpu.VMEM(residues.shape, F32),
            pltpu.VMEM(skip_row.shape, F32),
            pltpu.VMEM(finished.shape, jnp.int32),
            pltpu.VMEM((slots + 48, width), BF16),
            pltpu.VMEM((16, MODES, width), F32),
            pltpu.VMEM(qkv_kinds.shape, BF16),
            pltpu.VMEM(fir_buffer.shape, BF16),
            pltpu.VMEM(modal_state.shape, F32),
            pltpu.VMEM((groups, 2 * MODES + 2 * KINDS, width), BF16),
            pltpu.VMEM((16, width), F32),
            pltpu.SemaphoreType.DMA((6, slots // 16)),
        ],
        compiler_params=pltpu.CompilerParams(vmem_limit_bytes=56 * 1024 * 1024),
        name="home_rows",
    )(qkv_kinds, fir_buffer, modal_state, fir_taps, poles, residues, skip_row, finished)

    n, own_cols = lax.axis_size("tensor"), norm_gain.shape[0]
    gated_home, later_weight = lax.optimization_barrier((gated_home, out_weight))
    place = lax.axis_index("tensor").astype(jnp.int32)[None]
    far_place = (place[0] + n // 2) % n
    far_weight = lax.dynamic_slice_in_dim(later_weight, far_place * own_cols, own_cols, 1)
    got = swap(packed)
    far = dot(gated_home, far_weight).astype(BF16)
    half = far.shape[0] // 2
    right, left = pass_on(far[:half], far[half:])
    made = products(place, gated_home, out_weight, (3, -3, 2, -2))
    right, left = lax.optimization_barrier((right, left))
    right, left, gated_home = lax.optimization_barrier((*pass_on(*joined(made, 3, right, left)), gated_home))
    right, left = pass_on(*joined(made, 2, right, left))
    made = products(place, gated_home, out_weight, (1, -1, 0))
    right, left = lax.optimization_barrier((right, left))
    ride = jnp.stack(joined(made, 1, right, left))
    got, ride, own_home = lax.optimization_barrier((got, ride, made[0]))

    sent, gated_band, right, left = pl.pallas_call(
        band_kernel,
        in_specs=[
            pl.BlockSpec(memory_space=pltpu.SMEM),
        ]
        + [pl.BlockSpec(memory_space=pltpu.VMEM)] * 7,
        out_specs=[pl.BlockSpec(memory_space=pl.ANY)]
        + [pl.BlockSpec(memory_space=pltpu.VMEM)] * 3,
        out_shape=[
            jax.ShapeDtypeStruct((groups, 2 * MODES + 16, width), BF16),
            jax.ShapeDtypeStruct((3 * moving, width), BF16),
            jax.ShapeDtypeStruct((3 * moving // 2 + slots + 48, own_cols), BF16),
            jax.ShapeDtypeStruct((3 * moving // 2 + slots + 48, own_cols), BF16),
        ],
        scratch_shapes=[
            pltpu.VMEM((6, moving, width), F32),
            pltpu.VMEM((3, 3, moving, width), F32),
            pltpu.VMEM((2, moving, width), F32),
            pltpu.VMEM((3, moving, width), F32),
            pltpu.VMEM((3, moving, width), F32),
            pltpu.VMEM((3, moving, width), F32),
            pltpu.VMEM((KINDS - 6, moving, width), BF16),
            pltpu.VMEM((groups, 2 * MODES + 16, width), BF16),
            pltpu.SemaphoreType.DMA,
        ],
        compiler_params=pltpu.CompilerParams(vmem_limit_bytes=40 * 1024 * 1024),
        name="band_rows",
    )(turns, got, fir_taps, poles, residues, skip_row, far_weight, ride)

    half = 3 * moving // 2
    right, left = pass_on(right, left)
    made = products(place, gated_band, out_weight, (3, -3, 2, -2))
    right, left, gated_band, sent = lax.optimization_barrier((right, left, gated_band, sent))
    own_home = own_home + right[half:].astype(F32) + left[half:].astype(F32)
    right, left = pass_on(*joined(made, 3, right[:half], left[:half]))
    back = swap(sent)
    right, left, gated_band = lax.optimization_barrier((right, left, gated_band))
    right, left = pass_on(*joined(made, 2, right, left))
    made = products(place, gated_band, out_weight, (1, -1, 0))
    right, left = lax.optimization_barrier((right, left))
    right, left = pass_on(*joined(made, 1, right, left))
    right, left = lax.optimization_barrier((right, left))
    own_band = made[0] + right.astype(F32) + left.astype(F32)
    scales, back = row_scales([own_band, own_home], back)
    mixed_band = (own_band * scales[: 3 * moving] * norm_gain[None]).astype(BF16)
    mixed_band = jnp.transpose(mixed_band.reshape(3, groups, CAP, own_cols), (1, 0, 2, 3))
    back, mixed_band = lax.optimization_barrier((back, mixed_band))
    mixed_back = swap(mixed_band)
    final_state, final_lagged = pl.pallas_call(
        finish_kernel,
        in_specs=[pl.BlockSpec(memory_space=pl.ANY)] * 3 + [pl.BlockSpec(memory_space=pltpu.VMEM)],
        out_specs=[pl.BlockSpec(memory_space=pl.ANY)] * 2,
        out_shape=[
            jax.ShapeDtypeStruct(modal_state.shape, F32),
            jax.ShapeDtypeStruct(fir_buffer.shape, BF16),
        ],
        scratch_shapes=[
            pltpu.VMEM(back.shape, BF16),
            pltpu.VMEM((2, 3, slots, width), BF16),
            pltpu.VMEM(modal_state.shape, F32),
            pltpu.VMEM(fir_buffer.shape, BF16),
            pltpu.SemaphoreType.DMA((4, slots // 16)),
        ],
        compiler_params=pltpu.CompilerParams(vmem_limit_bytes=56 * 1024 * 1024),
        name="last_rows",
    )(back, qkv_kinds, stay_state, finished)

    mixed_later = jnp.transpose(mixed_back, (1, 0, 2, 3)).reshape(3, moving, own_cols)
    mixed_home = (own_home * scales[3 * moving :] * norm_gain[None]).astype(BF16)
    mixed_stay = mixed_home[slots:].reshape(3, 16, own_cols)
    mixed = jnp.concatenate(
        [mixed_home[None, :slots], jnp.concatenate([mixed_later, mixed_stay], axis=1)], axis=0
    )
    return (mixed, final_state, final_lagged)


def solution(mesh):
    return jax.shard_map(
        per_device,
        mesh=mesh,
        in_specs=(
            P(None, "dp", None, "tensor"),
            P("dp", None, None, "tensor"),
            P(None, None, "tensor"),
            P("dp", None, "tensor"),
            P(None, "tensor"),
            P(None, "tensor"),
            P("tensor"),
            P("tensor", None),
            P("tensor"),
            P(None, "dp"),
            P(None, "dp"),
        ),
        out_specs=(P(None, "dp", "tensor"), P("dp", None, "tensor"), P("dp", None, None, "tensor")),
        check_vma=False,
    )
```

```python
import jax
import jax.numpy as jnp
from jax import lax
from jax.experimental import pallas as pl
from jax.experimental.pallas import tpu as pltpu
from jax.sharding import PartitionSpec as P

CAP = 2
MODES = 16
KINDS = 16
F32, BF16 = jnp.float32, jnp.bfloat16


def dot(a, b):
    return jnp.dot(a, b, preferred_element_type=F32)


def wide(x, width):
    return jnp.concatenate([x] * (width // x.shape[-1]), axis=-1)


def home_kernel(qkv_hbm, fir_hbm, state_hbm, *rest):
    small_hbm, (packed_hbm, gated_hbm, stay_hbm), rest = rest[:5], rest[5:8], rest[8:]
    small_all, (gated, stay_state, qkv_all, fir_all, state_all, packed_all, y_rows, sems) = rest[:5], rest[5:]
    rows, width = 16, qkv_hbm.shape[-1]
    blocks = qkv_hbm.shape[2] // rows

    def fetches(block):
        at = pl.ds(block * rows, rows)
        return [
            pltpu.make_async_copy(state_hbm.at[at], state_all.at[at], sems.at[0, block]),
            pltpu.make_async_copy(qkv_hbm.at[:, :, at], qkv_all.at[:, :, at], sems.at[1, block]),
            pltpu.make_async_copy(fir_hbm.at[at], fir_all.at[at], sems.at[2, block]),
        ]

    def store(block):
        at = pl.ds(block * (rows // 2), rows // 2)
        return pltpu.make_async_copy(packed_all.at[at], packed_hbm.at[at], sems.at[3, block])

    small = [
        pltpu.make_async_copy(source, target, sems.at[4, i])
        for i, (source, target) in enumerate(zip(small_hbm, small_all))
    ]
    for fetch in small:
        fetch.start()
    for block in (blocks - 1, *range(blocks - 1)):
        for fetch in fetches(block):
            fetch.start()
    for fetch in small:
        fetch.wait()
    taps, poles, residues, skip, finished = small_all

    def first_step(block):
        for fetch in fetches(block):
            fetch.wait()
        start = pl.multiple_of(block * rows, rows)
        qkv = qkv_all.at[:, :, pl.ds(start, rows)]
        fir = fir_all.at[pl.ds(start, rows)]
        state = state_all.at[pl.ds(start, rows)]
        at = lax.broadcasted_iota(jnp.int32, (rows, finished.shape[1]), 0) + block * rows
        own = at == lax.broadcasted_iota(jnp.int32, at.shape, 1)
        alive = [
            jnp.broadcast_to(
                1.0 - jnp.sum(jnp.where(own, finished[t : t + 1].astype(F32), 0.0), axis=1, keepdims=True),
                (rows, width),
            )
            for t in range(3)
        ]
        alive0 = alive[0]
        q0 = [qkv[0, j].astype(F32) for j in range(3)]
        l0 = [fir[:, j].astype(F32)[:, 0] for j in range(3)]
        l1 = [fir[:, j].astype(F32)[:, 1] for j in range(3)]
        f = [
            taps[j, 0:1] * q0[j] + taps[j, 1:2] * l0[j] + taps[j, 2:3] * l1[j]
            for j in range(3)
        ]
        product = f[1] * f[2]
        modes = []
        for r in range(rows):
            s = poles[...] * state[r] + product[r : r + 1]
            y_rows[r : r + 1] = jnp.sum(residues[...] * s, axis=0, keepdims=True)
            modes.append(s * alive0[r : r + 1])
        gated[pl.ds(block * rows, rows)] = (f[0] * (y_rows[...] + skip[...] * product)).astype(BF16)
        return qkv, q0, l0, alive, modes

    qkv, q0, l0, alive, modes = first_step(blocks - 1)
    alive0 = alive[0]
    for r in range(rows):
        stay_state[r] = modes[r]
    lag0, lag1 = [x * alive0 for x in q0], [x * alive0 for x in l0]
    for t in range(1, 4):
        q = [qkv[t, j].astype(F32) for j in range(3)]
        g = [
            taps[j, 0:1] * q[j] + taps[j, 1:2] * lag0[j] + taps[j, 2:3] * lag1[j]
            for j in range(3)
        ]
        prod = g[1] * g[2]
        live = alive[t] if t < 3 else None
        for r in range(rows):
            s = poles[...] * stay_state[r] + prod[r : r + 1]
            y_rows[r : r + 1] = jnp.sum(residues[...] * s, axis=0, keepdims=True)
            stay_state[r] = s * live[r : r + 1] if t < 3 else s
        gated[64 + t * rows : 80 + t * rows] = (
            g[0] * (y_rows[...] + skip[...] * prod)
        ).astype(BF16)
        if t < 3:
            lag0, lag1 = [x * live for x in q], [x * live for x in lag0]
    stay_store = pltpu.make_async_copy(stay_state, stay_hbm, sems.at[3, blocks - 1])
    stay_store.start()

    @pl.loop(0, blocks - 1)
    def _(block):
        qkv, q0, l0, alive, modes = first_step(block)
        alive0 = alive[0]
        packed = packed_all.at[pl.ds(pl.multiple_of(block * (rows // 2), rows // 2), rows // 2)]
        for pair in range(rows // 2):
            both = jnp.concatenate([modes[2 * pair], modes[2 * pair + 1]], axis=0)
            packed[pair, 0 : 2 * MODES] = both.astype(BF16)
        sent = [(x * alive0).astype(BF16) for x in q0 + l0]
        sent += [qkv[t, j] for t in range(1, 4) for j in range(3)]
        half = width // 2
        sent.append(jnp.concatenate([alive[1][:, :half], alive[2][:, :half]], axis=-1).astype(BF16))
        stacked = jnp.concatenate(sent, axis=0)
        n = KINDS * rows
        r = lax.broadcasted_iota(jnp.int32, (n, n), 0)
        c = lax.broadcasted_iota(jnp.int32, (n, n), 1)
        source = ((r >> 1) & 15) * rows + (r >> 5) * 2 + (r & 1)
        order = jnp.where(c == source, 1.0, 0.0).astype(BF16)
        moved = dot(order, stacked).reshape(rows // 2, 2 * KINDS, width)
        packed[:, 2 * MODES :] = moved.astype(BF16)
        store(block).start()

    gated_store = pltpu.make_async_copy(gated, gated_hbm, sems.at[5, 0])
    gated_store.start()
    stay_store.wait()
    for block in range(blocks - 1):
        store(block).wait()
    gated_store.wait()


def band_kernel(
    turns, got, taps, poles, residues, skip, far_weight, ride, sent_hbm, gated, first_right, first_left, *scratch
):
    lags, inputs, live, heads, products, y_rows, kinds, sent, sem = scratch
    groups, _, width = got.shape
    rows = 2 * groups

    n = 16 * KINDS
    r = lax.broadcasted_iota(jnp.int32, (n, n), 0)
    c = lax.broadcasted_iota(jnp.int32, (n, n), 1)
    source = ((r >> 1) & 7) * (2 * KINDS) + (r >> 4) * 2 + (r & 1)
    order = jnp.where(c == source, 1.0, 0.0).astype(BF16)
    for g in range(0, groups, 8):
        part = dot(order, got[g : g + 8, 2 * MODES :].reshape(n, width)).reshape(KINDS, 16, width)
        lags[:, 2 * g : 2 * g + 16] = part[:6]
        kinds[:, 2 * g : 2 * g + 16] = part[6:].astype(BF16)

    r = lax.broadcasted_iota(jnp.int32, (rows, rows), 0)
    c = lax.broadcasted_iota(jnp.int32, (rows, rows), 1)
    half = width // 2
    for t in range(3):
        turn = jnp.where(c == ((r + 2 * turns[t]) & (rows - 1)), 1.0, 0.0).astype(BF16)
        for j in range(3):
            inputs[t, j] = dot(turn, kinds[3 * t + j])
        if t < 2:
            live[t] = wide(dot(turn, kinds[9, :, t * half : (t + 1) * half]), width)

    @pl.loop(0, rows // 8, unroll=2)
    def _(i):
        at = pl.ds(pl.multiple_of(i * 8, 8), 8)
        lag0 = [lags[j, at] for j in range(3)]
        lag1 = [lags[3 + j, at] for j in range(3)]
        for t in range(3):
            q = [inputs[t, j, at] for j in range(3)]
            f = [
                taps[j, 0:1] * q[j] + taps[j, 1:2] * lag0[j] + taps[j, 2:3] * lag1[j]
                for j in range(3)
            ]
            heads[t, at] = f[0]
            products[t, at] = f[1] * f[2]
            if t < 2:
                on = live[t, at]
                lag0, lag1 = [x * on for x in q], [x * on for x in lag0]
                if t == 1:
                    for j in range(3):
                        lags[j, at] = lag0[j]

    shape = (groups * 16, 3 * rows)
    r = lax.broadcasted_iota(jnp.int32, shape, 0)
    c = lax.broadcasted_iota(jnp.int32, shape, 1)
    group = ((r >> 4) - turns[2] + groups) & (groups - 1)
    source = ((r & 15) >> 1) * rows + group * 2 + (r & 1)
    order = jnp.where((c == source) & ((r & 15) < 6), 1.0, 0.0).astype(BF16)
    last = lags[0:3].reshape(3 * rows, width).astype(BF16)
    sent[:, 2 * MODES :] = dot(order, last).reshape(groups, 16, width).astype(BF16)

    @pl.loop(0, groups, unroll=2)
    def _(g):
        final = []
        for side in range(2):
            row = pl.ds(g * 2 + side, 1)
            s = got[g, side * MODES : (side + 1) * MODES].astype(F32)
            for t in range(3):
                product = products[t, row]
                s = poles[...] * s + product
                y = jnp.sum(residues[...] * s, axis=0, keepdims=True)
                there = ((g + turns[t]) & (groups - 1)) * 2 + side
                y_rows[t, pl.ds(there, 1)] = heads[t, row] * (y + skip[...] * product)
                if t < 2:
                    s = s * live[t, row]
            final.append(s)
        end = (g + turns[2]) & (groups - 1)
        sent[end, 0 : 2 * MODES] = jnp.concatenate(final, axis=0).astype(BF16)

    store = pltpu.make_async_copy(sent, sent_hbm, sem)
    store.start()
    gated[...] = y_rows[...].reshape(3 * rows, width).astype(BF16)
    half = 3 * rows // 2
    for way, first in enumerate((first_right, first_left)):
        load = dot(gated[way * half : (way + 1) * half], far_weight[...])
        first[:half] = load.astype(BF16)
        first[half:] = ride[way]
    store.wait()


def products_kernel(place, gated, weight, part):
    part[0] = dot(gated[...], weight[...])


def products(place, gated, weight, aways):
    n = lax.axis_size("tensor")
    rows, width = gated.shape
    own_cols = weight.shape[1] // n
    assert aways == tuple((aways[0] - i // 2) * (1 - 2 * (i % 2)) for i in range(len(aways)))

    def column(i, place):
        return 0, (place[0] + n + (aways[0] - i // 2) * (1 - 2 * (i % 2))) % n

    part = pl.pallas_call(
        products_kernel,
        grid_spec=pltpu.PrefetchScalarGridSpec(
            num_scalar_prefetch=1,
            grid=(len(aways),),
            in_specs=[
                whole((rows, width)),
                pl.BlockSpec((width, own_cols), column),
            ],
            out_specs=pl.BlockSpec((1, rows, own_cols), lambda i, place: (i, 0, 0)),
        ),
        out_shape=jax.ShapeDtypeStruct((len(aways), rows, own_cols), F32),
        cost_estimate=pl.CostEstimate(
            flops=16 * rows * width * weight.shape[1], bytes_accessed=2 * weight.size, transcendentals=0
        ),
        compiler_params=pltpu.CompilerParams(vmem_limit_bytes=52 * 1024 * 1024),
        name="ring_products",
    )(place, gated, weight)
    return dict(zip(aways, part))


def finish_kernel(back_hbm, qkv_hbm, stay_hbm, finished, state_hbm, lagged_hbm, *rest):
    back_all, qkv_all, state_all, lagged_all, sems = rest
    rows, width = 16, qkv_hbm.shape[-1]
    blocks = qkv_hbm.shape[2] // rows
    n = rows // 2

    def qkv_fetch(block):
        at = pl.ds(block * rows, rows)
        return pltpu.make_async_copy(qkv_hbm.at[2:4, :, at], qkv_all.at[:, :, at], sems.at[0, block])

    def back_fetch(block):
        at = pl.ds(block * n, n)
        return pltpu.make_async_copy(back_hbm.at[at], back_all.at[at], sems.at[1, block])

    def stores(block):
        at = pl.ds(block * rows, rows)
        return [
            pltpu.make_async_copy(state_all.at[at], state_hbm.at[at], sems.at[2, block]),
            pltpu.make_async_copy(lagged_all.at[at], lagged_hbm.at[at], sems.at[3, block]),
        ]

    for block in range(blocks):
        qkv_fetch(block).start()
        if block < blocks - 1:
            back_fetch(block).start()
    last_at = pl.ds((blocks - 1) * rows, rows)
    stay = pltpu.make_async_copy(stay_hbm, state_all.at[last_at], sems.at[1, blocks - 1])
    stay.start()

    def put(block, j, last):
        at = pl.ds(pl.multiple_of(block * rows, rows), rows)
        both = [qkv_all[1, j, at].astype(F32)[:, None], last[:, None]]
        lagged_all[at, j] = jnp.concatenate(both, axis=1).astype(BF16)

    r = lax.broadcasted_iota(jnp.int32, (3 * rows, n * 16), 0)
    c = lax.broadcasted_iota(jnp.int32, (3 * rows, n * 16), 1)
    source = ((r & 15) >> 1) * 16 + (r >> 4) * 2 + (r & 1)
    order = jnp.where(c == source, 1.0, 0.0).astype(BF16)

    @pl.loop(0, blocks - 1)
    def _(block):
        qkv_fetch(block).wait()
        back_fetch(block).wait()
        back = back_all.at[pl.ds(pl.multiple_of(block * n, n), n)]
        for b in range(n):
            for side in range(2):
                part = back[b, side * MODES : (side + 1) * MODES].astype(F32)
                state_all[block * rows + 2 * b + side] = part
        last = dot(order, back[:, 2 * MODES :].reshape(n * 16, width))
        for j in range(3):
            put(block, j, last[j * rows : (j + 1) * rows])
        for store in stores(block):
            store.start()

    qkv_fetch(blocks - 1).wait()
    stay.wait()
    at = lax.broadcasted_iota(jnp.int32, (rows, finished.shape[1]), 0) + (blocks - 1) * rows
    own = at == lax.broadcasted_iota(jnp.int32, at.shape, 1)
    ended = jnp.where(own, finished[2:3].astype(F32), 0.0)
    alive = 1.0 - jnp.sum(ended, axis=1, keepdims=True)
    for j in range(3):
        put(blocks - 1, j, qkv_all[0, j, last_at].astype(F32) * alive)
    for store in stores(blocks - 1):
        store.start()
    for block in range(blocks):
        for store in stores(block):
            store.wait()


def whole(shape):
    return pl.BlockSpec(shape, lambda *_: (0,) * len(shape))


def swap(blocks):
    return lax.all_to_all(blocks, "dp", split_axis=0, concat_axis=0, tiled=True)


def pass_on(right, left):
    n = lax.axis_size("tensor")
    right = lax.ppermute(right, "tensor", [(i, (i + 1) % n) for i in range(n)])
    left = lax.ppermute(left, "tensor", [(i, (i - 1) % n) for i in range(n)])
    return right, left


def joined(made, away, right, left):
    ahead, behind = made[away], made[-away]
    half = right.shape[0]
    if half < ahead.shape[0]:
        ahead = ahead.at[:half].add(right.astype(F32))
        behind = behind.at[half:].add(left.astype(F32))
    else:
        ahead, behind = ahead + right.astype(F32), behind + left.astype(F32)
    return ahead.astype(BF16), behind.astype(BF16)


def row_scales(own, back):
    n = lax.axis_size("tensor")
    squares = jnp.concatenate([jnp.sum(x * x, axis=1) for x in own])

    def sent_on(x, away):
        return lax.ppermute(x, "tensor", [(i, (i + away) % n) for i in range(n)])

    below = squares + sent_on(squares, 1)
    three = below + sent_on(squares, -1)
    three, below, back = lax.optimization_barrier((three, below, back))
    squares = three + (sent_on(three, 3) + sent_on(below, -3))
    return lax.rsqrt(squares / (n * own[0].shape[1]) + 1e-05)[:, None], back


def per_device(
    qkv,
    fir_buffer,
    fir_taps,
    modal_state,
    poles,
    residues,
    skip,
    out_weight,
    norm_gain,
    finished,
    dest_group,
):
    groups = lax.axis_size("dp")
    own_group = lax.axis_index("dp")
    slots, width = modal_state.shape[0], modal_state.shape[2]
    moving = groups * CAP
    qkv_kinds = jnp.transpose(qkv, (0, 2, 1, 3))
    skip_row = skip[None]
    shifts = lax.dynamic_slice_in_dim(dest_group, own_group * CAP, 1, 1)[:, 0] - own_group + groups
    turns = jnp.cumsum(shifts).astype(jnp.int32) % groups

    packed, gated_home, stay_state = pl.pallas_call(
        home_kernel,
        in_specs=[pl.BlockSpec(memory_space=pl.ANY)] * 8,
        out_specs=[pl.BlockSpec(memory_space=pl.ANY)] * 3,
        out_shape=[
            jax.ShapeDtypeStruct((groups, 2 * MODES + 2 * KINDS, width), BF16),
            jax.ShapeDtypeStruct((slots + 48, width), BF16),
            jax.ShapeDtypeStruct((16, MODES, width), F32),
        ],
        scratch_shapes=[
            pltpu.VMEM(fir_taps.shape, F32),
            pltpu.VMEM(poles.shape, F32),
            pltpu.VMEM(residues.shape, F32),
            pltpu.VMEM(skip_row.shape, F32),
            pltpu.VMEM(finished.shape, jnp.int32),
            pltpu.VMEM((slots + 48, width), BF16),
            pltpu.VMEM((16, MODES, width), F32),
            pltpu.VMEM(qkv_kinds.shape, BF16),
            pltpu.VMEM(fir_buffer.shape, BF16),
            pltpu.VMEM(modal_state.shape, F32),
            pltpu.VMEM((groups, 2 * MODES + 2 * KINDS, width), BF16),
            pltpu.VMEM((16, width), F32),
            pltpu.SemaphoreType.DMA((6, slots // 16)),
        ],
        compiler_params=pltpu.CompilerParams(vmem_limit_bytes=56 * 1024 * 1024),
        name="home_rows",
    )(qkv_kinds, fir_buffer, modal_state, fir_taps, poles, residues, skip_row, finished)

    n, own_cols = lax.axis_size("tensor"), norm_gain.shape[0]
    gated_home, later_weight = lax.optimization_barrier((gated_home, out_weight))
    place = lax.axis_index("tensor").astype(jnp.int32)[None]
    far_place = (place[0] + n // 2) % n
    far_weight = lax.dynamic_slice_in_dim(later_weight, far_place * own_cols, own_cols, 1)
    got = swap(packed)
    far = dot(gated_home, far_weight).astype(BF16)
    half = far.shape[0] // 2
    right, left = pass_on(far[:half], far[half:])
    made = products(place, gated_home, out_weight, (3, -3, 2, -2))
    right, left = lax.optimization_barrier((right, left))
    right, left, gated_home = lax.optimization_barrier((*pass_on(*joined(made, 3, right, left)), gated_home))
    right, left = pass_on(*joined(made, 2, right, left))
    made = products(place, gated_home, out_weight, (1, -1, 0))
    right, left = lax.optimization_barrier((right, left))
    ride = jnp.stack(joined(made, 1, right, left))
    got, ride, own_home = lax.optimization_barrier((got, ride, made[0]))

    sent, gated_band, right, left = pl.pallas_call(
        band_kernel,
        in_specs=[
            pl.BlockSpec(memory_space=pltpu.SMEM),
        ]
        + [pl.BlockSpec(memory_space=pltpu.VMEM)] * 7,
        out_specs=[pl.BlockSpec(memory_space=pl.ANY)]
        + [pl.BlockSpec(memory_space=pltpu.VMEM)] * 3,
        out_shape=[
            jax.ShapeDtypeStruct((groups, 2 * MODES + 16, width), BF16),
            jax.ShapeDtypeStruct((3 * moving, width), BF16),
            jax.ShapeDtypeStruct((3 * moving // 2 + slots + 48, own_cols), BF16),
            jax.ShapeDtypeStruct((3 * moving // 2 + slots + 48, own_cols), BF16),
        ],
        scratch_shapes=[
            pltpu.VMEM((6, moving, width), F32),
            pltpu.VMEM((3, 3, moving, width), F32),
            pltpu.VMEM((2, moving, width), F32),
            pltpu.VMEM((3, moving, width), F32),
            pltpu.VMEM((3, moving, width), F32),
            pltpu.VMEM((3, moving, width), F32),
            pltpu.VMEM((KINDS - 6, moving, width), BF16),
            pltpu.VMEM((groups, 2 * MODES + 16, width), BF16),
            pltpu.SemaphoreType.DMA,
        ],
        compiler_params=pltpu.CompilerParams(vmem_limit_bytes=40 * 1024 * 1024),
        name="band_rows",
    )(turns, got, fir_taps, poles, residues, skip_row, far_weight, ride)

    half = 3 * moving // 2
    right, left = pass_on(right, left)
    made = products(place, gated_band, out_weight, (3, -3, 2, -2))
    right, left, gated_band, sent = lax.optimization_barrier((right, left, gated_band, sent))
    own_home = own_home + right[half:].astype(F32) + left[half:].astype(F32)
    right, left = pass_on(*joined(made, 3, right[:half], left[:half]))
    back = swap(sent)
    right, left, gated_band = lax.optimization_barrier((right, left, gated_band))
    right, left = pass_on(*joined(made, 2, right, left))
    made = products(place, gated_band, out_weight, (1, -1, 0))
    right, left = lax.optimization_barrier((right, left))
    right, left = pass_on(*joined(made, 1, right, left))
    right, left = lax.optimization_barrier((right, left))
    own_band = made[0] + right.astype(F32) + left.astype(F32)
    scales, back = row_scales([own_band, own_home], back)
    mixed_band = (own_band * scales[: 3 * moving] * norm_gain[None]).astype(BF16)
    mixed_band = jnp.transpose(mixed_band.reshape(3, groups, CAP, own_cols), (1, 0, 2, 3))
    back, mixed_band = lax.optimization_barrier((back, mixed_band))
    mixed_back = swap(mixed_band)
    final_state, final_lagged = pl.pallas_call(
        finish_kernel,
        in_specs=[pl.BlockSpec(memory_space=pl.ANY)] * 3 + [pl.BlockSpec(memory_space=pltpu.VMEM)],
        out_specs=[pl.BlockSpec(memory_space=pl.ANY)] * 2,
        out_shape=[
            jax.ShapeDtypeStruct(modal_state.shape, F32),
            jax.ShapeDtypeStruct(fir_buffer.shape, BF16),
        ],
        scratch_shapes=[
            pltpu.VMEM(back.shape, BF16),
            pltpu.VMEM((2, 3, slots, width), BF16),
            pltpu.VMEM(modal_state.shape, F32),
            pltpu.VMEM(fir_buffer.shape, BF16),
            pltpu.SemaphoreType.DMA((4, slots // 16)),
        ],
        compiler_params=pltpu.CompilerParams(vmem_limit_bytes=56 * 1024 * 1024),
        name="last_rows",
    )(back, qkv_kinds, stay_state, finished)

    mixed_later = jnp.transpose(mixed_back, (1, 0, 2, 3)).reshape(3, moving, own_cols)
    mixed_home = (own_home * scales[3 * moving :] * norm_gain[None]).astype(BF16)
    mixed_stay = mixed_home[slots:].reshape(3, 16, own_cols)
    mixed = jnp.concatenate(
        [mixed_home[None, :slots], jnp.concatenate([mixed_later, mixed_stay], axis=1)], axis=0
    )
    return (mixed, final_state, final_lagged)


def solution(mesh):
    return jax.shard_map(
        per_device,
        mesh=mesh,
        in_specs=(
            P(None, "dp", None, "tensor"),
            P("dp", None, None, "tensor"),
            P(None, None, "tensor"),
            P("dp", None, "tensor"),
            P(None, "tensor"),
            P(None, "tensor"),
            P("tensor"),
            P("tensor", None),
            P("tensor"),
            P(None, "dp"),
            P(None, "dp"),
        ),
        out_specs=(P(None, "dp", "tensor"), P("dp", None, "tensor"), P("dp", None, None, "tensor")),
        check_vma=False,
    )
```

```python
import jax
import jax.numpy as jnp
from jax import lax
from jax.experimental import pallas as pl
from jax.experimental.pallas import tpu as pltpu
from jax.sharding import PartitionSpec as P

CAP = 2
MODES = 16
KINDS = 16
F32, BF16 = jnp.float32, jnp.bfloat16


def dot(a, b):
    return jnp.dot(a, b, preferred_element_type=F32)


def wide(x, width):
    return jnp.concatenate([x] * (width // x.shape[-1]), axis=-1)


def home_kernel(qkv_hbm, fir_hbm, state_hbm, *rest):
    small_hbm, (packed_hbm, gated_hbm, stay_hbm), rest = rest[:5], rest[5:8], rest[8:]
    small_all, (gated, stay_state, qkv_all, fir_all, state_all, packed_all, y_rows, sems) = rest[:5], rest[5:]
    rows, width = 16, qkv_hbm.shape[-1]
    blocks = qkv_hbm.shape[2] // rows

    def fetches(block):
        at = pl.ds(block * rows, rows)
        return [
            pltpu.make_async_copy(state_hbm.at[at], state_all.at[at], sems.at[0, block]),
            pltpu.make_async_copy(qkv_hbm.at[:, :, at], qkv_all.at[:, :, at], sems.at[1, block]),
            pltpu.make_async_copy(fir_hbm.at[at], fir_all.at[at], sems.at[2, block]),
        ]

    def store(block):
        at = pl.ds(block * (rows // 2), rows // 2)
        return pltpu.make_async_copy(packed_all.at[at], packed_hbm.at[at], sems.at[3, block])

    small = [
        pltpu.make_async_copy(source, target, sems.at[4, i])
        for i, (source, target) in enumerate(zip(small_hbm, small_all))
    ]
    for fetch in small:
        fetch.start()
    for block in (blocks - 1, *range(blocks - 1)):
        for fetch in fetches(block):
            fetch.start()
    for fetch in small:
        fetch.wait()
    taps, poles, residues, skip, finished = small_all

    def first_step(block):
        for fetch in fetches(block):
            fetch.wait()
        start = pl.multiple_of(block * rows, rows)
        qkv = qkv_all.at[:, :, pl.ds(start, rows)]
        fir = fir_all.at[pl.ds(start, rows)]
        state = state_all.at[pl.ds(start, rows)]
        at = lax.broadcasted_iota(jnp.int32, (rows, finished.shape[1]), 0) + block * rows
        own = at == lax.broadcasted_iota(jnp.int32, at.shape, 1)
        alive = [
            jnp.broadcast_to(
                1.0 - jnp.sum(jnp.where(own, finished[t : t + 1].astype(F32), 0.0), axis=1, keepdims=True),
                (rows, width),
            )
            for t in range(3)
        ]
        alive0 = alive[0]
        q0 = [qkv[0, j].astype(F32) for j in range(3)]
        l0 = [fir[:, j].astype(F32)[:, 0] for j in range(3)]
        l1 = [fir[:, j].astype(F32)[:, 1] for j in range(3)]
        f = [
            taps[j, 0:1] * q0[j] + taps[j, 1:2] * l0[j] + taps[j, 2:3] * l1[j]
            for j in range(3)
        ]
        product = f[1] * f[2]
        modes = []
        for r in range(rows):
            s = poles[...] * state[r] + product[r : r + 1]
            y_rows[r : r + 1] = jnp.sum(residues[...] * s, axis=0, keepdims=True)
            modes.append(s * alive0[r : r + 1])
        gated[pl.ds(block * rows, rows)] = (f[0] * (y_rows[...] + skip[...] * product)).astype(BF16)
        return qkv, q0, l0, alive, modes

    qkv, q0, l0, alive, modes = first_step(blocks - 1)
    alive0 = alive[0]
    for r in range(rows):
        stay_state[r] = modes[r]
    lag0, lag1 = [x * alive0 for x in q0], [x * alive0 for x in l0]
    for t in range(1, 4):
        q = [qkv[t, j].astype(F32) for j in range(3)]
        g = [
            taps[j, 0:1] * q[j] + taps[j, 1:2] * lag0[j] + taps[j, 2:3] * lag1[j]
            for j in range(3)
        ]
        prod = g[1] * g[2]
        live = alive[t] if t < 3 else None
        for r in range(rows):
            s = poles[...] * stay_state[r] + prod[r : r + 1]
            y_rows[r : r + 1] = jnp.sum(residues[...] * s, axis=0, keepdims=True)
            stay_state[r] = s * live[r : r + 1] if t < 3 else s
        gated[64 + t * rows : 80 + t * rows] = (
            g[0] * (y_rows[...] + skip[...] * prod)
        ).astype(BF16)
        if t < 3:
            lag0, lag1 = [x * live for x in q], [x * live for x in lag0]
    stay_store = pltpu.make_async_copy(stay_state, stay_hbm, sems.at[3, blocks - 1])
    stay_store.start()

    @pl.loop(0, blocks - 1)
    def _(block):
        qkv, q0, l0, alive, modes = first_step(block)
        alive0 = alive[0]
        packed = packed_all.at[pl.ds(pl.multiple_of(block * (rows // 2), rows // 2), rows // 2)]
        for pair in range(rows // 2):
            both = jnp.concatenate([modes[2 * pair], modes[2 * pair + 1]], axis=0)
            packed[pair, 0 : 2 * MODES] = both.astype(BF16)
        sent = [(x * alive0).astype(BF16) for x in q0 + l0]
        sent += [qkv[t, j] for t in range(1, 4) for j in range(3)]
        half = width // 2
        sent.append(jnp.concatenate([alive[1][:, :half], alive[2][:, :half]], axis=-1).astype(BF16))
        stacked = jnp.concatenate(sent, axis=0)
        n = KINDS * rows
        r = lax.broadcasted_iota(jnp.int32, (n, n), 0)
        c = lax.broadcasted_iota(jnp.int32, (n, n), 1)
        source = ((r >> 1) & 15) * rows + (r >> 5) * 2 + (r & 1)
        order = jnp.where(c == source, 1.0, 0.0).astype(BF16)
        moved = dot(order, stacked).reshape(rows // 2, 2 * KINDS, width)
        packed[:, 2 * MODES :] = moved.astype(BF16)
        store(block).start()

    gated_store = pltpu.make_async_copy(gated, gated_hbm, sems.at[5, 0])
    gated_store.start()
    stay_store.wait()
    for block in range(blocks - 1):
        store(block).wait()
    gated_store.wait()


def band_kernel(
    turns, got, taps, poles, residues, skip, far_weight, ride, sent_hbm, gated, first_right, first_left, *scratch
):
    lags, inputs, live, heads, products, y_rows, kinds, sent, sem = scratch
    groups, _, width = got.shape
    rows = 2 * groups

    n = 16 * KINDS
    r = lax.broadcasted_iota(jnp.int32, (n, n), 0)
    c = lax.broadcasted_iota(jnp.int32, (n, n), 1)
    source = ((r >> 1) & 7) * (2 * KINDS) + (r >> 4) * 2 + (r & 1)
    order = jnp.where(c == source, 1.0, 0.0).astype(BF16)
    for g in range(0, groups, 8):
        part = dot(order, got[g : g + 8, 2 * MODES :].reshape(n, width)).reshape(KINDS, 16, width)
        lags[:, 2 * g : 2 * g + 16] = part[:6]
        kinds[:, 2 * g : 2 * g + 16] = part[6:].astype(BF16)

    r = lax.broadcasted_iota(jnp.int32, (rows, rows), 0)
    c = lax.broadcasted_iota(jnp.int32, (rows, rows), 1)
    half = width // 2
    for t in range(3):
        turn = jnp.where(c == ((r + 2 * turns[t]) & (rows - 1)), 1.0, 0.0).astype(BF16)
        for j in range(3):
            inputs[t, j] = dot(turn, kinds[3 * t + j])
        if t < 2:
            live[t] = wide(dot(turn, kinds[9, :, t * half : (t + 1) * half]), width)

    @pl.loop(0, rows // 8, unroll=2)
    def _(i):
        at = pl.ds(pl.multiple_of(i * 8, 8), 8)
        lag0 = [lags[j, at] for j in range(3)]
        lag1 = [lags[3 + j, at] for j in range(3)]
        for t in range(3):
            q = [inputs[t, j, at] for j in range(3)]
            f = [
                taps[j, 0:1] * q[j] + taps[j, 1:2] * lag0[j] + taps[j, 2:3] * lag1[j]
                for j in range(3)
            ]
            heads[t, at] = f[0]
            products[t, at] = f[1] * f[2]
            if t < 2:
                on = live[t, at]
                lag0, lag1 = [x * on for x in q], [x * on for x in lag0]
                if t == 1:
                    for j in range(3):
                        lags[j, at] = lag0[j]

    shape = (groups * 16, 3 * rows)
    r = lax.broadcasted_iota(jnp.int32, shape, 0)
    c = lax.broadcasted_iota(jnp.int32, shape, 1)
    group = ((r >> 4) - turns[2] + groups) & (groups - 1)
    source = ((r & 15) >> 1) * rows + group * 2 + (r & 1)
    order = jnp.where((c == source) & ((r & 15) < 6), 1.0, 0.0).astype(BF16)
    last = lags[0:3].reshape(3 * rows, width).astype(BF16)
    sent[:, 2 * MODES :] = dot(order, last).reshape(groups, 16, width).astype(BF16)

    @pl.loop(0, groups, unroll=2)
    def _(g):
        final = []
        for side in range(2):
            row = pl.ds(g * 2 + side, 1)
            s = got[g, side * MODES : (side + 1) * MODES].astype(F32)
            for t in range(3):
                product = products[t, row]
                s = poles[...] * s + product
                y = jnp.sum(residues[...] * s, axis=0, keepdims=True)
                there = ((g + turns[t]) & (groups - 1)) * 2 + side
                y_rows[t, pl.ds(there, 1)] = heads[t, row] * (y + skip[...] * product)
                if t < 2:
                    s = s * live[t, row]
            final.append(s)
        end = (g + turns[2]) & (groups - 1)
        sent[end, 0 : 2 * MODES] = jnp.concatenate(final, axis=0).astype(BF16)

    store = pltpu.make_async_copy(sent, sent_hbm, sem)
    store.start()
    gated[...] = y_rows[...].reshape(3 * rows, width).astype(BF16)
    half = 3 * rows // 2
    for way, first in enumerate((first_right, first_left)):
        load = dot(gated[way * half : (way + 1) * half], far_weight[...])
        first[:half] = load.astype(BF16)
        first[half:] = ride[way]
    store.wait()


def products_kernel(place, gated, weight, part):
    part[0] = dot(gated[...], weight[...])


def products(place, gated, weight, aways):
    n = lax.axis_size("tensor")
    rows, width = gated.shape
    own_cols = weight.shape[1] // n
    assert aways == tuple((aways[0] - i // 2) * (1 - 2 * (i % 2)) for i in range(len(aways)))

    def column(i, place):
        return 0, (place[0] + n + (aways[0] - i // 2) * (1 - 2 * (i % 2))) % n

    part = pl.pallas_call(
        products_kernel,
        grid_spec=pltpu.PrefetchScalarGridSpec(
            num_scalar_prefetch=1,
            grid=(len(aways),),
            in_specs=[
                whole((rows, width)),
                pl.BlockSpec((width, own_cols), column),
            ],
            out_specs=pl.BlockSpec((1, rows, own_cols), lambda i, place: (i, 0, 0)),
        ),
        out_shape=jax.ShapeDtypeStruct((len(aways), rows, own_cols), F32),
        cost_estimate=pl.CostEstimate(
            flops=16 * rows * width * weight.shape[1], bytes_accessed=2 * weight.size, transcendentals=0
        ),
        compiler_params=pltpu.CompilerParams(vmem_limit_bytes=52 * 1024 * 1024),
        name="ring_products",
    )(place, gated, weight)
    return dict(zip(aways, part))


def finish_kernel(back_hbm, qkv_hbm, stay_hbm, finished, state_hbm, lagged_hbm, *rest):
    back_all, qkv_all, state_all, lagged_all, sems = rest
    rows, width = 16, qkv_hbm.shape[-1]
    blocks = qkv_hbm.shape[2] // rows
    n = rows // 2

    def qkv_fetch(block):
        at = pl.ds(block * rows, rows)
        return pltpu.make_async_copy(qkv_hbm.at[2:4, :, at], qkv_all.at[:, :, at], sems.at[0, block])

    def back_fetch(block):
        at = pl.ds(block * n, n)
        return pltpu.make_async_copy(back_hbm.at[at], back_all.at[at], sems.at[1, block])

    def stores(block):
        at = pl.ds(block * rows, rows)
        return [
            pltpu.make_async_copy(state_all.at[at], state_hbm.at[at], sems.at[2, block]),
            pltpu.make_async_copy(lagged_all.at[at], lagged_hbm.at[at], sems.at[3, block]),
        ]

    for block in range(blocks):
        qkv_fetch(block).start()
        if block < blocks - 1:
            back_fetch(block).start()
    last_at = pl.ds((blocks - 1) * rows, rows)
    stay = pltpu.make_async_copy(stay_hbm, state_all.at[last_at], sems.at[1, blocks - 1])
    stay.start()

    def put(block, j, last):
        at = pl.ds(pl.multiple_of(block * rows, rows), rows)
        both = [qkv_all[1, j, at].astype(F32)[:, None], last[:, None]]
        lagged_all[at, j] = jnp.concatenate(both, axis=1).astype(BF16)

    r = lax.broadcasted_iota(jnp.int32, (3 * rows, n * 16), 0)
    c = lax.broadcasted_iota(jnp.int32, (3 * rows, n * 16), 1)
    source = ((r & 15) >> 1) * 16 + (r >> 4) * 2 + (r & 1)
    order = jnp.where(c == source, 1.0, 0.0).astype(BF16)

    @pl.loop(0, blocks - 1)
    def _(block):
        qkv_fetch(block).wait()
        back_fetch(block).wait()
        back = back_all.at[pl.ds(pl.multiple_of(block * n, n), n)]
        for b in range(n):
            for side in range(2):
                part = back[b, side * MODES : (side + 1) * MODES].astype(F32)
                state_all[block * rows + 2 * b + side] = part
        last = dot(order, back[:, 2 * MODES :].reshape(n * 16, width))
        for j in range(3):
            put(block, j, last[j * rows : (j + 1) * rows])
        for store in stores(block):
            store.start()

    qkv_fetch(blocks - 1).wait()
    stay.wait()
    at = lax.broadcasted_iota(jnp.int32, (rows, finished.shape[1]), 0) + (blocks - 1) * rows
    own = at == lax.broadcasted_iota(jnp.int32, at.shape, 1)
    ended = jnp.where(own, finished[2:3].astype(F32), 0.0)
    alive = 1.0 - jnp.sum(ended, axis=1, keepdims=True)
    for j in range(3):
        put(blocks - 1, j, qkv_all[0, j, last_at].astype(F32) * alive)
    for store in stores(blocks - 1):
        store.start()
    for block in range(blocks):
        for store in stores(block):
            store.wait()


def whole(shape):
    return pl.BlockSpec(shape, lambda *_: (0,) * len(shape))


def swap(blocks):
    return lax.all_to_all(blocks, "dp", split_axis=0, concat_axis=0, tiled=True)


def pass_on(right, left):
    n = lax.axis_size("tensor")
    right = lax.ppermute(right, "tensor", [(i, (i + 1) % n) for i in range(n)])
    left = lax.ppermute(left, "tensor", [(i, (i - 1) % n) for i in range(n)])
    return right, left


def joined(made, away, right, left):
    ahead, behind = made[away], made[-away]
    half = right.shape[0]
    if half < ahead.shape[0]:
        ahead = ahead.at[:half].add(right.astype(F32))
        behind = behind.at[half:].add(left.astype(F32))
    else:
        ahead, behind = ahead + right.astype(F32), behind + left.astype(F32)
    return ahead.astype(BF16), behind.astype(BF16)


def row_scales(own, back):
    n = lax.axis_size("tensor")
    squares = jnp.concatenate([jnp.sum(x * x, axis=1) for x in own])

    def sent_on(x, away):
        return lax.ppermute(x, "tensor", [(i, (i + away) % n) for i in range(n)])

    four = squares + (sent_on(squares, 1) + sent_on(squares, -1)) + sent_on(squares, 2)
    four, back = lax.optimization_barrier((four, back))
    squares = sent_on(four, 2) + sent_on(four, -2)
    return lax.rsqrt(squares / (n * own[0].shape[1]) + 1e-05)[:, None], back


def per_device(
    qkv,
    fir_buffer,
    fir_taps,
    modal_state,
    poles,
    residues,
    skip,
    out_weight,
    norm_gain,
    finished,
    dest_group,
):
    groups = lax.axis_size("dp")
    own_group = lax.axis_index("dp")
    slots, width = modal_state.shape[0], modal_state.shape[2]
    moving = groups * CAP
    qkv_kinds = jnp.transpose(qkv, (0, 2, 1, 3))
    skip_row = skip[None]
    shifts = lax.dynamic_slice_in_dim(dest_group, own_group * CAP, 1, 1)[:, 0] - own_group + groups
    turns = jnp.cumsum(shifts).astype(jnp.int32) % groups

    packed, gated_home, stay_state = pl.pallas_call(
        home_kernel,
        in_specs=[pl.BlockSpec(memory_space=pl.ANY)] * 8,
        out_specs=[pl.BlockSpec(memory_space=pl.ANY)] * 3,
        out_shape=[
            jax.ShapeDtypeStruct((groups, 2 * MODES + 2 * KINDS, width), BF16),
            jax.ShapeDtypeStruct((slots + 48, width), BF16),
            jax.ShapeDtypeStruct((16, MODES, width), F32),
        ],
        scratch_shapes=[
            pltpu.VMEM(fir_taps.shape, F32),
            pltpu.VMEM(poles.shape, F32),
            pltpu.VMEM(residues.shape, F32),
            pltpu.VMEM(skip_row.shape, F32),
            pltpu.VMEM(finished.shape, jnp.int32),
            pltpu.VMEM((slots + 48, width), BF16),
            pltpu.VMEM((16, MODES, width), F32),
            pltpu.VMEM(qkv_kinds.shape, BF16),
            pltpu.VMEM(fir_buffer.shape, BF16),
            pltpu.VMEM(modal_state.shape, F32),
            pltpu.VMEM((groups, 2 * MODES + 2 * KINDS, width), BF16),
            pltpu.VMEM((16, width), F32),
            pltpu.SemaphoreType.DMA((6, slots // 16)),
        ],
        compiler_params=pltpu.CompilerParams(vmem_limit_bytes=56 * 1024 * 1024),
        name="home_rows",
    )(qkv_kinds, fir_buffer, modal_state, fir_taps, poles, residues, skip_row, finished)

    n, own_cols = lax.axis_size("tensor"), norm_gain.shape[0]
    gated_home, later_weight = lax.optimization_barrier((gated_home, out_weight))
    place = lax.axis_index("tensor").astype(jnp.int32)[None]
    far_place = (place[0] + n // 2) % n
    far_weight = lax.dynamic_slice_in_dim(later_weight, far_place * own_cols, own_cols, 1)
    got = swap(packed)
    far = dot(gated_home, far_weight).astype(BF16)
    half = far.shape[0] // 2
    right, left = pass_on(far[:half], far[half:])
    made = products(place, gated_home, out_weight, (3, -3, 2, -2))
    right, left = lax.optimization_barrier((right, left))
    right, left, gated_home = lax.optimization_barrier((*pass_on(*joined(made, 3, right, left)), gated_home))
    right, left = pass_on(*joined(made, 2, right, left))
    made = products(place, gated_home, out_weight, (1, -1, 0))
    right, left = lax.optimization_barrier((right, left))
    ride = jnp.stack(joined(made, 1, right, left))
    got, ride, own_home = lax.optimization_barrier((got, ride, made[0]))

    sent, gated_band, right, left = pl.pallas_call(
        band_kernel,
        in_specs=[
            pl.BlockSpec(memory_space=pltpu.SMEM),
        ]
        + [pl.BlockSpec(memory_space=pltpu.VMEM)] * 7,
        out_specs=[pl.BlockSpec(memory_space=pl.ANY)]
        + [pl.BlockSpec(memory_space=pltpu.VMEM)] * 3,
        out_shape=[
            jax.ShapeDtypeStruct((groups, 2 * MODES + 16, width), BF16),
            jax.ShapeDtypeStruct((3 * moving, width), BF16),
            jax.ShapeDtypeStruct((3 * moving // 2 + slots + 48, own_cols), BF16),
            jax.ShapeDtypeStruct((3 * moving // 2 + slots + 48, own_cols), BF16),
        ],
        scratch_shapes=[
            pltpu.VMEM((6, moving, width), F32),
            pltpu.VMEM((3, 3, moving, width), F32),
            pltpu.VMEM((2, moving, width), F32),
            pltpu.VMEM((3, moving, width), F32),
            pltpu.VMEM((3, moving, width), F32),
            pltpu.VMEM((3, moving, width), F32),
            pltpu.VMEM((KINDS - 6, moving, width), BF16),
            pltpu.VMEM((groups, 2 * MODES + 16, width), BF16),
            pltpu.SemaphoreType.DMA,
        ],
        compiler_params=pltpu.CompilerParams(vmem_limit_bytes=40 * 1024 * 1024),
        name="band_rows",
    )(turns, got, fir_taps, poles, residues, skip_row, far_weight, ride)

    half = 3 * moving // 2
    right, left = pass_on(right, left)
    made = products(place, gated_band, out_weight, (3, -3, 2, -2))
    right, left, gated_band, sent = lax.optimization_barrier((right, left, gated_band, sent))
    own_home = own_home + right[half:].astype(F32) + left[half:].astype(F32)
    right, left = pass_on(*joined(made, 3, right[:half], left[:half]))
    back = swap(sent)
    right, left, gated_band = lax.optimization_barrier((right, left, gated_band))
    right, left = pass_on(*joined(made, 2, right, left))
    made = products(place, gated_band, out_weight, (1, -1, 0))
    right, left = lax.optimization_barrier((right, left))
    right, left = pass_on(*joined(made, 1, right, left))
    right, left = lax.optimization_barrier((right, left))
    own_band = made[0] + right.astype(F32) + left.astype(F32)
    scales, back = row_scales([own_band, own_home], back)
    mixed_band = (own_band * scales[: 3 * moving] * norm_gain[None]).astype(BF16)
    mixed_band = jnp.transpose(mixed_band.reshape(3, groups, CAP, own_cols), (1, 0, 2, 3))
    back, mixed_band = lax.optimization_barrier((back, mixed_band))
    mixed_back = swap(mixed_band)
    final_state, final_lagged = pl.pallas_call(
        finish_kernel,
        in_specs=[pl.BlockSpec(memory_space=pl.ANY)] * 3 + [pl.BlockSpec(memory_space=pltpu.VMEM)],
        out_specs=[pl.BlockSpec(memory_space=pl.ANY)] * 2,
        out_shape=[
            jax.ShapeDtypeStruct(modal_state.shape, F32),
            jax.ShapeDtypeStruct(fir_buffer.shape, BF16),
        ],
        scratch_shapes=[
            pltpu.VMEM(back.shape, BF16),
            pltpu.VMEM((2, 3, slots, width), BF16),
            pltpu.VMEM(modal_state.shape, F32),
            pltpu.VMEM(fir_buffer.shape, BF16),
            pltpu.SemaphoreType.DMA((4, slots // 16)),
        ],
        compiler_params=pltpu.CompilerParams(vmem_limit_bytes=56 * 1024 * 1024),
        name="last_rows",
    )(back, qkv_kinds, stay_state, finished)

    mixed_later = jnp.transpose(mixed_back, (1, 0, 2, 3)).reshape(3, moving, own_cols)
    mixed_home = (own_home * scales[3 * moving :] * norm_gain[None]).astype(BF16)
    mixed_stay = mixed_home[slots:].reshape(3, 16, own_cols)
    mixed = jnp.concatenate(
        [mixed_home[None, :slots], jnp.concatenate([mixed_later, mixed_stay], axis=1)], axis=0
    )
    return (mixed, final_state, final_lagged)


def solution(mesh):
    return jax.shard_map(
        per_device,
        mesh=mesh,
        in_specs=(
            P(None, "dp", None, "tensor"),
            P("dp", None, None, "tensor"),
            P(None, None, "tensor"),
            P("dp", None, "tensor"),
            P(None, "tensor"),
            P(None, "tensor"),
            P("tensor"),
            P("tensor", None),
            P("tensor"),
            P(None, "dp"),
            P(None, "dp"),
        ),
        out_specs=(P(None, "dp", "tensor"), P("dp", None, "tensor"), P("dp", None, None, "tensor")),
        check_vma=False,
    )
```
